32 devices in a mesh: expert: 16 (over z, y, x), fsdp: 2 (over core).
Axes of the slice: x: 2, y: 2, z: 4, core: 2. Of those that a mesh axis runs over, the one named last changes fastest.
Arguments:
- hidden_in: bfloat16 [2, 2048, 2560], P('fsdp', 'expert'), may hold values from -6 to 6
- gain_attn: bfloat16 [2560], P('fsdp'), may hold values from 0.5 to 1.5
- query_weight: bfloat16 [2560, 2560], P('fsdp'), may hold values from -0.125 to 0.125
- key_matrix: bfloat16 [2560, 512], P('fsdp'), may hold values from -0.125 to 0.125
- value_matrix: bfloat16 [2560, 512], P('fsdp'), may hold values from -0.125 to 0.125
- out_weight: bfloat16 [2560, 2560], P('fsdp'), may hold values from -0.5 to 0.5
- gain_ffn: bfloat16 [2560], P('fsdp'), may hold values from 0.5 to 1.5
- router_weight: bfloat16 [2560, 16], P('fsdp'), may hold values from -0.0625 to 0.0625
- shared_gate: bfloat16 [2560, 3072], P('fsdp'), may hold values from -0.125 to 0.125
- shared_up: bfloat16 [2560, 3072], P('fsdp'), may hold values from -0.125 to 0.125
- shared_down: bfloat16 [3072, 2560], P('fsdp'), may hold values from -0.109375 to 0.109375
- expert_gate: bfloat16 [16, 2560, 1536], P('expert', 'fsdp'), may hold values from -0.125 to 0.125
- expert_up: bfloat16 [16, 2560, 1536], P('expert', 'fsdp'), may hold values from -0.125 to 0.125
- expert_down: bfloat16 [16, 1536, 2560], P('expert', 'fsdp'), may hold values from -0.15625 to 0.15625
- routes: int32 [2, 2048, 6], P('fsdp', 'expert'), may hold values from 0 to 15, all different within a row; in each aligned block of 128 rows (0 to 127, 128 to 255, ..., all dimensions but the last counted through in order) at most 64 rows name the same one
- segments: int32 [2, 2048], P('fsdp'), may hold values from 0 to 2, as said below
- positions: int32 [2, 2048], P('fsdp', 'expert'), may hold values from 0 to 4094, as said below
- grad_out: bfloat16 [2, 2048, 2560], P('fsdp', 'expert'), may hold values from -6 to 6
Outputs:
- output: bfloat16 [2, 2048, 2560], P('fsdp', 'expert')
- grad_in: bfloat16 [2, 2048, 2560], P('fsdp', 'expert')
- grad_gain_attn: float32 [2560], P('fsdp')
- grad_query: float32 [2560, 2560], P('fsdp')
- grad_key: float32 [2560, 512], P('fsdp')
- grad_value: float32 [2560, 512], P('fsdp')
- grad_out_weight: float32 [2560, 2560], P('fsdp')
- grad_gain_ffn: float32 [2560], P('fsdp')
- grad_router: float32 [2560, 16], P('fsdp')
- grad_shared_gate: float32 [2560, 3072], P('fsdp')
- grad_shared_up: float32 [2560, 3072], P('fsdp')
- grad_shared_down: float32 [3072, 2560], P('fsdp')
- grad_expert_gate: float32 [16, 2560, 1536], P('expert', 'fsdp')
- grad_expert_up: float32 [16, 2560, 1536], P('expert', 'fsdp')
- grad_expert_down: float32 [16, 1536, 2560], P('expert', 'fsdp')
The draws below stay inside these ranges and needn't reach their ends.
Inputs may be any that keep to these rules, and one draw needn't show every extreme that they name: `routes`: the 6 experts of a token differ. Among the 128 tokens of one device (aligned blocks of rows in sequence order) no expert is named more than 64 times, a bound that some block reaches in each draw. `segments`: document numbers never fall along a sequence; every sequence holds documents 0, 1 and 2; documents 0 and 2 each hold between 204 and 2 * (204) tokens, document 1 the rest. Within a document positions rise by one from token to token; document 0 of each sequence starts at position 0; the last token of each sequence has the largest position.
All inputs are finite; a program needn't handle non-finite values.
Results may differ from the reference program's by a relative error of at most 0.023.
Values may be sent and summed in bfloat16 or wider, within the bound.
A program may use at most 640 MiB of HBM per device.

```python
import math
import jax
import jax.numpy as jnp
import numpy as np
from jax import lax

MODEL_DIM = 2560
QUERY_HEADS = 20
KEY_HEADS = 4
HEAD_DIM = 128
FE = 1536
TOPK = 6
FS = 3072
TOK_DEV = 128
SEQ_LENGTH = 2048
SEQ_COUNT = 2
EXPERTS = 16
CAP = 64
N_EXPERT = 16


def documents(key):
    shortest = SEQ_LENGTH // 10
    opening = jax.random.randint(jax.random.fold_in(key, 11), (SEQ_COUNT,), shortest, 2 * shortest + 1)
    closing = jax.random.randint(jax.random.fold_in(key, 12), (SEQ_COUNT,), shortest, 2 * shortest + 1)
    place_index = jnp.arange(SEQ_LENGTH, dtype=jnp.int32)[None, :]
    number = (place_index >= opening[:, None]).astype(jnp.int32) + (place_index >= SEQ_LENGTH - closing[:, None]).astype(jnp.int32)
    return (number, opening, closing)


def draw_segments(key, part):
    number, opening, closing = documents(key)
    return number.astype(jnp.int32)


def draw_positions(key, part):
    number, opening, closing = documents(key)
    key = jax.random.fold_in(key, 5)
    offsets = jax.random.randint(key, (SEQ_COUNT, 3), 0, 2048)
    offsets = offsets.at[:, 0].set(0)
    offsets = offsets.at[:, 2].set(SEQ_LENGTH + 2047 - closing)
    starts = jnp.stack([jnp.zeros_like(opening), opening, SEQ_LENGTH - closing], axis=1)
    place_index = jnp.arange(SEQ_LENGTH, dtype=jnp.int32)[None, :]
    start_of = jnp.take_along_axis(starts, number, axis=1)
    offset_of = jnp.take_along_axis(offsets, number, axis=1)
    return (place_index - start_of + offset_of).astype(jnp.int32)


def raised(values, key, source, target, shards_of, factor):
    def block_of(position):
        return (jnp.arange(values.shape[position]) // (values.shape[position] // shards_of)).reshape((-1,) + (1,) * (values.ndim - 1 - position))

    one_side = jax.random.permutation(key, shards_of)[block_of(target)]
    second = (block_of(target) + shards_of // 2) % shards_of
    return jnp.where((block_of(source) == one_side) | (block_of(source) == second), factor * values, values)


def block_levels(own_key, extent, cuts, low, top_value):
    def one(axis_at, parts):
        steps = jax.random.uniform(jax.random.fold_in(jax.random.fold_in(own_key, 6), axis_at), (parts,), jnp.float32, low / len(cuts), top_value / len(cuts))
        return jnp.repeat(jnp.exp(steps), extent[axis_at] // parts).reshape((-1,) + (1,) * (len(extent) - axis_at - 1))

    loudness = one(*cuts[0])
    for cut in cuts[1:]:
        loudness = loudness * one(*cut)
    return loudness


def assign_block(key, own, number, rows, number_of, top, limit, slope):
    sequence = jax.random.permutation(key, number_of)
    crowded, usual = portions_of(number_of, rows * top, limit, slope, True), portions_of(number_of, rows * top, limit, slope, False)
    places = jnp.arange(number_of)

    def named(tallies, turn):
        used = int((tallies > 0).sum())
        fixed = max(1, used // 4)
        passed = fixed + (places - fixed + turn * (used - fixed)) % max(1, number_of - fixed)
        return jnp.zeros((number_of,), jnp.int32).at[sequence[jnp.where(places < fixed, places, passed)]].set(jnp.asarray(tallies, jnp.int32))

    tallies = jnp.where(number % 4 == 0, named(crowded, number // 4), named(usual, number - number // 4 - 1))
    mixed = jax.random.permutation(jax.random.fold_in(own, 3), number_of)
    source_of, receiver = mixed[0:number_of // 2 * 2:2], mixed[1:number_of // 2 * 2:2]
    slack = jnp.minimum(tallies[source_of] - 1, limit - tallies[receiver]) // 2
    slack = jnp.where((source_of == sequence[0]) | (receiver == sequence[0]) | (tallies[receiver] == 0), 0, jnp.maximum(slack, 0))
    passed = jax.random.randint(jax.random.fold_in(own, 4), (number_of // 2,), 0, 1 << 20) % (slack + 1)
    tallies = tallies.at[source_of].add(-passed).at[receiver].add(passed)
    members = jnp.searchsorted(jnp.cumsum(tallies), jnp.arange(rows * top), side="right").astype(jnp.int32)
    grid = members.reshape(top, rows).T
    grid = grid[jax.random.permutation(jax.random.fold_in(own, 1), rows)]
    turn = jax.random.randint(jax.random.fold_in(own, 2), (rows, 1), 0, top)
    return jnp.take_along_axis(grid, (jnp.arange(top)[None, :] + turn) % top, axis=1)


def portions_of(number_of, total, bound, skew, full):
    portions = [(1 << 20) // math.isqrt(grade ** skew) + 1 for grade in range(1, number_of + 1)]
    largest = bound if full else min(bound, max(-(-total // number_of), total * portions[0] // sum(portions)))
    least = 1 if total - largest >= number_of - 1 else 0
    holding, surplus = [largest] + [least] * (number_of - 1), total - largest - least * (number_of - 1)
    while surplus > 0:
        free = [i for i in range(1, number_of) if holding[i] < largest] or [i for i in range(1, number_of) if holding[i] < bound]
        whole, left = sum([portions[i] for i in free]), surplus
        for i in free:
            more = min(bound - holding[i], max(1, left * portions[i] // whole), surplus)
            holding[i] = holding[i] + more
            surplus = surplus - more
    return np.array(holding)


def centred(key, shape, scale, bound, cuts=(), kind=jnp.bfloat16):
    drawn = scale * jax.random.normal(key, shape, jnp.float32)
    if cuts:
        drawn = drawn * block_levels(key, shape, cuts, -0.22, 0.18)
    return jnp.clip(drawn, -bound, bound).astype(kind)


def gaussian_with(stream_key, shape, width, reach, split, heavy, kind=jnp.bfloat16):
    entries = width * jax.random.normal(stream_key, shape, jnp.float32)
    if split:
        entries = entries * block_levels(stream_key, shape, split, -0.22, 0.18)
    return jnp.clip(raised(entries, jax.random.fold_in(stream_key, 3), *heavy), -reach, reach).astype(kind)


def setup_inputs(seed: int = 0) -> dict:
    seeds = jax.random.split(jax.random.key(seed), 19)
    hidden_in = centred(seeds[0], (SEQ_COUNT, SEQ_LENGTH, MODEL_DIM), 1.0, 6.0, ((0, 2), (1, 16)))
    gain_attn = jnp.clip(1.0 + 0.1 * jax.random.normal(seeds[1], (MODEL_DIM,), jnp.float32), 0.5, 1.5).astype(jnp.bfloat16)
    query_weight = centred(seeds[2], (MODEL_DIM, QUERY_HEADS * HEAD_DIM), MODEL_DIM ** -0.5, 0.125, ((0, 2),))
    key_matrix = centred(seeds[3], (MODEL_DIM, KEY_HEADS * HEAD_DIM), MODEL_DIM ** -0.5, 0.125, ((0, 2),))
    value_matrix = centred(seeds[4], (MODEL_DIM, KEY_HEADS * HEAD_DIM), MODEL_DIM ** -0.5, 0.125, ((0, 2),))
    out_weight = centred(seeds[5], (QUERY_HEADS * HEAD_DIM, MODEL_DIM), (MODEL_DIM // 16) ** -0.5, 0.5, ((0, 2),))
    gain_ffn = jnp.clip(1.0 + 0.1 * jax.random.normal(seeds[6], (MODEL_DIM,), jnp.float32), 0.5, 1.5).astype(jnp.bfloat16)
    router_weight = centred(seeds[7], (MODEL_DIM, EXPERTS), (4 * MODEL_DIM) ** -0.5, 0.0625, ((0, 2),))
    shared_gate = centred(seeds[8], (MODEL_DIM, FS), MODEL_DIM ** -0.5, 0.125, ((0, 2),))
    shared_up = centred(seeds[9], (MODEL_DIM, FS), MODEL_DIM ** -0.5, 0.125, ((0, 2),))
    shared_down = centred(seeds[10], (FS, MODEL_DIM), FS ** -0.5, 0.109375, ((0, 2),))
    expert_gate = centred(seeds[11], (EXPERTS, MODEL_DIM, FE), MODEL_DIM ** -0.5, 0.125, ((0, 16), (1, 2)))
    expert_up = centred(seeds[12], (EXPERTS, MODEL_DIM, FE), MODEL_DIM ** -0.5, 0.125, ((0, 16), (1, 2)))
    expert_down = centred(seeds[13], (EXPERTS, FE, MODEL_DIM), FE ** -0.5, 0.15625, ((0, 16), (1, 2)))
    routes_keys = jax.random.split(jax.random.fold_in(seeds[14], 1), SEQ_COUNT * SEQ_LENGTH // TOK_DEV)
    routes_turns = jax.random.permutation(jax.random.fold_in(seeds[14], 3), SEQ_COUNT * SEQ_LENGTH // TOK_DEV)
    routes = jax.vmap(lambda own, number: assign_block(jax.random.fold_in(seeds[14], 2), own, number, TOK_DEV, EXPERTS, TOPK, CAP, 2))(routes_keys, routes_turns).reshape((SEQ_COUNT, SEQ_LENGTH, TOPK))
    segments = draw_segments(jax.random.fold_in(seeds[18], 71), 0)
    positions = draw_positions(jax.random.fold_in(seeds[18], 71), 0)
    grad_out = gaussian_with(seeds[17], (SEQ_COUNT, SEQ_LENGTH, MODEL_DIM), 1.0, 6.0, ((0, 2), (1, 16)), (1, 2, 16, 2.0))
    return {"hidden_in": hidden_in, "gain_attn": gain_attn, "query_weight": query_weight, "key_matrix": key_matrix, "value_matrix": value_matrix, "out_weight": out_weight, "gain_ffn": gain_ffn, "router_weight": router_weight, "shared_gate": shared_gate, "shared_up": shared_up, "shared_down": shared_down, "expert_gate": expert_gate, "expert_up": expert_up, "expert_down": expert_down, "routes": routes, "segments": segments, "positions": positions, "grad_out": grad_out}


@jax.custom_vjp
def low(v):
    return lax.optimization_barrier(v.astype(jnp.bfloat16)).astype(jnp.float32)

@jax.custom_vjp
def low_back(v):
    return v

def low_keep(v):
    return (low(v), None)

def low_pass(kept, grad):
    return (grad,)

def back_keep(v):
    return (v, None)

def back_low(kept, grad):
    return (low(grad),)
low.defvjp(low_keep, low_pass)
low_back.defvjp(back_keep, back_low)
epsilon = 1e-05
rope_base = 500000.0
masked_score = -1e+30
highest = lax.Precision.HIGHEST

def product_result(left, right):
    return jnp.dot(left, right, precision=highest, preferred_element_type=jnp.float32)

def rms_scale(vector, gain):
    factor = lax.rsqrt(lax.optimization_barrier(jnp.mean(vector * vector, axis=-1, keepdims=True)) + epsilon)
    return vector * factor * gain

def apply_rotation(heads, cosine_table, sine_table):
    halfway = heads.shape[-1] // 2
    front_part = heads[..., :halfway]
    back_part = heads[..., halfway:]
    return jnp.concatenate([front_part * cosine_table - back_part * sine_table, back_part * cosine_table + front_part * sine_table], axis=-1)

def rope_tables(positions):
    frequency = 1.0 / rope_base ** (jnp.arange(0, HEAD_DIM, 2, dtype=jnp.float32) / HEAD_DIM)
    turned = positions.astype(jnp.float32)[:, None] * frequency[None, :]
    return (jnp.cos(turned)[:, None, :], jnp.sin(turned)[:, None, :])

def swiglu(gate_in, up_in):
    return jax.nn.silu(gate_in) * up_in

def gate_values(logits, chosen_ids):
    router_probs = jax.nn.softmax(logits, axis=-1)
    chosen = jnp.take_along_axis(router_probs, chosen_ids, axis=1)
    return chosen / lax.optimization_barrier(jnp.sum(chosen, axis=1, keepdims=True))

def slot_table(routes):
    blocks = SEQ_COUNT * N_EXPERT
    block_ids = routes.reshape(blocks, TOK_DEV * TOPK).astype(jnp.int32)
    onehot = (block_ids[:, :, None] == jnp.arange(EXPERTS, dtype=jnp.int32)[None, None, :]).astype(jnp.int32)
    earlier = jnp.cumsum(onehot, axis=1) - onehot
    rank_in = lax.optimization_barrier(jnp.sum(earlier * onehot, axis=2)).astype(jnp.int32)
    block_index = jnp.arange(blocks, dtype=jnp.int32)[:, None]
    slot_of = ((block_index * EXPERTS + block_ids) * CAP + rank_in).astype(jnp.int32)
    pair_index = (block_index * (TOK_DEV * TOPK) + jnp.arange(TOK_DEV * TOPK, dtype=jnp.int32)[None, :]).astype(jnp.int32)
    table = jnp.full((blocks * EXPERTS * CAP,), -1, jnp.int32).at[slot_of.reshape(-1)].set(pair_index.reshape(-1))
    return table.reshape(blocks, EXPERTS, CAP).transpose(1, 0, 2).reshape(EXPERTS, blocks * CAP)

def attend_document(sequence_item):
    query_matrix, key_collection, value_collection, labels = sequence_item
    length_total = query_matrix.shape[0]
    rows_per_block = min(512, length_total)
    group_width = QUERY_HEADS // KEY_HEADS
    query_block_list = query_matrix.reshape(length_total // rows_per_block, rows_per_block, KEY_HEADS, group_width, HEAD_DIM)
    row_index = jnp.arange(length_total, dtype=jnp.int32).reshape(length_total // rows_per_block, rows_per_block)
    key_index = jnp.arange(length_total, dtype=jnp.int32)

    def one_block(block_item):
        query_block, query_rows = block_item
        scores = jnp.einsum('qgjd,kgd->gjqk', query_block, key_collection, precision=highest) * HEAD_DIM ** (-0.5)
        scores = low_back(scores)
        allowed = (labels[query_rows][:, None] == labels[None, :]) & (key_index[None, :] <= query_rows[:, None])
        scores = jnp.where(allowed[None, None], scores, masked_score)
        weights = low(jax.nn.softmax(scores, axis=-1))
        mixed_output = jnp.einsum('gjqk,kgd->qgjd', weights, value_collection, precision=highest)
        return mixed_output.reshape(rows_per_block, QUERY_HEADS * HEAD_DIM)
    outputs = lax.map(jax.checkpoint(one_block), (query_block_list, row_index))
    return outputs.reshape(length_total, QUERY_HEADS * HEAD_DIM)

def layer(hidden_in, gain_attn, query_weight, key_matrix, value_matrix, out_weight, gain_ffn, router_weight, shared_gate, shared_up, shared_down, expert_gate, expert_up, expert_down, chosen_ids, segments, cosine_table, sine_table, table):
    x_rows = hidden_in.reshape(-1, MODEL_DIM)
    first_normed = low(rms_scale(x_rows, gain_attn))
    query_matrix = low(apply_rotation(low_back(product_result(first_normed, query_weight)).reshape(-1, QUERY_HEADS, HEAD_DIM), cosine_table, sine_table))
    key_collection = low(apply_rotation(low_back(product_result(first_normed, key_matrix)).reshape(-1, KEY_HEADS, HEAD_DIM), cosine_table, sine_table))
    value_collection = low(low_back(product_result(first_normed, value_matrix))).reshape(-1, KEY_HEADS, HEAD_DIM)
    mixed_output = lax.map(jax.checkpoint(attend_document), (query_matrix.reshape(SEQ_COUNT, SEQ_LENGTH, QUERY_HEADS, HEAD_DIM), key_collection.reshape(SEQ_COUNT, SEQ_LENGTH, KEY_HEADS, HEAD_DIM), value_collection.reshape(SEQ_COUNT, SEQ_LENGTH, KEY_HEADS, HEAD_DIM), segments))
    attended = low_back(low(mixed_output.reshape(-1, QUERY_HEADS * HEAD_DIM)))
    residual_one = x_rows + low_back(product_result(attended, out_weight))
    normed_two = low(rms_scale(residual_one, gain_ffn))
    gate_weight = gate_values(product_result(normed_two, router_weight), chosen_ids).reshape(-1)
    shared_act = low(swiglu(low_back(product_result(normed_two, shared_gate)), low_back(product_result(normed_two, shared_up))))
    shared_out = product_result(shared_act, shared_down)

    def one_expert(expert_item):
        gate_in, up_in, down_in, pairs = expert_item
        valid = pairs >= 0
        safe_pair = jnp.where(valid, pairs, 0)
        taken = low_back(jnp.where(valid[:, None], normed_two[safe_pair // TOPK], 0.0))
        inner = low(swiglu(low_back(product_result(taken, gate_in)), low_back(product_result(taken, up_in))))
        result = low_back(low(product_result(inner, down_in)))
        scale_of = jnp.where(valid, gate_weight[safe_pair], 0.0)
        return scale_of[:, None] * result
    weighted = lax.map(jax.checkpoint(one_expert), (expert_gate, expert_up, expert_down, table))
    owner = (jnp.where(table >= 0, table, 0) // TOPK).astype(jnp.int32)
    expert_sum = jnp.zeros_like(x_rows).at[owner.reshape(-1)].add(weighted.reshape(-1, MODEL_DIM))
    return residual_one + shared_out + expert_sum

def reference(hidden_in, gain_attn, query_weight, key_matrix, value_matrix, out_weight, gain_ffn, router_weight, shared_gate, shared_up, shared_down, expert_gate, expert_up, expert_down, routes, segments, positions, grad_out):
    chosen_ids = routes.reshape(-1, TOPK).astype(jnp.int32)
    cosine_table, sine_table = rope_tables(positions.reshape(-1))
    table = slot_table(routes)
    floats = (hidden_in.astype(jnp.float32), gain_attn.astype(jnp.float32), query_weight.astype(jnp.float32), key_matrix.astype(jnp.float32), value_matrix.astype(jnp.float32), out_weight.astype(jnp.float32), gain_ffn.astype(jnp.float32), router_weight.astype(jnp.float32), shared_gate.astype(jnp.float32), shared_up.astype(jnp.float32), shared_down.astype(jnp.float32), expert_gate.astype(jnp.float32), expert_up.astype(jnp.float32), expert_down.astype(jnp.float32))

    def forward(*weights_in):
        return layer(*weights_in, chosen_ids, segments, cosine_table, sine_table, table)
    result, pull = jax.vjp(forward, *floats)
    grads = pull(grad_out.astype(jnp.float32).reshape(-1, MODEL_DIM))
    return (result.astype(jnp.bfloat16).reshape(SEQ_COUNT, SEQ_LENGTH, MODEL_DIM), grads[0].astype(jnp.bfloat16).reshape(SEQ_COUNT, SEQ_LENGTH, MODEL_DIM), grads[1], grads[2], grads[3], grads[4], grads[5], grads[6], grads[7], grads[8], grads[9], grads[10], grads[11], grads[12], grads[13])
```

```python
import jax
import jax.numpy as jnp
from jax import lax
from jax.experimental import pallas as pl
from jax.experimental.pallas import tpu as pltpu
from jax.sharding import PartitionSpec as P

QUERY_HEADS = 20
KEY_HEADS = 4
HEAD_DIM = 128

epsilon = 1e-05
rope_base = 500000.0
masked_score = -1e30
highest = lax.Precision.HIGHEST
LOW = jnp.bfloat16
MESH = pl.DeviceIdType.MESH


def dot_nn(left, right):
    return jnp.dot(left, right, preferred_element_type=jnp.float32)


def dot_nt(left, right):
    return lax.dot_general(
        left, right, (((1,), (1,)), ((), ())), preferred_element_type=jnp.float32
    )


def dot_tn(left, right):
    return lax.dot_general(
        left, right, (((0,), (0,)), ((), ())), preferred_element_type=jnp.float32
    )


def rms_scale(vector, gain):
    factor = lax.rsqrt(jnp.mean(vector * vector, axis=-1, keepdims=True) + epsilon)
    return vector * factor * gain


def rms_back(vector, gain, grad):
    factor = lax.rsqrt(jnp.mean(vector * vector, axis=-1, keepdims=True) + epsilon)
    scaled = grad * gain
    inner = jnp.mean(scaled * vector, axis=-1, keepdims=True)
    d_vector = factor * scaled - vector * (factor * factor * factor * inner)
    return d_vector, jnp.sum(grad * vector * factor, axis=0)


def rotate(heads, cosine, sine):
    half = heads.shape[-1] // 2
    front, back = heads[..., :half], heads[..., half:]
    return jnp.concatenate([front * cosine - back * sine, back * cosine + front * sine], axis=-1)


def rope_tables(positions):
    frequency = 1.0 / rope_base ** (jnp.arange(0, HEAD_DIM, 2, dtype=jnp.float32) / HEAD_DIM)
    turned = positions.astype(jnp.float32)[:, None] * frequency[None, :]
    return jnp.cos(turned)[:, None, :], jnp.sin(turned)[:, None, :]


def swiglu(gate, up):
    return gate * jax.nn.sigmoid(gate) * up


def swiglu_back(gate, up, grad):
    sigma = jax.nn.sigmoid(gate)
    return grad * up * (sigma * (1.0 + gate * (1.0 - sigma))), grad * gate * sigma


def coordinates():
    me = lax.axis_index("expert")
    quarter = lax.rem(me, 4)
    depth = me // 4
    across = quarter + 1 - 2 * lax.rem(quarter, 2)
    beside = quarter + 2 - 4 * (quarter // 2)
    return me, quarter, depth, across, beside


def when(condition):
    return pl.when(condition)


def send(source, target, send_sem, recv_sem, **device):
    return pltpu.make_async_remote_copy(
        src_ref=source,
        dst_ref=target,
        send_sem=send_sem,
        recv_sem=recv_sem,
        device_id=device,
        device_id_type=MESH,
    )


def enter(peers, everyone):
    me, quarter, depth, across, beside = coordinates()
    barrier = pltpu.get_barrier_semaphore()

    def greet(**device):
        pl.semaphore_signal(barrier, inc=1, device_id=device, device_id_type=MESH)

    if everyone:
        for step in range(1, 16):
            greet(expert=lax.rem(me + step, 16))
        near = 15
    else:
        greet(expert=depth * 4 + across)
        greet(expert=depth * 4 + beside)

        @when(depth < 3)
        def _():
            greet(expert=me + 4)

        @when(depth > 0)
        def _():
            greet(expert=me - 4)

        near = 2 + jnp.minimum(depth, 1) + jnp.minimum(3 - depth, 1)

    side = lax.axis_index("fsdp")
    for step in range(1, peers):
        greet(fsdp=lax.rem(side - step + peers, peers))
    pl.semaphore_wait(barrier, near + (peers - 1))


class Gather:
    def __init__(self, rows, width, peers):
        self.rows, self.width = rows, width
        self.peers = peers
        self.half = self.width // 2 // 128 * 128

    def scratch(self):
        shapes = [pltpu.SemaphoreType.DMA((11, 4)), pltpu.SemaphoreType.DMA((2,))]
        if self.peers > 1:
            shapes += [pltpu.SemaphoreType.DMA((2, self.peers - 1, 16))]
        return shapes

    def stages(self, source, out, sems, own_sem, mate_sems=None):
        rows, half = self.rows, self.half
        names = ("zr", "xr", "yr", "ar", "br", "us", "ds", "xs", "ys", "as", "bs")
        row_of = {name: index for index, name in enumerate(names)}
        spans = {"a": pl.ds(0, half), "b": pl.ds(half, self.width - half)}

        def sem(name, plane):
            return sems.at[row_of[name], plane]

        columns = pl.ds(0, self.width)

        def block(index):
            return out.at[0, index, :, columns]

        def part(index, name):
            return out.at[0, index, :, spans[name]]

        def hop(name, plane):
            me, quarter, depth, across, beside = coordinates()
            own = plane * 4 + quarter
            if name in ("u", "d"):
                shift = 4 if name == "u" else -4
                return send(
                    block(own), block(own), sem(name + "s", plane), sem("zr", plane),
                    expert=me + shift,
                )
            if name == "x":
                return send(
                    block(own), block(own), sem("xs", plane), sem("xr", plane),
                    expert=depth * 4 + across,
                )
            if name == "y":
                return send(
                    block(own), block(own), sem("ys", plane), sem("yr", plane),
                    expert=depth * 4 + beside,
                )
            if name == "a":
                index = plane * 4 + across
                return send(
                    part(index, "a"), part(index, "a"), sem("as", plane), sem("ar", plane),
                    expert=depth * 4 + beside,
                )
            index = plane * 4 + beside
            return send(
                part(index, "b"), part(index, "b"), sem("bs", plane), sem("br", plane),
                expert=depth * 4 + across,
            )

        def landed(name, plane):
            me, quarter, depth, across, beside = coordinates()
            index = {
                "z": plane * 4 + quarter,
                "x": plane * 4 + across,
                "y": plane * 4 + beside,
                "a": plane * 4 + (3 - quarter),
                "b": plane * 4 + (3 - quarter),
            }[name]
            ref = part(index, name) if name in ("a", "b") else block(index)
            return send(ref, ref, sem("us", plane), sem(name + "r", plane), expert=me)

        def mates(index, start):
            side = lax.axis_index("fsdp")
            for step in range(1, self.peers):
                copy = send(
                    out.at[0, index, :, columns],
                    out.at[step, index, :, columns],
                    mate_sems.at[0, step - 1, index],
                    mate_sems.at[1, step - 1, index],
                    fsdp=lax.rem(side - step + self.peers, self.peers),
                )
                if start:
                    copy.start()
                else:
                    copy.wait()

        def own_copy():
            me = lax.axis_index("expert")
            return pltpu.make_async_copy(source.at[:, columns], block(me), own_sem.at[0])

        def spread(plane):
            hop("x", plane).start()
            hop("y", plane).start()
            mates(plane * 4 + coordinates()[1], True)

        def first():
            depth = coordinates()[2]
            own_copy().start()
            own_copy().wait()

            @when(depth < 3)
            def _():
                hop("u", depth).start()

            @when(depth > 0)
            def _():
                hop("d", depth).start()

            spread(depth)

        def arrive(distance):
            depth = coordinates()[2]

            @when(depth >= distance)
            def _():
                plane = depth - distance
                landed("z", plane).wait_recv()

                @when(depth < 3)
                def _():
                    hop("u", plane).start()

                spread(plane)

            @when(depth + distance <= 3)
            def _():
                plane = depth + distance
                landed("z", plane).wait_recv()

                @when(depth > 0)
                def _():
                    hop("d", plane).start()

                spread(plane)

        def both(distance, action):
            depth = coordinates()[2]
            if distance == 0:
                action(depth)
                return

            @when(depth >= distance)
            def _():
                action(depth - distance)

            @when(depth + distance <= 3)
            def _():
                action(depth + distance)

        def cross(plane):
            me, quarter, depth, across, beside = coordinates()
            landed("x", plane).wait_recv()
            hop("a", plane).start()
            mates(plane * 4 + across, True)
            landed("y", plane).wait_recv()
            hop("b", plane).start()
            mates(plane * 4 + beside, True)

        def corner(plane):
            quarter = coordinates()[1]
            landed("a", plane).wait_recv()
            landed("b", plane).wait_recv()
            mates(plane * 4 + 3 - quarter, True)

        def finish():
            me, quarter, depth, across, beside = coordinates()
            for plane in range(4):
                for name in ("x", "y", "a", "b"):
                    hop(name, plane).wait_send()

                @when((plane <= depth) & (depth < 3))
                def _():
                    hop("u", plane).wait_send()

                @when((plane >= depth) & (depth > 0))
                def _():
                    hop("d", plane).wait_send()

            if self.peers > 1:
                def settle(index, carry):
                    mates(index, False)
                    return carry

                lax.fori_loop(0, 16, settle, 0)

        stages = [first]
        stages.append(lambda: arrive(1))
        stages.append(lambda: both(0, cross))
        stages.append(lambda: arrive(2))
        stages.append(lambda: both(1, cross))
        stages.append(lambda: (both(0, corner), arrive(3)))
        stages.append(lambda: both(2, cross))
        stages.append(lambda: both(1, corner))
        stages.append(lambda: both(3, cross))
        stages.append(lambda: both(2, corner))
        stages.append(lambda: (both(3, corner), finish()))
        return stages


class GatherLast:
    def __init__(self, rows, start, width, peers):
        self.rows, self.start, self.width, self.peers = rows, start, width, peers
        self.half = (rows // 2 + 15) // 16 * 16

    def scratch(self):
        shapes = [pltpu.SemaphoreType.DMA((8,)), pltpu.SemaphoreType.DMA((3, 16))]
        shapes += [pltpu.SemaphoreType.DMA((1,))]
        if self.peers > 1:
            shapes += [pltpu.SemaphoreType.DMA((2, self.peers - 1, 16))]
        return shapes

    def stages(self, source, out, sems, line_sems, own_sem, mate_sems=None):
        columns = pl.ds(self.start, self.width)
        spans = {"a": pl.ds(0, self.half), "b": pl.ds(self.half, self.rows - self.half)}

        def block(index, slot=0):
            return out.at[slot, index, :, columns]

        def part(index, name):
            return out.at[0, index, spans[name], columns]

        def hop(name):
            me, quarter, depth, across, beside = coordinates()
            at_x, at_y = depth * 4 + across, depth * 4 + beside
            if name == "x":
                return send(block(me), block(me), sems.at[0], sems.at[1], expert=at_x)
            if name == "y":
                return send(block(me), block(me), sems.at[2], sems.at[3], expert=at_y)
            if name == "a":
                ref = part(at_x, "a")
                return send(ref, ref, sems.at[4], sems.at[5], expert=at_y)
            ref = part(at_y, "b")
            return send(ref, ref, sems.at[6], sems.at[7], expert=at_x)

        def landed(name):
            me, quarter, depth, across, beside = coordinates()
            corner = depth * 4 + 3 - quarter
            ref = {
                "x": lambda: block(depth * 4 + across),
                "y": lambda: block(depth * 4 + beside),
                "a": lambda: part(corner, "a"),
                "b": lambda: part(corner, "b"),
            }[name]()
            number = {"x": 1, "y": 3, "a": 5, "b": 7}[name]
            return send(ref, ref, sems.at[number - 1], sems.at[number], expert=me)

        def along(index, up):
            me = lax.axis_index("expert")
            return send(
                block(index), block(index),
                line_sems.at[0 if up else 1, index], line_sems.at[2, index],
                expert=me + 4 if up else me - 4,
            )

        def mates(index, start):
            side = lax.axis_index("fsdp")
            for step in range(1, self.peers):
                copy = send(
                    block(index), block(index, step),
                    mate_sems.at[0, step - 1, index], mate_sems.at[1, step - 1, index],
                    fsdp=lax.rem(side - step + self.peers, self.peers),
                )
                if start:
                    copy.start()
                else:
                    copy.wait()

        def both_ways(index):
            depth = coordinates()[2]

            @when(depth < 3)
            def _():
                along(index, True).start()

            @when(depth > 0)
            def _():
                along(index, False).start()

            mates(index, True)

        def first():
            me = lax.axis_index("expert")
            own = pltpu.make_async_copy(source.at[:, columns], block(me), own_sem.at[0])
            own.start()
            own.wait()
            hop("x").start()
            hop("y").start()
            both_ways(me)

        def cross():
            me, quarter, depth, across, beside = coordinates()
            landed("x").wait_recv()
            hop("a").start()
            both_ways(depth * 4 + across)
            landed("y").wait_recv()
            hop("b").start()
            both_ways(depth * 4 + beside)

        def corner():
            me, quarter, depth, across, beside = coordinates()
            landed("a").wait_recv()
            landed("b").wait_recv()
            both_ways(depth * 4 + 3 - quarter)

        def arrive(distance, which):
            depth = coordinates()[2]

            @when(depth >= distance)
            def _():
                for quarter in which:
                    index = (depth - distance) * 4 + quarter
                    along(index, True).wait_recv()

                    @when(depth < 3)
                    def _(index=index):
                        along(index, True).start()

                    mates(index, True)

            @when(depth + distance <= 3)
            def _():
                for quarter in which:
                    index = (depth + distance) * 4 + quarter
                    along(index, False).wait_recv()

                    @when(depth > 0)
                    def _(index=index):
                        along(index, False).start()

                    mates(index, True)

        def finish():
            depth = coordinates()[2]
            for name in ("x", "y", "a", "b"):
                hop(name).wait_send()

            def settle(index, carry):
                plane = index // 4

                @when((plane <= depth) & (depth < 3))
                def _():
                    along(index, True).wait_send()

                @when((plane >= depth) & (depth > 0))
                def _():
                    along(index, False).wait_send()

                if self.peers > 1:
                    mates(index, False)
                return carry

            lax.fori_loop(0, 16, settle, 0)

        stages = [first, cross, corner]
        for distance in (1, 2, 3):
            for which in ((0, 1), (2, 3)):
                stages.append(lambda d=distance, w=which: arrive(d, w))
        return stages + [finish]


def plane_at(order):
    depth = coordinates()[2]
    inner = lax.rem(lax.rem(depth, 2) + depth // 2, 2)
    upper = depth // 2
    plane = (3 - order) + inner * (0, -2, 1, 1)[order]
    return plane + upper * (3 - 2 * plane)


def wide(value):
    return value.astype(jnp.float32)


def by_rows(start, rows, action):
    def step(index, carry):
        action(pl.ds(pl.multiple_of(start + index * 16, 16), 16))
        return carry

    lax.fori_loop(0, rows // 16, step, 0)


class Scatter:
    def __init__(self, rows, start, width):
        self.rows, self.start, self.width = rows, start, width
        self.half = self.width // 2 // 128 * 128

    def scratch(self):
        rows, half = self.rows, self.half
        rest = self.width - half
        return [
            pltpu.VMEM((2, 2, rows, half), LOW),
            pltpu.VMEM((2, 2, rows, rest), LOW),
            pltpu.VMEM((4, 2, rows, half), LOW),
            pltpu.VMEM((4, 2, rows, rest), LOW),
            pltpu.VMEM((4, rows, half), LOW),
            pltpu.VMEM((4, rows, rest), LOW),
            pltpu.VMEM((4, rows, self.width), LOW),
            pltpu.VMEM((5, rows, self.width), LOW),
            pltpu.SemaphoreType.DMA((14, 4)),
        ]

    def stages(
        self, terms, out, own_a, own_b, got_a, got_b, more_a, more_b, plane_sum, line, sems
    ):
        rows, half, width = self.rows, self.half, self.width
        left, right = pl.ds(0, half), pl.ds(half, width - half)
        mine = pl.ds(0, width)
        from_left = pl.ds(self.start, half)
        from_right = pl.ds(self.start + half, width - half)

        def over_rows(action):
            by_rows(0, rows, action)

        def bits():
            quarter = coordinates()[1]
            return lax.rem(quarter, 2), quarter // 2

        def load(order):
            plane, slot = plane_at(order), order % 2
            x, y = bits()
            return (
                pltpu.make_async_copy(
                    terms.at[plane, y, :, :, from_left], own_a.at[slot], sems.at[0, plane]
                ),
                pltpu.make_async_copy(
                    terms.at[plane, :, x, :, from_right], own_b.at[slot], sems.at[1, plane]
                ),
            )

        def first_hop(plane):
            me, quarter, depth, across, beside = coordinates()
            x, y = bits()
            return (
                send(
                    terms.at[plane, 1 - y, :, :, from_left], got_a.at[plane],
                    sems.at[2, plane], sems.at[3, plane], expert=depth * 4 + beside,
                ),
                send(
                    terms.at[plane, :, 1 - x, :, from_right], got_b.at[plane],
                    sems.at[4, plane], sems.at[5, plane], expert=depth * 4 + across,
                ),
            )

        def second_hop(order):
            me, quarter, depth, across, beside = coordinates()
            plane, slot = plane_at(order), order % 2
            x, y = bits()
            return (
                send(
                    own_a.at[slot, 1 - x], more_a.at[plane],
                    sems.at[6, plane], sems.at[7, plane], expert=depth * 4 + across,
                ),
                send(
                    own_b.at[slot, 1 - y], more_b.at[plane],
                    sems.at[8, plane], sems.at[9, plane], expert=depth * 4 + beside,
                ),
            )

        def upward(plane):
            me = lax.axis_index("expert")
            return send(
                plane_sum.at[plane], line.at[plane], sems.at[10, plane], sems.at[11, plane],
                expert=me + 4,
            )

        def downward(plane, receiver):
            me = lax.axis_index("expert")
            slot = plane + (4 - plane) * (1 - jnp.minimum(jnp.abs(plane - receiver), 1))
            return send(
                plane_sum.at[plane], line.at[slot], sems.at[12, plane], sems.at[13, plane],
                expert=me - 4,
            )

        def begin(copies):
            for copy in copies:
                copy.start()

        def pair_sums(order):
            plane, slot = plane_at(order), order % 2
            for copy in load(order):
                copy.wait()
            for copy in first_hop(plane):
                copy.wait_recv()
            for mine, got in ((own_a, got_a), (own_b, got_b)):
                for index in range(2):
                    def add(span, mine=mine, got=got, index=index):
                        mine[slot, index, span, :] = (
                            wide(mine[slot, index, span, :]) + wide(got[plane, index, span, :])
                        ).astype(LOW)

                    over_rows(add)
            begin(second_hop(order))
            if order + 2 < 4:
                begin(first_hop(plane_at(order + 2)))

        def plane_sums(order):
            plane, slot = plane_at(order), order % 2
            x, y = bits()
            for copy in second_hop(order):
                copy.wait_recv()

            def add(span):
                plane_sum[plane, span, left] = (
                    wide(own_a[slot, x, span, :]) + wide(more_a[plane, span, :])
                ).astype(LOW)
                plane_sum[plane, span, right] = (
                    wide(own_b[slot, y, span, :]) + wide(more_b[plane, span, :])
                ).astype(LOW)

            over_rows(add)
            for copy in second_hop(order):
                copy.wait_send()
            if order + 2 < 4:
                begin(load(order + 2))

        def pass_on(order):
            plane = plane_at(order)
            depth = coordinates()[2]

            def join(slot):
                def add(span):
                    plane_sum[plane, span, :] = (
                        wide(plane_sum[plane, span, :]) + wide(line[slot, span, :])
                    ).astype(LOW)

                over_rows(add)

            @when(plane > depth)
            def _():
                @when(depth > 0)
                def _():
                    upward(plane).wait_recv()
                    join(plane)

                upward(plane).start()

            @when(plane < depth)
            def _():
                @when(depth < 3)
                def _():
                    downward(plane, depth).wait_recv()
                    join(plane)

                downward(plane, depth - 1).start()

        def start():
            for order in range(2):
                begin(first_hop(plane_at(order)) + load(order))

        def finish():
            depth = coordinates()[2]

            def plain(span):
                out[span, mine] = wide(plane_sum[depth, span, :])

            over_rows(plain)

            @when(depth > 0)
            def _():
                upward(depth).wait_recv()

                def add(span):
                    out[span, mine] = out[span, mine] + wide(line[depth, span, :])

                over_rows(add)

            @when(depth < 3)
            def _():
                downward(depth, depth).wait_recv()

                def add(span):
                    out[span, mine] = out[span, mine] + wide(line[4, span, :])

                over_rows(add)

            for plane in range(4):
                for copy in first_hop(plane):
                    copy.wait_send()

                @when(plane > depth)
                def _():
                    upward(plane).wait_send()

                @when(plane < depth)
                def _():
                    downward(plane, depth - 1).wait_send()

        return [
            start,
            lambda: pair_sums(0),
            lambda: plane_sums(0),
            lambda: pair_sums(1),
            lambda: pass_on(0),
            lambda: plane_sums(1),
            lambda: pair_sums(2),
            lambda: pass_on(1),
            lambda: plane_sums(2),
            lambda: pair_sums(3),
            lambda: pass_on(2),
            lambda: plane_sums(3),
            finish,
        ]


class ScatterLast:
    def __init__(self, rows, start, width, place):
        self.rows, self.start, self.width, self.place = rows, start, width, place
        self.half = (rows // 2 + 15) // 16 * 16

    def scratch(self):
        rows, width, half = self.rows, self.width, self.half
        return [
            pltpu.VMEM((4, 2, 2, rows, width), LOW),
            pltpu.VMEM((5, 2, 2, rows, width), LOW),
            pltpu.VMEM((2, half, width), LOW),
            pltpu.VMEM((2, rows - half, width), LOW),
            pltpu.VMEM((half, width), LOW),
            pltpu.VMEM((rows - half, width), LOW),
            pltpu.SemaphoreType.DMA((5, 4)),
            pltpu.SemaphoreType.DMA((8,)),
        ]

    def stages(self, terms, out, own, line, got_a, got_b, more_a, more_b, sems, plane_sems):
        rows, half = self.rows, self.half
        columns = pl.ds(self.start, self.width)
        mine = pl.ds(self.place, self.width)
        upper, lower = pl.ds(0, half), pl.ds(half, rows - half)

        def bits():
            quarter = coordinates()[1]
            return lax.rem(quarter, 2), quarter // 2

        def load(plane):
            return pltpu.make_async_copy(
                terms.at[plane, :, :, :, columns], own.at[plane], sems.at[0, plane]
            )

        def upward(plane):
            me = lax.axis_index("expert")
            return send(
                own.at[plane], line.at[plane], sems.at[1, plane], sems.at[2, plane], expert=me + 4
            )

        def downward(plane, receiver):
            me = lax.axis_index("expert")
            slot = plane + (4 - plane) * (1 - jnp.minimum(jnp.abs(plane - receiver), 1))
            return send(
                own.at[plane], line.at[slot], sems.at[3, plane], sems.at[4, plane], expert=me - 4
            )

        def first_hop():
            me, quarter, depth, across, beside = coordinates()
            x, y = bits()
            return (
                send(
                    own.at[depth, 1 - y, :, upper], got_a, plane_sems.at[0], plane_sems.at[1],
                    expert=depth * 4 + beside,
                ),
                send(
                    own.at[depth, :, 1 - x, lower], got_b, plane_sems.at[2], plane_sems.at[3],
                    expert=depth * 4 + across,
                ),
            )

        def second_hop():
            me, quarter, depth, across, beside = coordinates()
            x, y = bits()
            return (
                send(
                    got_a.at[1 - x], more_a, plane_sems.at[4], plane_sems.at[5],
                    expert=depth * 4 + across,
                ),
                send(
                    got_b.at[1 - y], more_b, plane_sems.at[6], plane_sems.at[7],
                    expert=depth * 4 + beside,
                ),
            )

        def join(plane, slot):
            for index in range(4):
                y, x = index // 2, index % 2

                def add(span):
                    own[plane, y, x, span, :] = (
                        wide(own[plane, y, x, span, :]) + wide(line[slot, y, x, span, :])
                    ).astype(LOW)

                by_rows(0, rows, add)

        def start():
            for order in range(4):
                load(plane_at(order)).start()

        def pass_on(order):
            plane = plane_at(order)
            depth = coordinates()[2]
            load(plane).wait()

            @when(plane > depth)
            def _():
                @when(depth > 0)
                def _():
                    upward(plane).wait_recv()
                    join(plane, plane)

                upward(plane).start()

            @when(plane < depth)
            def _():
                @when(depth < 3)
                def _():
                    downward(plane, depth).wait_recv()
                    join(plane, plane)

                downward(plane, depth - 1).start()

        def gather_own():
            depth = coordinates()[2]
            load(depth).wait()

            @when(depth > 0)
            def _():
                upward(depth).wait_recv()
                join(depth, depth)

            @when(depth < 3)
            def _():
                downward(depth, depth).wait_recv()
                join(depth, 4)

            for copy in first_hop():
                copy.start()

        def pair():
            depth = coordinates()[2]
            x, y = bits()
            for copy in first_hop():
                copy.wait_recv()
            for index in range(2):

                def add_a(span):
                    got_a[index, span, :] = (
                        wide(got_a[index, span, :]) + wide(own[depth, y, index, span, :])
                    ).astype(LOW)

                by_rows(0, half, add_a)

                def add_b(span, index=index):
                    there = pl.ds(pl.multiple_of(span.start + half, 16), 16)
                    got_b[index, span, :] = (
                        wide(got_b[index, span, :]) + wide(own[depth, index, x, there, :])
                    ).astype(LOW)

                by_rows(0, rows - half, add_b)
            for copy in second_hop():
                copy.start()

        def finish():
            depth = coordinates()[2]
            x, y = bits()
            for copy in second_hop():
                copy.wait_recv()

            def total_a(span):
                out[span, mine] = wide(got_a[x, span, :]) + wide(more_a[span, :])

            by_rows(0, half, total_a)

            def total_b(span):
                there = pl.ds(pl.multiple_of(span.start + half, 16), 16)
                out[there, mine] = wide(got_b[y, span, :]) + wide(more_b[span, :])

            by_rows(0, rows - half, total_b)
            for copy in first_hop() + second_hop():
                copy.wait_send()
            for plane in range(4):

                @when(plane > depth)
                def _(plane=plane):
                    upward(plane).wait_send()

                @when(plane < depth)
                def _(plane=plane):
                    downward(plane, depth - 1).wait_send()

        return [start] + [lambda k=k: pass_on(k) for k in range(3)] + [gather_own, pair, finish]


class Direct:
    def scratch(self):
        return [pltpu.SemaphoreType.DMA((2, 16)), pltpu.SemaphoreType.DMA((1,))]

    def stages(self, source, out, sems, own_sem):
        def copy(step):
            me = lax.axis_index("expert")
            peer = lax.rem(me + step, 16)
            return send(source.at[peer], out.at[me], sems.at[0, peer], sems.at[1, me], expert=peer)

        def own():
            me = lax.axis_index("expert")
            return pltpu.make_async_copy(source.at[me], out.at[me], own_sem.at[0])

        def begin():
            own().start()
            for step in range(1, 16):
                copy(step).start()

        def finish():
            own().wait()
            me = lax.axis_index("expert")
            for step in range(1, 16):
                copy(step).wait_send()
                peer = lax.rem(me + step, 16)
                landed = send(
                    source.at[peer], out.at[peer], sems.at[0, peer], sems.at[1, peer], expert=peer
                )
                landed.wait_recv()

        return [begin, finish]


class Exchange:
    def __init__(self, peers, split):
        self.peers, self.split = peers, split

    def scratch(self):
        return [pltpu.SemaphoreType.DMA((2, self.peers - 1))]

    def stages(self, source, out, sems):
        def copies():
            side = lax.axis_index("fsdp")
            for step in range(1, self.peers):
                peer = lax.rem(side - step + self.peers, self.peers)
                part = source
                if self.split:
                    width = source.shape[1] // self.peers
                    part = source.at[:, pl.ds(pl.multiple_of(peer * width, 128), width)]
                yield send(
                    part, out.at[step - 1], sems.at[0, step - 1], sems.at[1, step - 1], fsdp=peer
                )

        def begin():
            for copy in copies():
                copy.start()

        def finish():
            for copy in copies():
                copy.wait()

        return [begin, finish]


class Work:
    def __init__(self, steps, inputs, outputs, body, scratch=(), held=()):
        self.steps, self.inputs, self.outputs, self.body = steps, inputs, outputs, body
        self.scratch, self.held = list(scratch), list(held)


def in_turn(lists):
    placed = []
    for number, one in enumerate(lists):
        for index, stage in enumerate(one[:-1]):
            placed.append((index / (len(one) - 1), number, index, stage))
    placed.sort(key=lambda item: item[:3])
    return [item[3] for item in placed] + [lambda: [one[-1]() for one in lists]]


def last_columns(width):
    return width // 4 // 128 * 128


def carry(
    name,
    collective_id,
    peers,
    gathers=(),
    scatters=(),
    directs=(),
    exchanges=(),
    works=(),
    lead=0,
    vmem=60,
):
    steps = max(1, sum(work.steps for work in works))
    any_spec = pl.BlockSpec(memory_space=pl.ANY)
    vmem_spec = pl.BlockSpec(memory_space=pltpu.VMEM)
    operands, in_specs, out_shapes, out_specs, scratch = [], [], [], [], []
    programs, places = [], []

    def add(array, out_shape, out_spec, *mine):
        for program in mine:
            programs.append(program)
            places.append((len(operands), len(out_shapes)))
        operands.append(array)
        in_specs.append(any_spec)
        out_shapes.append(out_shape)
        out_specs.append(out_spec)

    for block, own in gathers:
        rows, width = own.shape
        last = last_columns(width)
        mine = [Gather(rows, width - last, block)]
        if last:
            mine.append(GatherLast(rows, width - last, last, block))
        add(own, jax.ShapeDtypeStruct((block, 16, rows, width), own.dtype), any_spec, *mine)
    for terms, start, width in scatters:
        rows, columns = terms.shape[1:]
        last = last_columns(width)
        mine = [Scatter(rows, start, width - last)]
        if last:
            mine.append(ScatterLast(rows, start + width - last, last, width - last))
        add(
            terms.reshape(4, 2, 2, rows, columns),
            jax.ShapeDtypeStruct((rows, width), jnp.float32),
            vmem_spec,
            *mine,
        )
    for blocks in directs:
        add(blocks, jax.ShapeDtypeStruct(blocks.shape, blocks.dtype), any_spec, Direct())
    for array, split in exchanges:
        rows, width = array.shape
        width = width // peers if split else width
        shape = jax.ShapeDtypeStruct((peers - 1, rows, width), array.dtype)
        add(array, shape, any_spec, Exchange(peers, split))
    transfers = len(operands)
    scratch_counts = []
    for program in programs:
        shapes = program.scratch()
        scratch_counts.append(len(shapes))
        scratch += shapes
    begun = 0
    spans = []
    for work in works:
        def local(index, begun=begun, steps=work.steps):
            return jnp.clip(index - begun, 0, steps - 1)

        for array, shape, index_of in work.inputs:
            operands.append(array)
            in_specs.append(pl.BlockSpec(shape, lambda i, f=index_of, at=local: f(at(i))))
        for array, shape, _ in work.held:
            if isinstance(array, int):
                scratch.append(pltpu.VMEM(shape, out_shapes[array].dtype))
                continue
            operands.append(array)
            in_specs.append(any_spec)
            scratch.append(pltpu.VMEM(shape, array.dtype))
        if work.held:
            scratch.append(pltpu.SemaphoreType.DMA((len(work.held),)))
        for shape, dtype, block_shape, index_of in work.outputs:
            out_shapes.append(jax.ShapeDtypeStruct(shape, dtype))
            out_specs.append(pl.BlockSpec(block_shape, lambda i, f=index_of, at=local: f(at(i))))
        scratch += work.scratch
        spans.append((begun, begun + work.steps))
        begun += work.steps
    counts = (len(operands), len(out_shapes))

    def kernel(*refs):
        ins = refs[: counts[0]]
        outs = refs[counts[0] : counts[0] + counts[1]]
        rest = list(refs[counts[0] + counts[1] :])
        step = pl.program_id(0)
        lists = []
        for index, program in enumerate(programs):
            mine, rest = rest[: scratch_counts[index]], rest[scratch_counts[index] :]
            in_place, out_place = places[index]
            lists.append(program.stages(ins[in_place], outs[out_place], *mine))
        at = {0: [one[0] for one in lists[:lead]]}
        if lead:
            at[0] += [one[0] for one in lists[lead:]]
            at[0] += in_turn([one[1:] for one in lists[:lead]])
            lists = [one[1:] for one in lists[lead:]]
        stages = in_turn(lists)
        for index, stage in enumerate(stages):
            place = index * steps // len(stages) if index + 1 < len(stages) else steps - 1
            if lead:
                place = max(place, min(1, steps - 1))
            at.setdefault(place, []).append(stage)
        in_at, out_at = transfers, transfers
        holds, tasks = [], []
        for work, (low, high) in zip(works, spans):
            work_ins = list(ins[in_at : in_at + len(work.inputs)])
            in_at += len(work.inputs)
            sources = []
            for array, _, _ in work.held:
                sources.append(None if isinstance(array, int) else ins[in_at])
                in_at += not isinstance(array, int)
            work_outs = outs[out_at : out_at + len(work.outputs)]
            out_at += len(work.outputs)
            if work.held:
                held, sems, rest = rest[: len(sources)], rest[len(sources)], rest[len(sources) + 1 :]
                for index, (array, _, view) in enumerate(work.held):
                    source = outs[array] if isinstance(array, int) else sources[index]
                    holds.append((view(source), held[index], sems.at[index]))
                work_ins += held
            own, rest = rest[: len(work.scratch)], rest[len(work.scratch) :]
            tasks.append((work, low, high, work_ins, work_outs, own))
        for place in sorted(at):
            def act(place=place):
                if place == 0:
                    enter(peers, len(directs) > 0)
                for stage in at[place]:
                    stage()
                if place == 0:
                    for action in ("start", "wait"):
                        for hold in holds:
                            getattr(pltpu.make_async_copy(*hold), action)()

            if steps == 1:
                act()
            else:
                pl.when(step == place)(act)
        for work, low, high, work_ins, work_outs, own in tasks:
            def do(work=work, low=low, work_ins=work_ins, work_outs=work_outs, own=own):
                work.body(step - low, work_ins, work_outs, *own)

            if len(works) == 1:
                do()
            else:
                pl.when((step >= low) & (step < high))(do)

    return pl.pallas_call(
        kernel,
        name=name,
        grid=(steps,),
        out_shape=out_shapes,
        in_specs=in_specs,
        out_specs=out_specs,
        scratch_shapes=scratch,
        compiler_params=pltpu.CompilerParams(
            collective_id=collective_id,
            has_side_effects=True,
            vmem_limit_bytes=vmem * 1024 * 1024,
            dimension_semantics=("arbitrary",),
        ),
    )(*operands)


def tile_of(size):
    return 512 if size % 512 == 0 else size


def weight_parts(own, others):
    count, share, hidden = others.shape
    if share % 128:
        side = lax.axis_index("fsdp")
        mine = lax.dynamic_slice_in_dim(own, side * hidden, hidden, 1)
        twice = jnp.concatenate([mine] + [others[i] for i in range(count)], axis=0)
        twice = jnp.concatenate([twice, twice], axis=0)
        start = lax.rem(count + 1 - side, count + 1) * share
        whole = lax.dynamic_slice_in_dim(twice, start, (count + 1) * share, 0)
        return [(whole, whole.shape, lambda ref: ref)]

    def own_view(ref):
        start = pl.multiple_of(lax.axis_index("fsdp") * hidden, 128)
        return ref.at[:, pl.ds(start, hidden)]

    return [(own, (share, hidden), own_view)] + [
        (others, (share, hidden), lambda ref, w=w: ref.at[w]) for w in range(count)
    ]


def down_back(upstream, down):
    total, model = upstream.shape
    hidden = down.shape[0]
    tile = tile_of(hidden)
    across = hidden // tile

    def body(step, ins, outs):
        part = pl.ds(pl.multiple_of(lax.rem(step, across) * tile, tile), tile)
        outs[0][...] = dot_nt(ins[0][...], ins[1][part, :]).astype(LOW)

    return Work(
        total // 512 * across,
        [(upstream, (512, model), lambda s: (s // across, 0))],
        [((total, hidden), LOW, (512, tile), lambda s: (s // across, lax.rem(s, across)))],
        body,
        held=[(down, down.shape, lambda ref: ref)],
    )


def hidden_units(rows_all, d_act, gates, ups, tokens, groups):
    total, model = rows_all.shape
    count = len(gates)
    share, hidden = gates[0][1]
    tile = tile_of(hidden)
    across, height = hidden // tile, 256
    each, holds = total // groups // height, height // tokens

    def body(step, ins, outs, own_gate, own_up):
        part = pl.ds(pl.multiple_of(lax.rem(step, across) * tile, tile), tile)
        side = lax.axis_index("fsdp")
        me = lax.axis_index("expert")
        weights = ins[2:]
        pre_gate = pre_up = None
        for which in range(count):
            start = 0
            if count > 1:
                start = pl.multiple_of(lax.rem(side + which, count) * share, 128)
            rows = ins[0][:, pl.ds(start, share)]
            more_gate = dot_nn(rows, weights[which][:, part])
            more_up = dot_nn(rows, weights[count + which][:, part])
            pre_gate = more_gate if pre_gate is None else pre_gate + more_gate
            pre_up = more_up if pre_up is None else pre_up + more_up
        grad = ins[1][...].astype(jnp.float32)
        sigma = 1.0 / (1.0 + jnp.exp(-pre_gate))
        silu = pre_gate * sigma
        outs[0][...] = (silu * pre_up).astype(LOW)
        outs[1][...] = (grad * pre_up * (sigma * (1.0 + pre_gate * (1.0 - sigma)))).astype(LOW)
        outs[2][...] = (grad * silu).astype(LOW)
        row_tile = step // across

        @pl.when(lax.rem(row_tile, each) == 0)
        def _():
            here = pl.ds(pl.multiple_of(lax.rem(me, holds) * tokens, tokens), tokens)
            there = pl.ds(pl.multiple_of(row_tile // each * tokens, tokens), tokens)
            own_gate[there, part] = outs[1][here, :]
            own_up[there, part] = outs[2][here, :]

        for which in range(count):

            @pl.when(step == (groups - 1) * each * across + across + which)
            def _(which=which):
                start = 0
                if count > 1:
                    start = pl.multiple_of(lax.rem(side + which, count) * share, 128)
                outs[3][:, pl.ds(start, share)] = (
                    dot_nt(own_gate[...], weights[which][...])
                    + dot_nt(own_up[...], weights[count + which][...])
                ).astype(LOW)

    def row_tile(s):
        number = s // across
        turned = lax.rem(lax.rem(number, each) + lax.axis_index("expert") // holds, each)
        return number // each * each + turned

    def spot(s):
        return row_tile(s), lax.rem(s, across)

    return Work(
        total // height * across,
        [(rows_all, (height, model), lambda s: (row_tile(s), 0)), (d_act, (height, tile), spot)],
        [((total, hidden), LOW, (height, tile), spot)] * 3
        + [((groups * tokens, model), LOW, (groups * tokens, model), lambda s: (0, 0))],
        body,
        [pltpu.VMEM((groups * tokens, hidden), LOW)] * 2,
        held=list(gates) + list(ups),
    )


def turned_products(left, rights, dtype, depth):
    total, height = left.shape
    width = rights[0].shape[1]
    tall, tile = tile_of(height), tile_of(width)
    across, deep = width // tile, total // depth

    def body(step, ins, outs, turned, *sums):
        now = lax.rem(step, deep)
        span = pl.ds(pl.multiple_of(now * depth, depth), depth)

        @pl.when(lax.rem(step // deep, across) == 0)
        def _():
            turned[:, span] = ins[0][...].T

        for which in range(len(rights)):
            product = dot_nn(turned[:, span], ins[1 + which][...])
            if deep == 1:
                outs[which][...] = product.astype(dtype)
            else:
                sums[which][...] = jnp.where(now == 0, 0.0, sums[which][...]) + product

        if deep > 1:

            @pl.when(now == deep - 1)
            def _():
                for which in range(len(rights)):
                    outs[which][...] = sums[which][...].astype(dtype)

    def left_spot(s):
        first = lax.rem(s // deep, across) == 0
        return jnp.where(first, lax.rem(s, deep), deep - 1), s // (deep * across)

    def right_spot(s):
        return lax.rem(s, deep), lax.rem(s // deep, across)

    work = Work(
        height // tall * across * deep,
        [(left, (depth, tall), left_spot)]
        + [(right, (depth, tile), right_spot) for right in rights],
        [
            (
                (height, width),
                dtype,
                (tall, tile),
                lambda s: (s // (deep * across), lax.rem(s // deep, across)),
            )
        ]
        * len(rights),
        body,
        [pltpu.VMEM((tall, total), left.dtype)]
        + [pltpu.VMEM((tall, tile), jnp.float32)] * (len(rights) if deep > 1 else 0),
    )
    work.flops = 2 * total * height * width * len(rights)
    work.traffic = 2 * total * (height + len(rights) * width * (height // tall))
    return work


def alone(name, work, vmem=60):
    count = len(work.inputs)

    def kernel(*refs):
        outs = refs[count : count + len(work.outputs)]
        work.body(pl.program_id(0), refs[:count], outs, *refs[count + len(work.outputs) :])

    return pl.pallas_call(
        kernel,
        name=name,
        grid=(work.steps,),
        in_specs=[
            pl.BlockSpec(shape, index_of) for _, shape, index_of in work.inputs
        ],
        out_specs=[pl.BlockSpec(shape, index_of) for _, _, shape, index_of in work.outputs],
        out_shape=[jax.ShapeDtypeStruct(shape, dtype) for shape, dtype, _, _ in work.outputs],
        scratch_shapes=work.scratch,
        compiler_params=pltpu.CompilerParams(vmem_limit_bytes=vmem * 1024 * 1024),
        cost_estimate=pl.CostEstimate(
            flops=work.flops, bytes_accessed=work.traffic, transcendentals=0
        ),
    )(*[array for array, _, _ in work.inputs])


CHUNK = 256


def tile_columns(value, count):
    return jnp.concatenate([value] * count, axis=1)


def stacked(ref, count):
    return jnp.concatenate(
        [ref[:, index * HEAD_DIM : (index + 1) * HEAD_DIM] for index in range(count)], axis=0
    )


def unstacked(turned, count, tokens):
    return jnp.concatenate(
        [turned[:, index * tokens : (index + 1) * tokens].T for index in range(count)], axis=1
    )


def chunks_of(ref, columns=None):
    def chunk(index):
        if columns is None:
            return ref[pl.ds(pl.multiple_of(index * CHUNK, CHUNK), CHUNK), :]
        blocks = CHUNK // ref.shape[1]
        return ref[pl.ds(index * blocks, blocks), :, columns].reshape(CHUNK, HEAD_DIM)

    return chunk


def chunk_scores(keys, queries, key_labels, query_labels, chunk, place, count):
    tokens = queries.shape[0] // count
    span = pl.ds(pl.multiple_of(chunk * CHUNK, CHUNK), CHUNK)
    raw = dot_nt(keys(chunk), queries) * HEAD_DIM ** (-0.5)
    row = chunk * CHUNK + lax.broadcasted_iota(jnp.int32, (CHUNK, tokens), 0)
    column = place * tokens + lax.broadcasted_iota(jnp.int32, (CHUNK, tokens), 1)
    allowed = (key_labels[span, :] == query_labels[...]) & (row <= column)
    bias = jnp.where(allowed, 0.0, masked_score)
    return span, raw + tile_columns(bias, count)


def attend_kernel(place, q_ref, keys, values, kl_ref, ql_ref, out_ref, log_ref, score_ref):
    tokens = q_ref.shape[0]
    count = q_ref.shape[1] // HEAD_DIM
    queries = stacked(q_ref, count)
    chunks = kl_ref.shape[0] // CHUNK

    def scores(chunk, top):
        span, value = chunk_scores(keys, queries, kl_ref, ql_ref, chunk, place[0], count)
        score_ref[span, :] = value
        return jnp.maximum(top, jnp.max(value, axis=0, keepdims=True))

    top = lax.fori_loop(
        0, chunks, scores, jnp.full((1, count * tokens), masked_score, jnp.float32)
    )

    def mix(chunk, carried):
        total, mixed = carried
        span = pl.ds(pl.multiple_of(chunk * CHUNK, CHUNK), CHUNK)
        prob = jnp.exp(score_ref[span, :] - top)
        return (
            total + jnp.sum(prob, axis=0, keepdims=True),
            mixed + dot_tn(values(chunk), prob.astype(LOW)),
        )

    total, mixed = lax.fori_loop(
        0,
        chunks,
        mix,
        (
            jnp.zeros((1, count * tokens), jnp.float32),
            jnp.zeros((HEAD_DIM, count * tokens), jnp.float32),
        ),
    )
    out_ref[...] = unstacked(mixed / total, count, tokens).astype(LOW)
    log_ref[0] = jnp.broadcast_to(top + jnp.log(total), log_ref.shape[1:])


def attend_back_kernel(
    place, q_ref, k_ref, v_ref, kl_ref, ql_ref, grad_ref, log_ref, dq_ref, pair_ref, p_ref, dp_ref
):
    tokens = q_ref.shape[0]
    count = q_ref.shape[1] // HEAD_DIM
    queries = stacked(q_ref, count)
    grads = stacked(grad_ref, count)
    chunks = k_ref.shape[0] // CHUNK
    keys, values = chunks_of(k_ref), chunks_of(v_ref)
    log_total = log_ref[0, 0:1, :]
    scale = HEAD_DIM ** (-0.5)

    def probs(chunk, row_dot):
        span, value = chunk_scores(keys, queries, kl_ref, ql_ref, chunk, place[0], count)
        prob = jnp.exp(value - log_total)
        d_prob = dot_nt(values(chunk), grads)
        p_ref[span, :] = prob
        dp_ref[span, :] = d_prob
        return row_dot + jnp.sum(prob * d_prob, axis=0, keepdims=True)

    row_dot = lax.fori_loop(
        0, chunks, probs, jnp.zeros((1, count * tokens), jnp.float32)
    )

    def back(chunk, d_query):
        span = pl.ds(pl.multiple_of(chunk * CHUNK, CHUNK), CHUNK)
        prob = p_ref[span, :]
        d_score = (prob * (dp_ref[span, :] - row_dot)).astype(LOW)
        pair_ref[span, :HEAD_DIM] = (dot_nn(d_score, queries) * scale).astype(LOW)
        pair_ref[span, HEAD_DIM:] = dot_nn(prob.astype(LOW), grads).astype(LOW)
        return d_query + dot_tn(keys(chunk), d_score)

    d_query = lax.fori_loop(
        0, chunks, back, jnp.zeros((HEAD_DIM, count * tokens), jnp.float32)
    )
    dq_ref[...] = unstacked(d_query * scale, count, tokens)


def attention_specs(tokens, length, group):
    return [
        pl.BlockSpec(memory_space=pltpu.SMEM),
        pl.BlockSpec((tokens, group), lambda g: (0, g)),
        pl.BlockSpec((length, HEAD_DIM), lambda g: (0, g)),
        pl.BlockSpec((length, HEAD_DIM), lambda g: (0, KEY_HEADS + g)),
        pl.BlockSpec((length, 1), lambda g: (0, 0)),
        pl.BlockSpec((1, tokens), lambda g: (0, 0)),
    ]


def attend_work(queries, pairs_at, key_labels, query_labels):
    tokens, width = queries.shape
    length, group = key_labels.shape[0], width // KEY_HEADS
    stack = group // HEAD_DIM * tokens
    pair_width = 2 * KEY_HEADS * HEAD_DIM

    def body(step, ins, outs, scores):
        q_ref, kl_ref, ql_ref, pairs = ins
        start = pl.multiple_of(step * HEAD_DIM, HEAD_DIM)
        keys = chunks_of(pairs, pl.ds(start, HEAD_DIM))
        values = chunks_of(pairs, pl.ds(KEY_HEADS * HEAD_DIM + start, HEAD_DIM))
        place = [lax.axis_index("expert")]
        attend_kernel(place, q_ref, keys, values, kl_ref, ql_ref, *outs, scores)

    return Work(
        KEY_HEADS,
        [
            (queries, (tokens, group), lambda s: (0, s)),
            (key_labels, (length, 1), lambda s: (0, 0)),
            (query_labels, (1, tokens), lambda s: (0, 0)),
        ],
        [
            ((tokens, width), LOW, (tokens, group), lambda s: (0, s)),
            ((KEY_HEADS, 8, stack), jnp.float32, (1, 8, stack), lambda s: (s, 0, 0)),
        ],
        body,
        [pltpu.VMEM((length, stack), jnp.float32)],
        held=[
            (
                pairs_at,
                (length // tokens, tokens, pair_width),
                lambda ref: ref.at[0, :, :, pl.ds(0, pair_width)],
            )
        ],
    )


def attend_back(place, queries, pairs, key_labels, query_labels, grads, log_total):
    tokens, width = queries.shape
    length, group = pairs.shape[0], width // KEY_HEADS
    stack = group // HEAD_DIM * tokens
    return pl.pallas_call(
        attend_back_kernel,
        name="attend_back",
        grid=(KEY_HEADS,),
        in_specs=attention_specs(tokens, length, group)
        + [
            pl.BlockSpec((tokens, group), lambda g: (0, g)),
            pl.BlockSpec((1, 8, stack), lambda g: (g, 0, 0)),
        ],
        out_specs=[
            pl.BlockSpec((tokens, group), lambda g: (0, g)),
            pl.BlockSpec((length, 2 * HEAD_DIM), lambda g: (0, g)),
        ],
        out_shape=[
            jax.ShapeDtypeStruct((tokens, width), jnp.float32),
            jax.ShapeDtypeStruct((length, 2 * KEY_HEADS * HEAD_DIM), LOW),
        ],
        scratch_shapes=[pltpu.VMEM((length, stack), jnp.float32)] * 2,
        compiler_params=pltpu.CompilerParams(vmem_limit_bytes=50 * 1024 * 1024),
    )(place, queries, pairs, pairs, key_labels, query_labels, grads, log_total)


def dispatch_kernel(place, n_ref, u_ref, p_ref, m_ref, w_ref, rows_ref, up_ref, pair_ref, g_ref):
    rows = n_ref[0]
    pick = p_ref[0]
    logits = dot_nt(w_ref[...], rows)
    chosen = m_ref[...] > 0.5
    top = jnp.max(jnp.where(chosen, logits, masked_score), axis=0, keepdims=True)
    power = jnp.where(chosen, jnp.exp(jnp.where(chosen, logits - top, 0.0)), 0.0)
    mine = lax.broadcasted_iota(jnp.int32, logits.shape, 0) == place[0]
    gate = jnp.sum(jnp.where(mine, power, 0.0), axis=0, keepdims=True) / jnp.sum(
        power, axis=0, keepdims=True
    )
    slot_gate = jnp.sum(pick.astype(jnp.float32) * gate, axis=1, keepdims=True)
    rows_ref[...] = dot_nn(pick, rows).astype(LOW)
    ups = dot_nn(pick, u_ref[...])
    up_ref[...] = ups.astype(LOW)
    pair_ref[...] = (slot_gate * ups).astype(LOW)
    g_ref[...] = slot_gate


def dispatch(place, normed, upstream, pick, chosen, w_router):
    blocks, capacity, tokens = pick.shape
    model = upstream.shape[1]
    experts = w_router.shape[0]
    wide = pl.BlockSpec((capacity, model), lambda b: (b, 0))
    return pl.pallas_call(
        dispatch_kernel,
        name="dispatch",
        grid=(blocks,),
        in_specs=[
            pl.BlockSpec(memory_space=pltpu.SMEM),
            pl.BlockSpec((1, tokens, model), lambda b: (b, 0, 0)),
            pl.BlockSpec((tokens, model), lambda b: (b, 0)),
            pl.BlockSpec((1, capacity, tokens), lambda b: (b, 0, 0)),
            pl.BlockSpec((experts, tokens), lambda b: (0, b)),
            pl.BlockSpec((experts, model), lambda b: (0, 0)),
        ],
        out_specs=[wide, wide, wide, pl.BlockSpec((capacity, 1), lambda b: (b, 0))],
        out_shape=[jax.ShapeDtypeStruct((blocks * capacity, model), LOW)] * 3
        + [jax.ShapeDtypeStruct((blocks * capacity, 1), jnp.float32)],
    )(place, normed, upstream, pick, chosen, w_router)


def join_columns(side, groups, own, others):
    rows, columns = others[0].shape
    tile = rows // 10

    def kernel(side_ref, *refs):
        for step, ref in enumerate(refs[:-1]):
            start = lax.rem(side_ref[0] + step, groups) * columns
            refs[-1][:, pl.ds(pl.multiple_of(start, 128), columns)] = ref[...].astype(jnp.float32)

    return pl.pallas_call(
        kernel,
        name="join_columns",
        grid_spec=pltpu.PrefetchScalarGridSpec(
            num_scalar_prefetch=1,
            grid=(10,),
            in_specs=[pl.BlockSpec((tile, columns), lambda i, side: (side[0] * 10 + i, 0))]
            + [pl.BlockSpec((tile, columns), lambda i, side: (i, 0))] * len(others),
            out_specs=pl.BlockSpec((tile, groups * columns), lambda i, side: (i, 0)),
        ),
        out_shape=jax.ShapeDtypeStruct((rows, groups * columns), jnp.float32),
    )(side, own, *others)


def widen(arrays, cuts):
    rows = arrays[0].shape[0]
    steps = 10 if rows % 10 == 0 else 12
    tile = rows // steps
    widths = [
        [high - low for low, high in zip([0] + cut, cut + [array.shape[1]])]
        for array, cut in zip(arrays, cuts)
    ]

    def kernel(*refs):
        outs = iter(refs[len(arrays) :])
        for ref, parts in zip(refs, widths):
            start = 0
            for part in parts:
                next(outs)[...] = ref[:, start : start + part].astype(jnp.float32)
                start += part

    flat = [part for parts in widths for part in parts]
    return pl.pallas_call(
        kernel,
        name="widen",
        grid=(steps,),
        in_specs=[pl.BlockSpec((tile, array.shape[1]), lambda i: (i, 0)) for array in arrays],
        out_specs=[pl.BlockSpec((tile, part), lambda i: (i, 0)) for part in flat],
        out_shape=[jax.ShapeDtypeStruct((rows, part), jnp.float32) for part in flat],
    )(*arrays)


def expert_kernel(
    count, side, rows_ref, up_ref, pair_ref, gate_ref, back_ref, *refs
):
    w_gate, w_up, w_down = refs[:count], refs[count : 2 * count], refs[2 * count : 3 * count]
    act_ref, dg_ref, du_ref, d_gate_ref, out_ref, term_ref = refs[3 * count :]
    share = w_gate[0].shape[0]
    units = w_down[0].shape[0]
    model = rows_ref.shape[1]
    blocks, tokens, capacity = back_ref.shape

    def place(which, size):
        if count == 1:
            return pl.ds(0, size)
        return pl.ds(pl.multiple_of(lax.rem(side[0] + which, count) * size, 128), size)

    for which in range(count):
        span = place(which, units)
        pre_gate = pre_up = None
        for part in range(count):
            rows = rows_ref[:, place(part, share)]
            more_gate = dot_nn(rows, w_gate[part][:, span])
            more_up = dot_nn(rows, w_up[part][:, span])
            pre_gate = more_gate if pre_gate is None else pre_gate + more_gate
            pre_up = more_up if pre_up is None else pre_up + more_up
        d_act = dot_nt(pair_ref[...], w_down[which][...])
        sigma = 1.0 / (1.0 + jnp.exp(-pre_gate))
        silu = pre_gate * sigma
        act_ref[:, span] = (silu * pre_up).astype(LOW)
        dg_ref[:, span] = (
            d_act * pre_up * (sigma * (1.0 + pre_gate * (1.0 - sigma)))
        ).astype(LOW)
        du_ref[:, span] = (d_act * silu).astype(LOW)

    def returned(target, values, span):
        for block in range(blocks):
            mine = values[block * capacity : (block + 1) * capacity]
            target[block, :, span] = dot_nn(back_ref[block], mine).astype(LOW)

    d_gate = jnp.zeros(d_gate_ref.shape, jnp.float32)
    tile = tile_of(model)
    for index in range(model // tile):
        span = pl.ds(index * tile, tile)
        produced = None
        for part in range(count):
            more = dot_nn(act_ref[:, place(part, units)], w_down[part][:, span])
            produced = more if produced is None else produced + more
        produced = produced.astype(LOW).astype(jnp.float32)
        d_gate += jnp.sum(produced * up_ref[:, span].astype(jnp.float32), axis=1, keepdims=True)
        returned(out_ref, (gate_ref[...] * produced).astype(LOW), span)
    d_gate_ref[...] = d_gate
    for part in range(count):
        pieces = 2 if share % 256 == 0 else 1
        for piece in range(pieces):
            width = share // pieces
            rows = pl.ds(piece * width, width)
            d_rows = dot_nt(dg_ref[...], w_gate[part][rows, :]) + dot_nt(
                du_ref[...], w_up[part][rows, :]
            )
            start = piece * width
            if count > 1:
                start = pl.multiple_of(lax.rem(side[0] + part, count) * share + start, 128)
            returned(term_ref, d_rows.astype(LOW), pl.ds(start, width))


def run_expert(side, rows_in, rows_up, d_pair, slot_gate, pick, gates, ups, downs):
    slots, model = rows_in.shape
    blocks, capacity, tokens = pick.shape
    hidden = gates[0].shape[1]
    count = len(gates)
    group = 4
    tile = group * capacity
    wide = pl.BlockSpec((tile, model), lambda i, side: (i, 0))
    narrow = pl.BlockSpec((tile, hidden), lambda i, side: (i, 0))
    single = pl.BlockSpec((tile, 1), lambda i, side: (i, 0))
    terms = pl.BlockSpec((group, tokens, model), lambda i, side: (i, 0, 0))
    weights = list(gates) + list(ups) + list(downs)

    def kernel(*refs):
        expert_kernel(count, *refs)

    return pl.pallas_call(
        kernel,
        name="expert",
        grid_spec=pltpu.PrefetchScalarGridSpec(
            num_scalar_prefetch=1,
            grid=(blocks // group,),
            in_specs=[
                wide,
                wide,
                wide,
                single,
                pl.BlockSpec((group, tokens, capacity), lambda i, side: (i, 0, 0)),
            ]
            + [
                pl.BlockSpec(w.shape, lambda i, side: (0, 0), pipeline_mode=pl.Buffered(1))
                for w in weights
            ],
            out_specs=[narrow, narrow, narrow, single, terms, terms],
        ),
        out_shape=[jax.ShapeDtypeStruct((slots, hidden), LOW)] * 3
        + [jax.ShapeDtypeStruct((slots, 1), jnp.float32)]
        + [jax.ShapeDtypeStruct((blocks, tokens, model), LOW)] * 2,
        compiler_params=pltpu.CompilerParams(vmem_limit_bytes=60 * 1024 * 1024),
    )(side, rows_in, rows_up, d_pair, slot_gate, pick.transpose(0, 2, 1), *weights)


def local(
    hidden_in,
    gain_attn,
    query_weight,
    key_matrix,
    value_matrix,
    out_weight,
    gain_ffn,
    router_weight,
    shared_gate,
    shared_up,
    shared_down,
    expert_gate,
    expert_up,
    expert_down,
    routes,
    segments,
    positions,
    grad_out,
):
    tokens = hidden_in.shape[1]
    model = hidden_in.shape[2]
    experts = lax.axis_size("expert")
    groups = lax.axis_size("fsdp")
    topk = routes.shape[2]
    capacity = min(tokens, 4 * tokens * topk // (3 * experts))
    length = tokens * experts
    group_width = QUERY_HEADS // KEY_HEADS
    score_scale = HEAD_DIM ** (-0.5)
    place = lax.axis_index("expert")
    side = lax.axis_index("fsdp")
    share = model // groups

    def peer(values, step):
        if step == 0:
            return values
        return lax.ppermute(
            values, "fsdp", [((i + step) % groups, i) for i in range(groups)]
        )

    def ring(values):
        return [peer(values, step) for step in range(groups)]

    def scattered(values, axis):
        size = values.shape[axis] // groups
        return [
            peer(
                lax.dynamic_slice_in_dim(
                    values, ((side - step + groups) % groups) * size, size, axis
                ),
                step,
            )
            for step in range(groups)
        ]

    def in_order(parts, axis):
        if groups == 2:
            first = side == 0
            return jnp.concatenate(
                [jnp.where(first, parts[0], parts[1]), jnp.where(first, parts[1], parts[0])], axis
            )
        size = parts[0].shape[axis]
        twice = jnp.concatenate(parts + parts, axis)
        start = ((groups - side) % groups) * size
        return lax.dynamic_slice_in_dim(twice, start, groups * size, axis)

    def own_columns(values, step):
        size = values.shape[-1] // groups
        return lax.dynamic_slice_in_dim(values, ((side + step) % groups) * size, size, 1)

    def rows_product(values, parts):
        if len(parts) == 1:
            return dot_nn(values, parts[0])
        total = dot_nn(own_columns(values, 0), parts[0])
        for step in range(1, groups):
            total = total + dot_nn(own_columns(values, step), parts[step])
        return total

    small = jnp.concatenate([gain_attn[None], gain_ffn[None], router_weight.T], axis=0)
    small_full = in_order(ring(small), 1)
    gain_first = small_full[0].astype(jnp.float32)
    gain_second = small_full[1].astype(jnp.float32)
    w_router = small_full[2:]
    w_query, w_key, w_value, w_out = (
        ring(query_weight),
        ring(key_matrix),
        ring(value_matrix),
        ring(out_weight),
    )
    expert_ids = jnp.arange(experts, dtype=jnp.int32)
    chosen = jnp.any(routes[0][:, :, None] == expert_ids[None, None, :], axis=1)
    upstream_low = grad_out[0]
    upstream = upstream_low.astype(jnp.float32)

    x_rows = hidden_in[0].astype(jnp.float32)
    labels = segments[0]
    cosine, sine = rope_tables(positions[0])
    normed_one = rms_scale(x_rows, gain_first).astype(LOW)
    key_rows = rotate(
        rows_product(normed_one, w_key).reshape(tokens, KEY_HEADS, HEAD_DIM), cosine, sine
    ).astype(LOW)
    value_rows = rows_product(normed_one, w_value).astype(LOW)
    wide = KEY_HEADS * HEAD_DIM
    pair_rows = jnp.concatenate(
        [
            key_rows.reshape(tokens, wide),
            value_rows,
            jnp.pad(chosen.astype(LOW), ((0, 0), (0, 128 - experts))),
        ],
        axis=1,
    )
    here = place.reshape(1)
    queries = (
        rotate(
            rows_product(normed_one, w_query).reshape(tokens, QUERY_HEADS, HEAD_DIM), cosine, sine
        )
        .astype(LOW)
        .reshape(tokens, QUERY_HEADS * HEAD_DIM)
    )
    key_labels = labels[:, None]
    query_labels = lax.dynamic_slice_in_dim(labels, place * tokens, tokens)[None]
    (
        every_pair,
        upstream_each,
        gate_others,
        up_others,
        eg_others,
        eu_others,
        ed_others,
        attended,
        log_total,
    ) = carry(
        "attend",
        7,
        groups,
        gathers=[(1, pair_rows), (groups, upstream_low)],
        exchanges=[
            (shared_gate, True),
            (shared_up, True),
            (expert_gate[0], False),
            (expert_up[0], False),
            (expert_down[0], False),
        ],
        works=[attend_work(queries, 0, key_labels, query_labels)],
        lead=2,
    )
    every_pair = every_pair.reshape(length, 2 * wide + 128)
    chosen_all = every_pair[:, 2 * wide : 2 * wide + experts].T.astype(jnp.float32)
    upstream_each = upstream_each.reshape(groups * length, model)
    residual_one = x_rows + rows_product(attended, w_out)
    normed_two = rms_scale(residual_one, gain_second).astype(LOW)

    gate_parts = weight_parts(shared_gate, gate_others)
    up_parts = weight_parts(shared_up, up_others)
    normed_each, shared_d_act = carry(
        "rows",
        2,
        groups,
        gathers=[(groups, normed_two)],
        works=[down_back(upstream_each, shared_down)],
    )
    normed_blocks = normed_each.reshape(groups * experts, tokens, model)
    normed_each = normed_each.reshape(groups * length, model)

    logits = dot_nt(normed_two, w_router)
    router_probs = jax.nn.softmax(logits, axis=-1)
    chosen_probs = jnp.where(chosen, router_probs, 0.0)
    chosen_sum = jnp.sum(chosen_probs, axis=1, keepdims=True)
    gate_own = chosen_probs / chosen_sum

    def shares(own, others):
        parts = [own[0]] + [others[index] for index in range(groups - 1)]
        aligned = share % 128 == 0 and expert_down.shape[1] % 128 == 0
        return parts if aligned else [in_order(parts, 0)]

    member = (
        lax.dynamic_index_in_dim(chosen_all, place, 0, keepdims=False).reshape(experts, tokens)
        > 0.5
    )
    below = jnp.tril(jnp.ones((tokens, tokens), LOW), -1)
    rank = dot_nt(member.astype(LOW), below)
    slots = (
        member[:, None, :]
        & (rank.astype(jnp.int32)[:, None, :] == jnp.arange(capacity, dtype=jnp.int32)[None, :, None])
    )
    pick = slots.astype(LOW)

    rows_in, rows_up, d_pair, slot_weight = dispatch(
        here, normed_blocks, upstream_each, pick, chosen_all, w_router
    )
    here_side = side.reshape(1)
    expert_act, d_gate_pre, d_up_pre, d_gate_slots, out_terms, row_terms = run_expert(
        here_side,
        rows_in,
        rows_up,
        d_pair,
        slot_weight,
        pick,
        shares(expert_gate, eg_others),
        shares(expert_up, eu_others),
        shares(expert_down, ed_others),
    )
    d_gate_slots = d_gate_slots.reshape(experts, capacity, 1)
    d_gate_rows = jnp.sum(jnp.where(slots, d_gate_slots, 0.0), axis=1)
    d_gate_rows = jnp.broadcast_to(d_gate_rows[:, None, :], (experts, 8, tokens))
    half_model = model // 2
    (
        expert_back,
        out_left,
        d_gate_own,
        shared_act,
        shared_d_gate,
        shared_d_up,
        back_parts,
    ) = carry(
        "row_grads",
        3,
        1,
        scatters=[(row_terms, 0, model), (out_terms, 0, half_model)],
        directs=[d_gate_rows],
        works=[
            hidden_units(normed_each, shared_d_act, gate_parts, up_parts, tokens, groups)
        ],
    )
    d_gate_own = d_gate_own[:, 0, :].T
    def returned(terms):
        total = terms[0].astype(jnp.float32)
        for step in range(1, groups):
            back = lax.ppermute(
                terms[step], "fsdp", [(i, (i + step) % groups) for i in range(groups)]
            )
            total = total + back.astype(jnp.float32)
        return total

    shared_back = returned(back_parts.reshape(groups, tokens, model))

    d_chosen = jnp.where(
        chosen,
        (d_gate_own - jnp.sum(gate_own * d_gate_own, axis=1, keepdims=True)) / chosen_sum,
        0.0,
    )
    d_logits = router_probs * (
        d_chosen - jnp.sum(router_probs * d_chosen, axis=1, keepdims=True)
    )
    d_normed_two = (
        shared_back
        + expert_back
        + lax.dot_general(
            d_logits,
            w_router.astype(jnp.float32),
            (((1,), (0,)), ((), ())),
            precision=highest,
            preferred_element_type=jnp.float32,
        )
    )
    d_residual_norm, d_gain_two = rms_back(residual_one, gain_second, d_normed_two)
    d_residual = upstream + d_residual_norm
    d_attn_out = d_residual.astype(LOW)
    grad_router = lax.dot_general(
        d_logits,
        normed_two.astype(jnp.float32),
        (((0,), (0,)), ((), ())),
        precision=highest,
        preferred_element_type=jnp.float32,
    )

    def chip_term(left, right):
        return dot_tn(
            jnp.concatenate(scattered(left, 1), axis=0), jnp.concatenate(ring(right), axis=0)
        ).astype(LOW)

    def blocks(term):
        rows, width = term.shape
        rows = rows // experts
        term = term.reshape(experts, rows, width)
        return jnp.pad(term, ((0, 0), (0, -rows % 16), (0, 0)))

    term_o = chip_term(attended, d_attn_out)

    d_attended = in_order([dot_nt(d_attn_out, part) for part in w_out], 1).astype(LOW)
    d_query, term_pairs = attend_back(
        here, queries, every_pair, key_labels, query_labels, d_attended, log_total
    )
    d_pairs, out_right, mine_o, grad_sg, grad_su = carry(
        "pair_grads",
        4,
        1,
        scatters=[
            (term_pairs.reshape(experts, tokens, -1), 0, 2 * wide),
            (out_terms, half_model, half_model),
            (blocks(term_o), 0, model),
        ],
        works=[turned_products(normed_each, [shared_d_gate, shared_d_up], LOW, length)],
    )
    d_pairs = d_pairs.reshape(tokens, KEY_HEADS, 2, HEAD_DIM)
    d_query_low = rotate(
        d_query.reshape(tokens, QUERY_HEADS, HEAD_DIM), cosine, -sine
    ).reshape(tokens, -1).astype(LOW)
    d_key_low = rotate(d_pairs[:, :, 0], cosine, -sine).reshape(tokens, -1).astype(LOW)
    d_value_low = d_pairs[:, :, 1].reshape(tokens, -1).astype(LOW)
    d_normed_one = in_order(
        [
            dot_nt(d_query_low, w_query[step])
            + dot_nt(d_key_low, w_key[step])
            + dot_nt(d_value_low, w_value[step])
            for step in range(groups)
        ],
        1,
    )
    d_rows_norm, d_gain_one = rms_back(x_rows, gain_first, d_normed_one)
    grad_in = (d_residual + d_rows_norm).astype(LOW)
    small_grads = jnp.concatenate([d_gain_one[None], d_gain_two[None], grad_router], axis=0)
    small_grads = jnp.pad(small_grads, ((0, 256 - small_grads.shape[0]), (0, 0))).astype(LOW)
    small_parts = [part.astype(jnp.float32) for part in scattered(small_grads, 1)]
    small_term = sum(small_parts).astype(LOW).T
    term_pre = chip_term(
        normed_one, jnp.concatenate([d_query_low, d_key_low, d_value_low], axis=1)
    )
    all_o, mine_pre, mine_small, term_eg, term_eu, term_ed = carry(
        "sums",
        5,
        1,
        gathers=[(1, mine_o.astype(LOW))],
        scatters=[(blocks(term_pre), 0, term_pre.shape[1]), (blocks(small_term), 0, 256)],
        works=[
            turned_products(rows_in, [d_gate_pre, d_up_pre], LOW, rows_in.shape[0]),
            turned_products(expert_act, [d_pair], LOW, rows_in.shape[0]),
        ],
    )
    all_o = all_o.reshape(experts, -1, model)[:, : share // experts].reshape(share, model)
    mine_pre = jnp.concatenate([mine_pre, mine_small], axis=1)[: share // experts].astype(LOW)
    all_pre = lax.all_gather(mine_pre, "expert", axis=0, tiled=True)

    mine_pre, shared_act, term_eg, term_eu, term_ed, grad_sg, grad_su = lax.optimization_barrier(
        (mine_pre, shared_act, term_eg, term_eu, term_ed, grad_sg, grad_su)
    )

    own_act = lax.dynamic_slice_in_dim(
        shared_act.reshape(groups, length, -1), place * tokens, tokens, 1
    ).reshape(groups * tokens, -1)
    out_parts = dot_nn(own_act, shared_down).astype(LOW).reshape(groups, tokens, model)
    expert_sum = jnp.concatenate([out_left, out_right], axis=1)
    output = residual_one + returned(out_parts) + expert_sum

    def summed(term):
        parts = scattered(term, 0)
        size = term.shape[0] // groups
        total = lax.dynamic_slice_in_dim(term, side * size, size, 0).astype(jnp.float32)
        for part in parts[1:]:
            total = total + part.astype(jnp.float32)
        return total

    grad_eg, grad_eu, grad_ed = summed(term_eg), summed(term_eu), summed(term_ed)
    (grad_sd,) = alone(
        "down_grads", turned_products(shared_act, [upstream_each], jnp.float32, length)
    )
    grad_sg, grad_su = [
        join_columns(here_side, groups, term, scattered(term, 0)[1:])
        for term in (grad_sg, grad_su)
    ]
    grad_o, grad_q, grad_k, grad_v, small_grads = widen(
        [all_o, all_pre], [[], [model, model + wide, model + 2 * wide]]
    )
    small_grads = small_grads[:, : 2 + experts].T
    return (
        output.astype(LOW)[None],
        grad_in[None],
        small_grads[0],
        grad_q,
        grad_k,
        grad_v,
        grad_o,
        small_grads[1],
        small_grads[2:].T,
        grad_sg,
        grad_su,
        grad_sd,
        grad_eg[None],
        grad_eu[None],
        grad_ed[None],
    )


def solution(mesh):
    rows, split = P("fsdp", None), P("fsdp")
    tokens, expert = P("fsdp", "expert", None), P("expert", "fsdp", None)
    return jax.shard_map(
        local,
        mesh=mesh,
        in_specs=(
            (tokens, split, rows, rows, rows, rows, split)
            + (rows,) * 4
            + (expert,) * 3
            + (tokens, rows, P("fsdp", "expert"), tokens)
        ),
        out_specs=(
            (tokens, tokens, split)
            + (rows,) * 4
            + (split,)
            + (rows,) * 4
            + (expert,) * 3
        ),
        check_vma=False,
    )
```

```python
import jax
import jax.numpy as jnp
from jax import lax
from jax.experimental import pallas as pl
from jax.experimental.pallas import tpu as pltpu
from jax.sharding import PartitionSpec as P

QUERY_HEADS = 20
KEY_HEADS = 4
HEAD_DIM = 128

epsilon = 1e-05
rope_base = 500000.0
masked_score = -1e30
highest = lax.Precision.HIGHEST
LOW = jnp.bfloat16
MESH = pl.DeviceIdType.MESH


def dot_nn(left, right):
    return jnp.dot(left, right, preferred_element_type=jnp.float32)


def dot_nt(left, right):
    return lax.dot_general(
        left, right, (((1,), (1,)), ((), ())), preferred_element_type=jnp.float32
    )


def dot_tn(left, right):
    return lax.dot_general(
        left, right, (((0,), (0,)), ((), ())), preferred_element_type=jnp.float32
    )


def rms_scale(vector, gain):
    factor = lax.rsqrt(jnp.mean(vector * vector, axis=-1, keepdims=True) + epsilon)
    return vector * factor * gain


def rms_back(vector, gain, grad):
    factor = lax.rsqrt(jnp.mean(vector * vector, axis=-1, keepdims=True) + epsilon)
    scaled = grad * gain
    inner = jnp.mean(scaled * vector, axis=-1, keepdims=True)
    d_vector = factor * scaled - vector * (factor * factor * factor * inner)
    return d_vector, jnp.sum(grad * vector * factor, axis=0)


def rotate(heads, cosine, sine):
    half = heads.shape[-1] // 2
    front, back = heads[..., :half], heads[..., half:]
    return jnp.concatenate([front * cosine - back * sine, back * cosine + front * sine], axis=-1)


def rope_tables(positions):
    frequency = 1.0 / rope_base ** (jnp.arange(0, HEAD_DIM, 2, dtype=jnp.float32) / HEAD_DIM)
    turned = positions.astype(jnp.float32)[:, None] * frequency[None, :]
    return jnp.cos(turned)[:, None, :], jnp.sin(turned)[:, None, :]


def swiglu(gate, up):
    return gate * jax.nn.sigmoid(gate) * up


def swiglu_back(gate, up, grad):
    sigma = jax.nn.sigmoid(gate)
    return grad * up * (sigma * (1.0 + gate * (1.0 - sigma))), grad * gate * sigma


def coordinates():
    me = lax.axis_index("expert")
    quarter = lax.rem(me, 4)
    depth = me // 4
    across = quarter + 1 - 2 * lax.rem(quarter, 2)
    beside = quarter + 2 - 4 * (quarter // 2)
    return me, quarter, depth, across, beside


def when(condition):
    return pl.when(condition)


def send(source, target, send_sem, recv_sem, **device):
    return pltpu.make_async_remote_copy(
        src_ref=source,
        dst_ref=target,
        send_sem=send_sem,
        recv_sem=recv_sem,
        device_id=device,
        device_id_type=MESH,
    )


def enter(peers, everyone):
    me, quarter, depth, across, beside = coordinates()
    barrier = pltpu.get_barrier_semaphore()

    def greet(**device):
        pl.semaphore_signal(barrier, inc=1, device_id=device, device_id_type=MESH)

    if everyone:
        for step in range(1, 16):
            greet(expert=lax.rem(me + step, 16))
        near = 15
    else:
        greet(expert=depth * 4 + across)
        greet(expert=depth * 4 + beside)

        @when(depth < 3)
        def _():
            greet(expert=me + 4)

        @when(depth > 0)
        def _():
            greet(expert=me - 4)

        near = 2 + jnp.minimum(depth, 1) + jnp.minimum(3 - depth, 1)

    side = lax.axis_index("fsdp")
    for step in range(1, peers):
        greet(fsdp=lax.rem(side - step + peers, peers))
    pl.semaphore_wait(barrier, near + (peers - 1))


class Gather:
    def __init__(self, rows, width, peers):
        self.rows, self.width = rows, width
        self.peers = peers
        self.half = self.width // 2 // 128 * 128

    def scratch(self):
        shapes = [pltpu.SemaphoreType.DMA((11, 4)), pltpu.SemaphoreType.DMA((2,))]
        if self.peers > 1:
            shapes += [pltpu.SemaphoreType.DMA((2, self.peers - 1, 16))]
        return shapes

    def stages(self, source, out, sems, own_sem, mate_sems=None):
        rows, half = self.rows, self.half
        names = ("zr", "xr", "yr", "ar", "br", "us", "ds", "xs", "ys", "as", "bs")
        row_of = {name: index for index, name in enumerate(names)}
        spans = {"a": pl.ds(0, half), "b": pl.ds(half, self.width - half)}

        def sem(name, plane):
            return sems.at[row_of[name], plane]

        columns = pl.ds(0, self.width)

        def block(index):
            return out.at[0, index, :, columns]

        def part(index, name):
            return out.at[0, index, :, spans[name]]

        def hop(name, plane):
            me, quarter, depth, across, beside = coordinates()
            own = plane * 4 + quarter
            if name in ("u", "d"):
                shift = 4 if name == "u" else -4
                return send(
                    block(own), block(own), sem(name + "s", plane), sem("zr", plane),
                    expert=me + shift,
                )
            if name == "x":
                return send(
                    block(own), block(own), sem("xs", plane), sem("xr", plane),
                    expert=depth * 4 + across,
                )
            if name == "y":
                return send(
                    block(own), block(own), sem("ys", plane), sem("yr", plane),
                    expert=depth * 4 + beside,
                )
            if name == "a":
                index = plane * 4 + across
                return send(
                    part(index, "a"), part(index, "a"), sem("as", plane), sem("ar", plane),
                    expert=depth * 4 + beside,
                )
            index = plane * 4 + beside
            return send(
                part(index, "b"), part(index, "b"), sem("bs", plane), sem("br", plane),
                expert=depth * 4 + across,
            )

        def landed(name, plane):
            me, quarter, depth, across, beside = coordinates()
            index = {
                "z": plane * 4 + quarter,
                "x": plane * 4 + across,
                "y": plane * 4 + beside,
                "a": plane * 4 + (3 - quarter),
                "b": plane * 4 + (3 - quarter),
            }[name]
            ref = part(index, name) if name in ("a", "b") else block(index)
            return send(ref, ref, sem("us", plane), sem(name + "r", plane), expert=me)

        def mates(index, start):
            side = lax.axis_index("fsdp")
            for step in range(1, self.peers):
                copy = send(
                    out.at[0, index, :, columns],
                    out.at[step, index, :, columns],
                    mate_sems.at[0, step - 1, index],
                    mate_sems.at[1, step - 1, index],
                    fsdp=lax.rem(side - step + self.peers, self.peers),
                )
                if start:
                    copy.start()
                else:
                    copy.wait()

        def own_copy():
            me = lax.axis_index("expert")
            return pltpu.make_async_copy(source.at[:, columns], block(me), own_sem.at[0])

        def spread(plane):
            hop("x", plane).start()
            hop("y", plane).start()
            mates(plane * 4 + coordinates()[1], True)

        def first():
            depth = coordinates()[2]
            own_copy().start()
            own_copy().wait()

            @when(depth < 3)
            def _():
                hop("u", depth).start()

            @when(depth > 0)
            def _():
                hop("d", depth).start()

            spread(depth)

        def arrive(distance):
            depth = coordinates()[2]

            @when(depth >= distance)
            def _():
                plane = depth - distance
                landed("z", plane).wait_recv()

                @when(depth < 3)
                def _():
                    hop("u", plane).start()

                spread(plane)

            @when(depth + distance <= 3)
            def _():
                plane = depth + distance
                landed("z", plane).wait_recv()

                @when(depth > 0)
                def _():
                    hop("d", plane).start()

                spread(plane)

        def both(distance, action):
            depth = coordinates()[2]
            if distance == 0:
                action(depth)
                return

            @when(depth >= distance)
            def _():
                action(depth - distance)

            @when(depth + distance <= 3)
            def _():
                action(depth + distance)

        def cross(plane):
            me, quarter, depth, across, beside = coordinates()
            landed("x", plane).wait_recv()
            hop("a", plane).start()
            mates(plane * 4 + across, True)
            landed("y", plane).wait_recv()
            hop("b", plane).start()
            mates(plane * 4 + beside, True)

        def corner(plane):
            quarter = coordinates()[1]
            landed("a", plane).wait_recv()
            landed("b", plane).wait_recv()
            mates(plane * 4 + 3 - quarter, True)

        def finish():
            me, quarter, depth, across, beside = coordinates()
            for plane in range(4):
                for name in ("x", "y", "a", "b"):
                    hop(name, plane).wait_send()

                @when((plane <= depth) & (depth < 3))
                def _():
                    hop("u", plane).wait_send()

                @when((plane >= depth) & (depth > 0))
                def _():
                    hop("d", plane).wait_send()

            if self.peers > 1:
                def settle(index, carry):
                    mates(index, False)
                    return carry

                lax.fori_loop(0, 16, settle, 0)

        stages = [first]
        stages.append(lambda: arrive(1))
        stages.append(lambda: both(0, cross))
        stages.append(lambda: arrive(2))
        stages.append(lambda: both(1, cross))
        stages.append(lambda: (both(0, corner), arrive(3)))
        stages.append(lambda: both(2, cross))
        stages.append(lambda: both(1, corner))
        stages.append(lambda: both(3, cross))
        stages.append(lambda: both(2, corner))
        stages.append(lambda: (both(3, corner), finish()))
        return stages


class GatherLast:
    def __init__(self, rows, start, width, peers):
        self.rows, self.start, self.width, self.peers = rows, start, width, peers
        self.half = (rows // 2 + 15) // 16 * 16

    def scratch(self):
        shapes = [pltpu.SemaphoreType.DMA((8,)), pltpu.SemaphoreType.DMA((3, 16))]
        shapes += [pltpu.SemaphoreType.DMA((1,))]
        if self.peers > 1:
            shapes += [pltpu.SemaphoreType.DMA((2, self.peers - 1, 16))]
        return shapes

    def stages(self, source, out, sems, line_sems, own_sem, mate_sems=None):
        columns = pl.ds(self.start, self.width)
        spans = {"a": pl.ds(0, self.half), "b": pl.ds(self.half, self.rows - self.half)}

        def block(index, slot=0):
            return out.at[slot, index, :, columns]

        def part(index, name):
            return out.at[0, index, spans[name], columns]

        def hop(name):
            me, quarter, depth, across, beside = coordinates()
            at_x, at_y = depth * 4 + across, depth * 4 + beside
            if name == "x":
                return send(block(me), block(me), sems.at[0], sems.at[1], expert=at_x)
            if name == "y":
                return send(block(me), block(me), sems.at[2], sems.at[3], expert=at_y)
            if name == "a":
                ref = part(at_x, "a")
                return send(ref, ref, sems.at[4], sems.at[5], expert=at_y)
            ref = part(at_y, "b")
            return send(ref, ref, sems.at[6], sems.at[7], expert=at_x)

        def landed(name):
            me, quarter, depth, across, beside = coordinates()
            corner = depth * 4 + 3 - quarter
            ref = {
                "x": lambda: block(depth * 4 + across),
                "y": lambda: block(depth * 4 + beside),
                "a": lambda: part(corner, "a"),
                "b": lambda: part(corner, "b"),
            }[name]()
            number = {"x": 1, "y": 3, "a": 5, "b": 7}[name]
            return send(ref, ref, sems.at[number - 1], sems.at[number], expert=me)

        def along(index, up):
            me = lax.axis_index("expert")
            return send(
                block(index), block(index),
                line_sems.at[0 if up else 1, index], line_sems.at[2, index],
                expert=me + 4 if up else me - 4,
            )

        def mates(index, start):
            side = lax.axis_index("fsdp")
            for step in range(1, self.peers):
                copy = send(
                    block(index), block(index, step),
                    mate_sems.at[0, step - 1, index], mate_sems.at[1, step - 1, index],
                    fsdp=lax.rem(side - step + self.peers, self.peers),
                )
                if start:
                    copy.start()
                else:
                    copy.wait()

        def both_ways(index):
            depth = coordinates()[2]

            @when(depth < 3)
            def _():
                along(index, True).start()

            @when(depth > 0)
            def _():
                along(index, False).start()

            mates(index, True)

        def first():
            me = lax.axis_index("expert")
            own = pltpu.make_async_copy(source.at[:, columns], block(me), own_sem.at[0])
            own.start()
            own.wait()
            hop("x").start()
            hop("y").start()
            both_ways(me)

        def cross():
            me, quarter, depth, across, beside = coordinates()
            landed("x").wait_recv()
            hop("a").start()
            both_ways(depth * 4 + across)
            landed("y").wait_recv()
            hop("b").start()
            both_ways(depth * 4 + beside)

        def corner():
            me, quarter, depth, across, beside = coordinates()
            landed("a").wait_recv()
            landed("b").wait_recv()
            both_ways(depth * 4 + 3 - quarter)

        def arrive(distance, which):
            depth = coordinates()[2]

            @when(depth >= distance)
            def _():
                for quarter in which:
                    index = (depth - distance) * 4 + quarter
                    along(index, True).wait_recv()

                    @when(depth < 3)
                    def _(index=index):
                        along(index, True).start()

                    mates(index, True)

            @when(depth + distance <= 3)
            def _():
                for quarter in which:
                    index = (depth + distance) * 4 + quarter
                    along(index, False).wait_recv()

                    @when(depth > 0)
                    def _(index=index):
                        along(index, False).start()

                    mates(index, True)

        def finish():
            depth = coordinates()[2]
            for name in ("x", "y", "a", "b"):
                hop(name).wait_send()

            def settle(index, carry):
                plane = index // 4

                @when((plane <= depth) & (depth < 3))
                def _():
                    along(index, True).wait_send()

                @when((plane >= depth) & (depth > 0))
                def _():
                    along(index, False).wait_send()

                if self.peers > 1:
                    mates(index, False)
                return carry

            lax.fori_loop(0, 16, settle, 0)

        stages = [first, cross, corner]
        for distance in (1, 2, 3):
            for which in ((0, 1), (2, 3)):
                stages.append(lambda d=distance, w=which: arrive(d, w))
        return stages + [finish]


def plane_at(order):
    depth = coordinates()[2]
    inner = lax.rem(lax.rem(depth, 2) + depth // 2, 2)
    upper = depth // 2
    plane = (3 - order) + inner * (0, -2, 1, 1)[order]
    return plane + upper * (3 - 2 * plane)


def wide(value):
    return value.astype(jnp.float32)


def by_rows(start, rows, action):
    def step(index, carry):
        action(pl.ds(pl.multiple_of(start + index * 16, 16), 16))
        return carry

    lax.fori_loop(0, rows // 16, step, 0)


class Scatter:
    def __init__(self, rows, start, width):
        self.rows, self.start, self.width = rows, start, width
        self.half = self.width // 2 // 128 * 128

    def scratch(self):
        rows, half = self.rows, self.half
        rest = self.width - half
        return [
            pltpu.VMEM((2, 2, rows, half), LOW),
            pltpu.VMEM((2, 2, rows, rest), LOW),
            pltpu.VMEM((4, 2, rows, half), LOW),
            pltpu.VMEM((4, 2, rows, rest), LOW),
            pltpu.VMEM((4, rows, half), LOW),
            pltpu.VMEM((4, rows, rest), LOW),
            pltpu.VMEM((5, rows, self.width), LOW),
            pltpu.SemaphoreType.DMA((18, 4)),
        ]

    def stages(
        self, terms, out, own_a, own_b, got_a, got_b, more_a, more_b, line, sems
    ):
        rows, half, width = self.rows, self.half, self.width
        left, right = pl.ds(0, half), pl.ds(half, width - half)
        mine = pl.ds(0, width)
        mine_left, mine_right = pl.ds(0, half), pl.ds(half, width - half)
        from_left = pl.ds(self.start, half)
        from_right = pl.ds(self.start + half, width - half)

        def over_rows(action):
            by_rows(0, rows, action)

        def bits():
            quarter = coordinates()[1]
            return lax.rem(quarter, 2), quarter // 2

        def load(order):
            plane, slot = plane_at(order), order % 2
            x, y = bits()
            return (
                pltpu.make_async_copy(
                    terms.at[plane, y, :, :, from_left], own_a.at[slot], sems.at[0, plane]
                ),
                pltpu.make_async_copy(
                    terms.at[plane, :, x, :, from_right], own_b.at[slot], sems.at[1, plane]
                ),
            )

        def first_hop(plane):
            me, quarter, depth, across, beside = coordinates()
            x, y = bits()
            return (
                send(
                    terms.at[plane, 1 - y, :, :, from_left], got_a.at[plane],
                    sems.at[2, plane], sems.at[3, plane], expert=depth * 4 + beside,
                ),
                send(
                    terms.at[plane, :, 1 - x, :, from_right], got_b.at[plane],
                    sems.at[4, plane], sems.at[5, plane], expert=depth * 4 + across,
                ),
            )

        def second_hop(order):
            me, quarter, depth, across, beside = coordinates()
            plane, slot = plane_at(order), order % 2
            x, y = bits()
            return (
                send(
                    own_a.at[slot, 1 - x], more_a.at[plane],
                    sems.at[6, plane], sems.at[7, plane], expert=depth * 4 + across,
                ),
                send(
                    own_b.at[slot, 1 - y], more_b.at[plane],
                    sems.at[8, plane], sems.at[9, plane], expert=depth * 4 + beside,
                ),
            )

        def upward(plane):
            me = lax.axis_index("expert")
            return (
                send(
                    more_a.at[plane], line.at[plane, :, left],
                    sems.at[10, plane], sems.at[11, plane], expert=me + 4,
                ),
                send(
                    more_b.at[plane], line.at[plane, :, right],
                    sems.at[12, plane], sems.at[13, plane], expert=me + 4,
                ),
            )

        def downward(plane, receiver):
            me = lax.axis_index("expert")
            slot = plane + (4 - plane) * (1 - jnp.minimum(jnp.abs(plane - receiver), 1))
            return (
                send(
                    more_a.at[plane], line.at[slot, :, left],
                    sems.at[14, plane], sems.at[15, plane], expert=me - 4,
                ),
                send(
                    more_b.at[plane], line.at[slot, :, right],
                    sems.at[16, plane], sems.at[17, plane], expert=me - 4,
                ),
            )

        def arrived(copies):
            for copy in copies:
                copy.wait_recv()

        def begin(copies):
            for copy in copies:
                copy.start()

        def pair_sums(order):
            plane, slot = plane_at(order), order % 2
            for copy in load(order):
                copy.wait()
            for copy in first_hop(plane):
                copy.wait_recv()
            for mine, got in ((own_a, got_a), (own_b, got_b)):
                for index in range(2):
                    def add(span, mine=mine, got=got, index=index):
                        mine[slot, index, span, :] = (
                            wide(mine[slot, index, span, :]) + wide(got[plane, index, span, :])
                        ).astype(LOW)

                    over_rows(add)
            begin(second_hop(order))
            if order + 2 < 4:
                begin(first_hop(plane_at(order + 2)))

        def plane_sums(order):
            plane, slot = plane_at(order), order % 2
            x, y = bits()
            for copy in second_hop(order):
                copy.wait_recv()

            def add(span):
                more_a[plane, span, :] = (
                    wide(own_a[slot, x, span, :]) + wide(more_a[plane, span, :])
                ).astype(LOW)
                more_b[plane, span, :] = (
                    wide(own_b[slot, y, span, :]) + wide(more_b[plane, span, :])
                ).astype(LOW)

            over_rows(add)
            for copy in second_hop(order):
                copy.wait_send()
            if order + 2 < 4:
                begin(load(order + 2))

        def pass_on(order):
            plane = plane_at(order)
            depth = coordinates()[2]

            def join(slot):
                def add(span):
                    more_a[plane, span, :] = (
                        wide(more_a[plane, span, :]) + wide(line[slot, span, left])
                    ).astype(LOW)
                    more_b[plane, span, :] = (
                        wide(more_b[plane, span, :]) + wide(line[slot, span, right])
                    ).astype(LOW)

                over_rows(add)

            @when(plane > depth)
            def _():
                @when(depth > 0)
                def _():
                    arrived(upward(plane))
                    join(plane)

                begin(upward(plane))

            @when(plane < depth)
            def _():
                @when(depth < 3)
                def _():
                    arrived(downward(plane, depth))
                    join(plane)

                begin(downward(plane, depth - 1))

        def start():
            for order in range(2):
                begin(first_hop(plane_at(order)) + load(order))

        def finish():
            depth = coordinates()[2]

            def plain(span):
                out[span, mine_left] = wide(more_a[depth, span, :])
                out[span, mine_right] = wide(more_b[depth, span, :])

            over_rows(plain)

            @when(depth > 0)
            def _():
                arrived(upward(depth))

                def add(span):
                    out[span, mine] = out[span, mine] + wide(line[depth, span, :])

                over_rows(add)

            @when(depth < 3)
            def _():
                arrived(downward(depth, depth))

                def add(span):
                    out[span, mine] = out[span, mine] + wide(line[4, span, :])

                over_rows(add)

            for plane in range(4):
                for copy in first_hop(plane):
                    copy.wait_send()

                @when(plane > depth)
                def _(plane=plane):
                    for copy in upward(plane):
                        copy.wait_send()

                @when(plane < depth)
                def _(plane=plane):
                    for copy in downward(plane, depth - 1):
                        copy.wait_send()

        return [
            start,
            lambda: pair_sums(0),
            lambda: plane_sums(0),
            lambda: pair_sums(1),
            lambda: pass_on(0),
            lambda: plane_sums(1),
            lambda: pair_sums(2),
            lambda: pass_on(1),
            lambda: plane_sums(2),
            lambda: pair_sums(3),
            lambda: pass_on(2),
            lambda: plane_sums(3),
            finish,
        ]


class ScatterLast:
    def __init__(self, rows, start, width, place):
        self.rows, self.start, self.width, self.place = rows, start, width, place
        self.half = (rows // 2 + 15) // 16 * 16

    def scratch(self):
        rows, width, half = self.rows, self.width, self.half
        return [
            pltpu.VMEM((4, 2, 2, rows, width), LOW),
            pltpu.VMEM((5, 2, 2, rows, width), LOW),
            pltpu.VMEM((2, half, width), LOW),
            pltpu.VMEM((2, rows - half, width), LOW),
            pltpu.VMEM((half, width), LOW),
            pltpu.VMEM((rows - half, width), LOW),
            pltpu.SemaphoreType.DMA((5, 4)),
            pltpu.SemaphoreType.DMA((8,)),
        ]

    def stages(self, terms, out, own, line, got_a, got_b, more_a, more_b, sems, plane_sems):
        rows, half = self.rows, self.half
        columns = pl.ds(self.start, self.width)
        mine = pl.ds(self.place, self.width)
        upper, lower = pl.ds(0, half), pl.ds(half, rows - half)

        def bits():
            quarter = coordinates()[1]
            return lax.rem(quarter, 2), quarter // 2

        def load(plane):
            return pltpu.make_async_copy(
                terms.at[plane, :, :, :, columns], own.at[plane], sems.at[0, plane]
            )

        def upward(plane):
            me = lax.axis_index("expert")
            return send(
                own.at[plane], line.at[plane], sems.at[1, plane], sems.at[2, plane], expert=me + 4
            )

        def downward(plane, receiver):
            me = lax.axis_index("expert")
            slot = plane + (4 - plane) * (1 - jnp.minimum(jnp.abs(plane - receiver), 1))
            return send(
                own.at[plane], line.at[slot], sems.at[3, plane], sems.at[4, plane], expert=me - 4
            )

        def first_hop():
            me, quarter, depth, across, beside = coordinates()
            x, y = bits()
            return (
                send(
                    own.at[depth, 1 - y, :, upper], got_a, plane_sems.at[0], plane_sems.at[1],
                    expert=depth * 4 + beside,
                ),
                send(
                    own.at[depth, :, 1 - x, lower], got_b, plane_sems.at[2], plane_sems.at[3],
                    expert=depth * 4 + across,
                ),
            )

        def second_hop():
            me, quarter, depth, across, beside = coordinates()
            x, y = bits()
            return (
                send(
                    got_a.at[1 - x], more_a, plane_sems.at[4], plane_sems.at[5],
                    expert=depth * 4 + across,
                ),
                send(
                    got_b.at[1 - y], more_b, plane_sems.at[6], plane_sems.at[7],
                    expert=depth * 4 + beside,
                ),
            )

        def join(plane, slot):
            for index in range(4):
                y, x = index // 2, index % 2

                def add(span):
                    own[plane, y, x, span, :] = (
                        wide(own[plane, y, x, span, :]) + wide(line[slot, y, x, span, :])
                    ).astype(LOW)

                by_rows(0, rows, add)

        def start():
            for order in range(4):
                load(plane_at(order)).start()

        def pass_on(order):
            plane = plane_at(order)
            depth = coordinates()[2]
            load(plane).wait()

            @when(plane > depth)
            def _():
                @when(depth > 0)
                def _():
                    upward(plane).wait_recv()
                    join(plane, plane)

                upward(plane).start()

            @when(plane < depth)
            def _():
                @when(depth < 3)
                def _():
                    downward(plane, depth).wait_recv()
                    join(plane, plane)

                downward(plane, depth - 1).start()

        def gather_own():
            depth = coordinates()[2]
            load(depth).wait()

            @when(depth > 0)
            def _():
                upward(depth).wait_recv()
                join(depth, depth)

            @when(depth < 3)
            def _():
                downward(depth, depth).wait_recv()
                join(depth, 4)

            for copy in first_hop():
                copy.start()

        def pair():
            depth = coordinates()[2]
            x, y = bits()
            for copy in first_hop():
                copy.wait_recv()
            for index in range(2):

                def add_a(span):
                    got_a[index, span, :] = (
                        wide(got_a[index, span, :]) + wide(own[depth, y, index, span, :])
                    ).astype(LOW)

                by_rows(0, half, add_a)

                def add_b(span, index=index):
                    there = pl.ds(pl.multiple_of(span.start + half, 16), 16)
                    got_b[index, span, :] = (
                        wide(got_b[index, span, :]) + wide(own[depth, index, x, there, :])
                    ).astype(LOW)

                by_rows(0, rows - half, add_b)
            for copy in second_hop():
                copy.start()

        def finish():
            depth = coordinates()[2]
            x, y = bits()
            for copy in second_hop():
                copy.wait_recv()

            def total_a(span):
                out[span, mine] = wide(got_a[x, span, :]) + wide(more_a[span, :])

            by_rows(0, half, total_a)

            def total_b(span):
                there = pl.ds(pl.multiple_of(span.start + half, 16), 16)
                out[there, mine] = wide(got_b[y, span, :]) + wide(more_b[span, :])

            by_rows(0, rows - half, total_b)
            for copy in first_hop() + second_hop():
                copy.wait_send()
            for plane in range(4):

                @when(plane > depth)
                def _(plane=plane):
                    upward(plane).wait_send()

                @when(plane < depth)
                def _(plane=plane):
                    downward(plane, depth - 1).wait_send()

        return [start] + [lambda k=k: pass_on(k) for k in range(3)] + [gather_own, pair, finish]


class Direct:
    def scratch(self):
        return [pltpu.SemaphoreType.DMA((2, 16)), pltpu.SemaphoreType.DMA((1,))]

    def stages(self, source, out, sems, own_sem):
        def copy(step):
            me = lax.axis_index("expert")
            peer = lax.rem(me + step, 16)
            return send(source.at[peer], out.at[me], sems.at[0, peer], sems.at[1, me], expert=peer)

        def own():
            me = lax.axis_index("expert")
            return pltpu.make_async_copy(source.at[me], out.at[me], own_sem.at[0])

        def begin():
            own().start()
            for step in range(1, 16):
                copy(step).start()

        def finish():
            own().wait()
            me = lax.axis_index("expert")
            for step in range(1, 16):
                copy(step).wait_send()
                peer = lax.rem(me + step, 16)
                landed = send(
                    source.at[peer], out.at[peer], sems.at[0, peer], sems.at[1, peer], expert=peer
                )
                landed.wait_recv()

        return [begin, finish]


class Exchange:
    def __init__(self, peers, split):
        self.peers, self.split = peers, split

    def scratch(self):
        return [pltpu.SemaphoreType.DMA((2, self.peers - 1))]

    def stages(self, source, out, sems):
        def copies():
            side = lax.axis_index("fsdp")
            for step in range(1, self.peers):
                peer = lax.rem(side - step + self.peers, self.peers)
                part = source
                if self.split:
                    width = source.shape[1] // self.peers
                    part = source.at[:, pl.ds(pl.multiple_of(peer * width, 128), width)]
                yield send(
                    part, out.at[step - 1], sems.at[0, step - 1], sems.at[1, step - 1], fsdp=peer
                )

        def begin():
            for copy in copies():
                copy.start()

        def finish():
            for copy in copies():
                copy.wait()

        return [begin, finish]


class Work:
    def __init__(self, steps, inputs, outputs, body, scratch=(), held=()):
        self.steps, self.inputs, self.outputs, self.body = steps, inputs, outputs, body
        self.scratch, self.held = list(scratch), list(held)


def in_turn(lists):
    placed = []
    for number, one in enumerate(lists):
        for index, stage in enumerate(one[:-1]):
            placed.append((index / (len(one) - 1), number, index, stage))
    placed.sort(key=lambda item: item[:3])
    return [item[3] for item in placed] + [lambda: [one[-1]() for one in lists]]


def last_columns(width):
    return width // 4 // 128 * 128


def carry(
    name,
    collective_id,
    peers,
    gathers=(),
    scatters=(),
    directs=(),
    exchanges=(),
    works=(),
    lead=0,
    vmem=62,
):
    steps = max(1, sum(work.steps for work in works))
    any_spec = pl.BlockSpec(memory_space=pl.ANY)
    vmem_spec = pl.BlockSpec(memory_space=pltpu.VMEM)
    operands, in_specs, out_shapes, out_specs, scratch = [], [], [], [], []
    programs, places = [], []

    def add(array, out_shape, out_spec, *mine):
        for program in mine:
            programs.append(program)
            places.append((len(operands), len(out_shapes)))
        operands.append(array)
        in_specs.append(any_spec)
        out_shapes.append(out_shape)
        out_specs.append(out_spec)

    for block, own in gathers:
        rows, width = own.shape
        last = last_columns(width)
        mine = [Gather(rows, width - last, block)]
        if last:
            mine.append(GatherLast(rows, width - last, last, block))
        add(own, jax.ShapeDtypeStruct((block, 16, rows, width), own.dtype), any_spec, *mine)
    for terms, start, width in scatters:
        rows, columns = terms.shape[1:]
        last = last_columns(width)
        mine = [Scatter(rows, start, width - last)]
        if last:
            mine.append(ScatterLast(rows, start + width - last, last, width - last))
        add(
            terms.reshape(4, 2, 2, rows, columns),
            jax.ShapeDtypeStruct((rows, width), jnp.float32),
            vmem_spec,
            *mine,
        )
    for blocks in directs:
        add(blocks, jax.ShapeDtypeStruct(blocks.shape, blocks.dtype), any_spec, Direct())
    for array, split in exchanges:
        rows, width = array.shape
        width = width // peers if split else width
        shape = jax.ShapeDtypeStruct((peers - 1, rows, width), array.dtype)
        add(array, shape, any_spec, Exchange(peers, split))
    transfers = len(operands)
    scratch_counts = []
    for program in programs:
        shapes = program.scratch()
        scratch_counts.append(len(shapes))
        scratch += shapes
    begun = 0
    spans = []
    for work in works:
        def local(index, begun=begun, steps=work.steps):
            return jnp.clip(index - begun, 0, steps - 1)

        for array, shape, index_of in work.inputs:
            operands.append(array)
            in_specs.append(pl.BlockSpec(shape, lambda i, f=index_of, at=local: f(at(i))))
        for array, shape, _ in work.held:
            if isinstance(array, int):
                scratch.append(pltpu.VMEM(shape, out_shapes[array].dtype))
                continue
            operands.append(array)
            in_specs.append(any_spec)
            scratch.append(pltpu.VMEM(shape, array.dtype))
        if work.held:
            scratch.append(pltpu.SemaphoreType.DMA((len(work.held),)))
        for shape, dtype, block_shape, index_of in work.outputs:
            out_shapes.append(jax.ShapeDtypeStruct(shape, dtype))
            out_specs.append(pl.BlockSpec(block_shape, lambda i, f=index_of, at=local: f(at(i))))
        scratch += work.scratch
        spans.append((begun, begun + work.steps))
        begun += work.steps
    counts = (len(operands), len(out_shapes))

    def kernel(*refs):
        ins = refs[: counts[0]]
        outs = refs[counts[0] : counts[0] + counts[1]]
        rest = list(refs[counts[0] + counts[1] :])
        step = pl.program_id(0)
        lists = []
        for index, program in enumerate(programs):
            mine, rest = rest[: scratch_counts[index]], rest[scratch_counts[index] :]
            in_place, out_place = places[index]
            lists.append(program.stages(ins[in_place], outs[out_place], *mine))
        at = {0: [one[0] for one in lists[:lead]]}
        if lead:
            at[0] += [one[0] for one in lists[lead:]]
            at[0] += in_turn([one[1:] for one in lists[:lead]])
            lists = [one[1:] for one in lists[lead:]]
        stages = in_turn(lists)
        for index, stage in enumerate(stages):
            place = index * steps // len(stages) if index + 1 < len(stages) else steps - 1
            if lead:
                place = max(place, min(1, steps - 1))
            at.setdefault(place, []).append(stage)
        in_at, out_at = transfers, transfers
        holds, tasks = [], []
        for work, (low, high) in zip(works, spans):
            work_ins = list(ins[in_at : in_at + len(work.inputs)])
            in_at += len(work.inputs)
            sources = []
            for array, _, _ in work.held:
                sources.append(None if isinstance(array, int) else ins[in_at])
                in_at += not isinstance(array, int)
            work_outs = outs[out_at : out_at + len(work.outputs)]
            out_at += len(work.outputs)
            if work.held:
                held, sems, rest = rest[: len(sources)], rest[len(sources)], rest[len(sources) + 1 :]
                for index, (array, _, view) in enumerate(work.held):
                    source = outs[array] if isinstance(array, int) else sources[index]
                    holds.append((view(source), held[index], sems.at[index]))
                work_ins += held
            own, rest = rest[: len(work.scratch)], rest[len(work.scratch) :]
            tasks.append((work, low, high, work_ins, work_outs, own))
        for place in sorted(at):
            def act(place=place):
                if place == 0:
                    enter(peers, len(directs) > 0)
                for stage in at[place]:
                    stage()
                if place == 0:
                    for action in ("start", "wait"):
                        for hold in holds:
                            getattr(pltpu.make_async_copy(*hold), action)()

            if steps == 1:
                act()
            else:
                pl.when(step == place)(act)
        for work, low, high, work_ins, work_outs, own in tasks:
            def do(work=work, low=low, work_ins=work_ins, work_outs=work_outs, own=own):
                work.body(step - low, work_ins, work_outs, *own)

            if len(works) == 1:
                do()
            else:
                pl.when((step >= low) & (step < high))(do)

    return pl.pallas_call(
        kernel,
        name=name,
        grid=(steps,),
        out_shape=out_shapes,
        in_specs=in_specs,
        out_specs=out_specs,
        scratch_shapes=scratch,
        compiler_params=pltpu.CompilerParams(
            collective_id=collective_id,
            has_side_effects=True,
            vmem_limit_bytes=vmem * 1024 * 1024,
            dimension_semantics=("arbitrary",),
        ),
    )(*operands)


def tile_of(size):
    return 512 if size % 512 == 0 else size


def over_columns(width, action):
    size = 256 if width % 256 == 0 else 128

    def step(index, carry):
        action(pl.multiple_of(index * size, size), size)
        return carry

    lax.fori_loop(0, width // size, step, 0)


def weight_parts(own, others):
    count, share, hidden = others.shape
    if share % 128:
        side = lax.axis_index("fsdp")
        mine = lax.dynamic_slice_in_dim(own, side * hidden, hidden, 1)
        twice = jnp.concatenate([mine] + [others[i] for i in range(count)], axis=0)
        twice = jnp.concatenate([twice, twice], axis=0)
        start = lax.rem(count + 1 - side, count + 1) * share
        whole = lax.dynamic_slice_in_dim(twice, start, (count + 1) * share, 0)
        return [(whole, whole.shape, lambda ref: ref)]

    def own_view(ref):
        start = pl.multiple_of(lax.axis_index("fsdp") * hidden, 128)
        return ref.at[:, pl.ds(start, hidden)]

    return [(own, (share, hidden), own_view)] + [
        (others, (share, hidden), lambda ref, w=w: ref.at[w]) for w in range(count)
    ]


def down_back(upstream, down):
    total, model = upstream.shape
    hidden = down.shape[0]
    tile = tile_of(hidden)
    across = hidden // tile

    def body(step, ins, outs):
        base = lax.rem(step, across) * tile

        def columns(start, size):
            part = pl.ds(pl.multiple_of(base + start, size), size)
            outs[0][:, pl.ds(start, size)] = dot_nt(ins[0][...], ins[1][part, :]).astype(LOW)

        over_columns(tile, columns)

    return Work(
        total // 512 * across,
        [(upstream, (512, model), lambda s: (s // across, 0))],
        [((total, hidden), LOW, (512, tile), lambda s: (s // across, lax.rem(s, across)))],
        body,
        held=[(down, down.shape, lambda ref: ref)],
    )


def hidden_units(rows_all, d_act, gates, ups, tokens, groups):
    total, model = rows_all.shape
    count = len(gates)
    share, hidden = gates[0][1]
    tile = tile_of(hidden)
    across, height = hidden // tile, 512
    each, holds = total // groups // height, height // tokens

    def body(step, ins, outs, own_gate, own_up):
        base = pl.multiple_of(lax.rem(step, across) * tile, tile)
        part = pl.ds(base, tile)
        side = lax.axis_index("fsdp")
        me = lax.axis_index("expert")
        weights = ins[2:]

        def columns(start, size):
            there, here = pl.ds(pl.multiple_of(base + start, size), size), pl.ds(start, size)
            pre_gate = pre_up = None
            for which in range(count):
                first = 0
                if count > 1:
                    first = pl.multiple_of(lax.rem(side + which, count) * share, 128)
                rows = ins[0][:, pl.ds(first, share)]
                more_gate = dot_nn(rows, weights[which][:, there])
                more_up = dot_nn(rows, weights[count + which][:, there])
                pre_gate = more_gate if pre_gate is None else pre_gate + more_gate
                pre_up = more_up if pre_up is None else pre_up + more_up
            grad = ins[1][:, here].astype(jnp.float32)
            sigma = 0.5 + 0.5 * jnp.tanh(0.5 * pre_gate)
            silu = pre_gate * sigma
            outs[0][:, here] = (silu * pre_up).astype(LOW)
            outs[1][:, here] = (
                grad * pre_up * (sigma * (1.0 + pre_gate * (1.0 - sigma)))
            ).astype(LOW)
            outs[2][:, here] = (grad * silu).astype(LOW)

        over_columns(tile, columns)
        row_tile = step // across

        @pl.when(lax.rem(row_tile, each) == 0)
        def _():
            here = pl.ds(pl.multiple_of(lax.rem(me, holds) * tokens, tokens), tokens)
            there = pl.ds(pl.multiple_of(row_tile // each * tokens, tokens), tokens)
            own_gate[there, part] = outs[1][here, :]
            own_up[there, part] = outs[2][here, :]

        for which in range(count):

            @pl.when(step == (groups - 1) * each * across + across + which)
            def _(which=which):
                start = 0
                if count > 1:
                    start = pl.multiple_of(lax.rem(side + which, count) * share, 128)
                outs[3][:, pl.ds(start, share)] = (
                    dot_nt(own_gate[...], weights[which][...])
                    + dot_nt(own_up[...], weights[count + which][...])
                ).astype(LOW)

    def row_tile(s):
        number = s // across
        turned = lax.rem(lax.rem(number, each) + lax.axis_index("expert") // holds, each)
        return number // each * each + turned

    def spot(s):
        return row_tile(s), lax.rem(s, across)

    return Work(
        total // height * across,
        [(rows_all, (height, model), lambda s: (row_tile(s), 0)), (d_act, (height, tile), spot)],
        [((total, hidden), LOW, (height, tile), spot)] * 3
        + [((groups * tokens, model), LOW, (groups * tokens, model), lambda s: (0, 0))],
        body,
        [pltpu.VMEM((groups * tokens, hidden), LOW)] * 2,
        held=list(gates) + list(ups),
    )


def turned_products(left, rights, depth):
    total, height = left.shape
    width = rights[0].shape[1]
    tall, tile = tile_of(height), tile_of(width)
    across, deep = width // tile, total // depth
    chunk = 512 if depth % 512 == 0 else depth

    def body(step, ins, outs, turned, *sums):
        now = lax.rem(step, deep)

        @pl.when(lax.rem(step // deep, across) == 0)
        def _():
            def turn(index, carry):
                start = pl.multiple_of(index * chunk, chunk)
                there = pl.ds(pl.multiple_of(now * depth + start, chunk), chunk)
                turned[:, there] = ins[0][pl.ds(start, chunk), :].T
                return carry

            lax.fori_loop(0, depth // chunk, turn, 0)

        @pl.when(now == 0)
        def _():
            for ref in sums:
                ref[...] = jnp.zeros(ref.shape, jnp.float32)

        def add(index, carry):
            start = pl.multiple_of(index * chunk, chunk)
            there = pl.ds(pl.multiple_of(now * depth + start, chunk), chunk)
            for ref, right in zip(sums, ins[1:]):
                ref[...] += dot_nn(turned[:, there], right[pl.ds(start, chunk), :])
            return carry

        lax.fori_loop(0, depth // chunk, add, 0)

        @pl.when(now == deep - 1)
        def _():
            for ref, out in zip(sums, outs):
                out[...] = ref[...].astype(LOW)

    def left_spot(s):
        first = lax.rem(s // deep, across) == 0
        return jnp.where(first, lax.rem(s, deep), deep - 1), s // (deep * across)

    def right_spot(s):
        return lax.rem(s, deep), lax.rem(s // deep, across)

    return Work(
        height // tall * across * deep,
        [(left, (depth, tall), left_spot)]
        + [(right, (depth, tile), right_spot) for right in rights],
        [
            (
                (height, width),
                LOW,
                (tall, tile),
                lambda s: (s // (deep * across), lax.rem(s // deep, across)),
            )
        ]
        * len(rights),
        body,
        [pltpu.VMEM((tall, total), LOW)] + [pltpu.VMEM((tall, tile), jnp.float32)] * len(rights),
    )


CHUNK = 256


def tile_columns(value, count):
    return jnp.concatenate([value] * count, axis=1)


def stacked(ref, count):
    return jnp.concatenate(
        [ref[:, index * HEAD_DIM : (index + 1) * HEAD_DIM] for index in range(count)], axis=0
    )


def unstacked(turned, count, tokens):
    return jnp.concatenate(
        [turned[:, index * tokens : (index + 1) * tokens].T for index in range(count)], axis=1
    )


def chunks_of(ref, columns=None):
    def chunk(index):
        if columns is None:
            return ref[pl.ds(pl.multiple_of(index * CHUNK, CHUNK), CHUNK), :]
        blocks = CHUNK // ref.shape[1]
        return ref[pl.ds(index * blocks, blocks), :, columns].reshape(CHUNK, HEAD_DIM)

    return chunk


def chunk_scores(keys, queries, key_labels, query_labels, chunk, place, count):
    tokens = queries.shape[0] // count
    span = pl.ds(pl.multiple_of(chunk * CHUNK, CHUNK), CHUNK)
    raw = dot_nt(keys(chunk), queries) * HEAD_DIM ** (-0.5)
    row = chunk * CHUNK + lax.broadcasted_iota(jnp.int32, (CHUNK, tokens), 0)
    column = place * tokens + lax.broadcasted_iota(jnp.int32, (CHUNK, tokens), 1)
    allowed = (key_labels[span, :] == query_labels[...]) & (row <= column)
    bias = jnp.where(allowed, 0.0, masked_score)
    return span, raw + tile_columns(bias, count)


def attend_kernel(place, q_ref, keys, values, kl_ref, ql_ref, out_ref, log_ref, score_ref):
    tokens = q_ref.shape[0]
    count = q_ref.shape[1] // HEAD_DIM
    queries = stacked(q_ref, count)
    chunks = kl_ref.shape[0] // CHUNK

    def scores(chunk, top):
        span, value = chunk_scores(keys, queries, kl_ref, ql_ref, chunk, place[0], count)
        score_ref[span, :] = value
        return jnp.maximum(top, jnp.max(value, axis=0, keepdims=True))

    top = lax.fori_loop(
        0, chunks, scores, jnp.full((1, count * tokens), masked_score, jnp.float32)
    )

    def mix(chunk, carried):
        total, mixed = carried
        span = pl.ds(pl.multiple_of(chunk * CHUNK, CHUNK), CHUNK)
        prob = jnp.exp(score_ref[span, :] - top)
        return (
            total + jnp.sum(prob, axis=0, keepdims=True),
            mixed + dot_tn(values(chunk), prob.astype(LOW)),
        )

    total, mixed = lax.fori_loop(
        0,
        chunks,
        mix,
        (
            jnp.zeros((1, count * tokens), jnp.float32),
            jnp.zeros((HEAD_DIM, count * tokens), jnp.float32),
        ),
    )
    out_ref[...] = unstacked(mixed / total, count, tokens).astype(LOW)
    log_ref[0] = jnp.broadcast_to(top + jnp.log(total), log_ref.shape[1:])


def attend_back_kernel(
    place, q_ref, k_ref, v_ref, kl_ref, ql_ref, grad_ref, log_ref, dq_ref, pair_ref, p_ref, dp_ref
):
    tokens = q_ref.shape[0]
    count = q_ref.shape[1] // HEAD_DIM
    queries = stacked(q_ref, count)
    grads = stacked(grad_ref, count)
    chunks = k_ref.shape[0] // CHUNK
    keys, values = chunks_of(k_ref), chunks_of(v_ref)
    log_total = log_ref[0, 0:1, :]
    scale = HEAD_DIM ** (-0.5)

    def probs(chunk, row_dot):
        span, value = chunk_scores(keys, queries, kl_ref, ql_ref, chunk, place[0], count)
        prob = jnp.exp(value - log_total)
        d_prob = dot_nt(values(chunk), grads)
        p_ref[span, :] = prob
        dp_ref[span, :] = d_prob
        return row_dot + jnp.sum(prob * d_prob, axis=0, keepdims=True)

    row_dot = lax.fori_loop(
        0, chunks, probs, jnp.zeros((1, count * tokens), jnp.float32)
    )

    def back(chunk, d_query):
        span = pl.ds(pl.multiple_of(chunk * CHUNK, CHUNK), CHUNK)
        prob = p_ref[span, :]
        d_score = (prob * (dp_ref[span, :] - row_dot)).astype(LOW)
        pair_ref[span, :HEAD_DIM] = (dot_nn(d_score, queries) * scale).astype(LOW)
        pair_ref[span, HEAD_DIM:] = dot_nn(prob.astype(LOW), grads).astype(LOW)
        return d_query + dot_tn(keys(chunk), d_score)

    d_query = lax.fori_loop(
        0, chunks, back, jnp.zeros((HEAD_DIM, count * tokens), jnp.float32)
    )
    dq_ref[...] = unstacked(d_query * scale, count, tokens)


def attention_specs(tokens, length, group):
    return [
        pl.BlockSpec(memory_space=pltpu.SMEM),
        pl.BlockSpec((tokens, group), lambda g: (0, g)),
        pl.BlockSpec((length, HEAD_DIM), lambda g: (0, g)),
        pl.BlockSpec((length, HEAD_DIM), lambda g: (0, KEY_HEADS + g)),
        pl.BlockSpec((length, 1), lambda g: (0, 0)),
        pl.BlockSpec((1, tokens), lambda g: (0, 0)),
    ]


def attend_work(queries, pairs_at, key_labels, query_labels):
    tokens, width = queries.shape
    length, group = key_labels.shape[0], width // KEY_HEADS
    stack = group // HEAD_DIM * tokens
    pair_width = 2 * KEY_HEADS * HEAD_DIM

    def body(step, ins, outs, scores):
        q_ref, kl_ref, ql_ref, pairs = ins
        start = pl.multiple_of(step * HEAD_DIM, HEAD_DIM)
        keys = chunks_of(pairs, pl.ds(start, HEAD_DIM))
        values = chunks_of(pairs, pl.ds(KEY_HEADS * HEAD_DIM + start, HEAD_DIM))
        place = [lax.axis_index("expert")]
        attend_kernel(place, q_ref, keys, values, kl_ref, ql_ref, *outs, scores)

    return Work(
        KEY_HEADS,
        [
            (queries, (tokens, group), lambda s: (0, s)),
            (key_labels, (length, 1), lambda s: (0, 0)),
            (query_labels, (1, tokens), lambda s: (0, 0)),
        ],
        [
            ((tokens, width), LOW, (tokens, group), lambda s: (0, s)),
            ((KEY_HEADS, 8, stack), jnp.float32, (1, 8, stack), lambda s: (s, 0, 0)),
        ],
        body,
        [pltpu.VMEM((length, stack), jnp.float32)],
        held=[
            (
                pairs_at,
                (length // tokens, tokens, pair_width),
                lambda ref: ref.at[0, :, :, pl.ds(0, pair_width)],
            )
        ],
    )


def attend_back(place, queries, pairs, key_labels, query_labels, grads, log_total):
    tokens, width = queries.shape
    length, group = pairs.shape[0], width // KEY_HEADS
    stack = group // HEAD_DIM * tokens
    return pl.pallas_call(
        attend_back_kernel,
        name="attend_back",
        grid=(KEY_HEADS,),
        in_specs=attention_specs(tokens, length, group)
        + [
            pl.BlockSpec((tokens, group), lambda g: (0, g)),
            pl.BlockSpec((1, 8, stack), lambda g: (g, 0, 0)),
        ],
        out_specs=[
            pl.BlockSpec((tokens, group), lambda g: (0, g)),
            pl.BlockSpec((length, 2 * HEAD_DIM), lambda g: (0, g)),
        ],
        out_shape=[
            jax.ShapeDtypeStruct((tokens, width), jnp.float32),
            jax.ShapeDtypeStruct((length, 2 * KEY_HEADS * HEAD_DIM), LOW),
        ],
        scratch_shapes=[pltpu.VMEM((length, stack), jnp.float32)] * 2,
        compiler_params=pltpu.CompilerParams(vmem_limit_bytes=50 * 1024 * 1024),
    )(place, queries, pairs, pairs, key_labels, query_labels, grads, log_total)


def dispatch_kernel(
    place, n_ref, u_ref, p_ref, m_ref, w_ref, rows_ref, up_ref, pair_ref, g_ref, pick_ref
):
    blocks, tokens, model = n_ref.shape
    capacity = p_ref.shape[1]

    @pl.when(pl.program_id(0) == 0)
    def _():
        pick_ref[...] = jnp.zeros(pick_ref.shape, LOW)

    for block in range(blocks):
        pick_ref[
            block * capacity : (block + 1) * capacity, block * tokens : (block + 1) * tokens
        ] = p_ref[block]
    pick = pick_ref[...]
    logits = dot_nt(w_ref[...], n_ref[...].reshape(blocks * tokens, model))
    chosen = m_ref[...] > 0.5
    top = jnp.max(jnp.where(chosen, logits, masked_score), axis=0, keepdims=True)
    power = jnp.where(chosen, jnp.exp(jnp.where(chosen, logits - top, 0.0)), 0.0)
    mine = lax.broadcasted_iota(jnp.int32, logits.shape, 0) == place[0]
    gate = jnp.sum(jnp.where(mine, power, 0.0), axis=0, keepdims=True) / jnp.sum(
        power, axis=0, keepdims=True
    )
    slot_gate = jnp.sum(pick.astype(jnp.float32) * gate, axis=1, keepdims=True)
    g_ref[...] = slot_gate
    tile = tile_of(model)
    for index in range(model // tile):
        span = pl.ds(index * tile, tile)
        rows = n_ref[:, :, span].reshape(blocks * tokens, tile)
        rows_ref[:, span] = dot_nn(pick, rows).astype(LOW)
        ups = dot_nn(pick, u_ref[:, span])
        up_ref[:, span] = ups.astype(LOW)
        pair_ref[:, span] = (slot_gate * ups).astype(LOW)


def dispatch(place, normed, upstream, pick, chosen, w_router):
    blocks, capacity, tokens = pick.shape
    model = upstream.shape[1]
    experts = w_router.shape[0]
    group = 4
    wide_spec = pl.BlockSpec((group * capacity, model), lambda b: (b, 0))
    return pl.pallas_call(
        dispatch_kernel,
        name="dispatch",
        grid=(blocks // group,),
        in_specs=[
            pl.BlockSpec(memory_space=pltpu.SMEM),
            pl.BlockSpec((group, tokens, model), lambda b: (b, 0, 0)),
            pl.BlockSpec((group * tokens, model), lambda b: (b, 0)),
            pl.BlockSpec((group, capacity, tokens), lambda b: (b, 0, 0)),
            pl.BlockSpec((experts, group * tokens), lambda b: (0, b)),
            pl.BlockSpec((experts, model), lambda b: (0, 0)),
        ],
        out_specs=[wide_spec] * 3 + [pl.BlockSpec((group * capacity, 1), lambda b: (b, 0))],
        out_shape=[jax.ShapeDtypeStruct((blocks * capacity, model), LOW)] * 3
        + [jax.ShapeDtypeStruct((blocks * capacity, 1), jnp.float32)],
        scratch_shapes=[pltpu.VMEM((group * capacity, group * tokens), LOW)],
        compiler_params=pltpu.CompilerParams(vmem_limit_bytes=50 * 1024 * 1024),
    )(place, normed, upstream, pick, chosen, w_router)


def join_columns(side, groups, own, others):
    rows, columns = others[0].shape
    tile = rows // 10

    def kernel(side_ref, *refs):
        for step, ref in enumerate(refs[:-1]):
            start = lax.rem(side_ref[0] + step, groups) * columns
            refs[-1][:, pl.ds(pl.multiple_of(start, 128), columns)] = ref[...].astype(jnp.float32)

    return pl.pallas_call(
        kernel,
        name="join_columns",
        grid_spec=pltpu.PrefetchScalarGridSpec(
            num_scalar_prefetch=1,
            grid=(10,),
            in_specs=[pl.BlockSpec((tile, columns), lambda i, side: (side[0] * 10 + i, 0))]
            + [pl.BlockSpec((tile, columns), lambda i, side: (i, 0))] * len(others),
            out_specs=pl.BlockSpec((tile, groups * columns), lambda i, side: (i, 0)),
        ),
        out_shape=jax.ShapeDtypeStruct((rows, groups * columns), jnp.float32),
    )(side, own, *others)


def widen(arrays, cuts):
    rows = arrays[0].shape[0]
    steps = 10 if rows % 10 == 0 else 12
    tile = rows // steps
    widths = [
        [high - low for low, high in zip([0] + cut, cut + [array.shape[1]])]
        for array, cut in zip(arrays, cuts)
    ]

    def kernel(*refs):
        outs = iter(refs[len(arrays) :])
        for ref, parts in zip(refs, widths):
            start = 0
            for part in parts:
                next(outs)[...] = ref[:, start : start + part].astype(jnp.float32)
                start += part

    flat = [part for parts in widths for part in parts]
    return pl.pallas_call(
        kernel,
        name="widen",
        grid=(steps,),
        in_specs=[pl.BlockSpec((tile, array.shape[1]), lambda i: (i, 0)) for array in arrays],
        out_specs=[pl.BlockSpec((tile, part), lambda i: (i, 0)) for part in flat],
        out_shape=[jax.ShapeDtypeStruct((rows, part), jnp.float32) for part in flat],
    )(*arrays)


def expert_kernel(
    count, side, rows_ref, up_ref, pair_ref, gate_ref, back_ref, *refs
):
    w_gate, w_up, w_down = refs[:count], refs[count : 2 * count], refs[2 * count : 3 * count]
    act_ref, dg_ref, du_ref, d_gate_ref, out_ref, term_ref = refs[3 * count :]
    share = w_gate[0].shape[0]
    units = w_down[0].shape[0]
    model = rows_ref.shape[1]
    blocks, tokens, capacity = back_ref.shape

    def place(which, size):
        if count == 1:
            return pl.ds(0, size)
        return pl.ds(pl.multiple_of(lax.rem(side[0] + which, count) * size, 128), size)

    def offset(which, size, start):
        if count == 1:
            return start
        return pl.multiple_of(lax.rem(side[0] + which, count) * size + start, 128)

    for which in range(count):

        def hidden_columns(start, size, which=which):
            span = pl.ds(offset(which, units, start), size)
            pre_gate = pre_up = None
            for part in range(count):
                rows = rows_ref[:, place(part, share)]
                more_gate = dot_nn(rows, w_gate[part][:, span])
                more_up = dot_nn(rows, w_up[part][:, span])
                pre_gate = more_gate if pre_gate is None else pre_gate + more_gate
                pre_up = more_up if pre_up is None else pre_up + more_up
            d_act = dot_nt(pair_ref[...], w_down[which][pl.ds(start, size), :])
            sigma = 0.5 + 0.5 * jnp.tanh(0.5 * pre_gate)
            silu = pre_gate * sigma
            act_ref[:, span] = (silu * pre_up).astype(LOW)
            dg_ref[:, span] = (
                d_act * pre_up * (sigma * (1.0 + pre_gate * (1.0 - sigma)))
            ).astype(LOW)
            du_ref[:, span] = (d_act * silu).astype(LOW)

        over_columns(units, hidden_columns)

    def returned(target, values, span):
        for block in range(blocks):
            mine = values[block * capacity : (block + 1) * capacity]
            target[block, :, span] = dot_nn(back_ref[block], mine).astype(LOW)

    d_gate_ref[...] = jnp.zeros(d_gate_ref.shape, jnp.float32)

    def model_columns(start, size):
        span = pl.ds(start, size)
        produced = None
        for part in range(count):
            more = dot_nn(act_ref[:, place(part, units)], w_down[part][:, span])
            produced = more if produced is None else produced + more
        produced = produced.astype(LOW).astype(jnp.float32)
        d_gate_ref[...] += jnp.sum(
            produced * up_ref[:, span].astype(jnp.float32), axis=1, keepdims=True
        )
        returned(out_ref, (gate_ref[...] * produced).astype(LOW), span)

    over_columns(model, model_columns)
    for part in range(count):

        def row_columns(start, size, part=part):
            rows = pl.ds(start, size)
            d_rows = dot_nt(dg_ref[...], w_gate[part][rows, :]) + dot_nt(
                du_ref[...], w_up[part][rows, :]
            )
            returned(term_ref, d_rows.astype(LOW), pl.ds(offset(part, share, start), size))

        over_columns(share, row_columns)


def run_expert(side, rows_in, rows_up, d_pair, slot_gate, pick, gates, ups, downs):
    slots, model = rows_in.shape
    blocks, capacity, tokens = pick.shape
    hidden = gates[0].shape[1]
    count = len(gates)
    group = 4
    tile = group * capacity
    wide = pl.BlockSpec((tile, model), lambda i, side: (i, 0))
    narrow = pl.BlockSpec((tile, hidden), lambda i, side: (i, 0))
    single = pl.BlockSpec((tile, 1), lambda i, side: (i, 0))
    terms = pl.BlockSpec((group, tokens, model), lambda i, side: (i, 0, 0))
    weights = list(gates) + list(ups) + list(downs)

    def kernel(*refs):
        expert_kernel(count, *refs)

    return pl.pallas_call(
        kernel,
        name="expert",
        grid_spec=pltpu.PrefetchScalarGridSpec(
            num_scalar_prefetch=1,
            grid=(blocks // group,),
            in_specs=[
                wide,
                wide,
                wide,
                single,
                pl.BlockSpec((group, tokens, capacity), lambda i, side: (i, 0, 0)),
            ]
            + [
                pl.BlockSpec(w.shape, lambda i, side: (0, 0), pipeline_mode=pl.Buffered(1))
                for w in weights
            ],
            out_specs=[narrow, narrow, narrow, single, terms, terms],
        ),
        out_shape=[jax.ShapeDtypeStruct((slots, hidden), LOW)] * 3
        + [jax.ShapeDtypeStruct((slots, 1), jnp.float32)]
        + [jax.ShapeDtypeStruct((blocks, tokens, model), LOW)] * 2,
        compiler_params=pltpu.CompilerParams(vmem_limit_bytes=60 * 1024 * 1024),
    )(side, rows_in, rows_up, d_pair, slot_gate, pick.transpose(0, 2, 1), *weights)


def local(
    hidden_in,
    gain_attn,
    query_weight,
    key_matrix,
    value_matrix,
    out_weight,
    gain_ffn,
    router_weight,
    shared_gate,
    shared_up,
    shared_down,
    expert_gate,
    expert_up,
    expert_down,
    routes,
    segments,
    positions,
    grad_out,
):
    tokens = hidden_in.shape[1]
    model = hidden_in.shape[2]
    experts = lax.axis_size("expert")
    groups = lax.axis_size("fsdp")
    topk = routes.shape[2]
    capacity = min(tokens, 4 * tokens * topk // (3 * experts))
    length = tokens * experts
    group_width = QUERY_HEADS // KEY_HEADS
    score_scale = HEAD_DIM ** (-0.5)
    place = lax.axis_index("expert")
    side = lax.axis_index("fsdp")
    share = model // groups

    def peer(values, step):
        if step == 0:
            return values
        return lax.ppermute(
            values, "fsdp", [((i + step) % groups, i) for i in range(groups)]
        )

    def ring(values):
        return [peer(values, step) for step in range(groups)]

    def scattered(values, axis):
        size = values.shape[axis] // groups
        return [
            peer(
                lax.dynamic_slice_in_dim(
                    values, ((side - step + groups) % groups) * size, size, axis
                ),
                step,
            )
            for step in range(groups)
        ]

    def in_order(parts, axis):
        if groups == 2:
            first = side == 0
            return jnp.concatenate(
                [jnp.where(first, parts[0], parts[1]), jnp.where(first, parts[1], parts[0])], axis
            )
        size = parts[0].shape[axis]
        twice = jnp.concatenate(parts + parts, axis)
        start = ((groups - side) % groups) * size
        return lax.dynamic_slice_in_dim(twice, start, groups * size, axis)

    def own_columns(values, step):
        size = values.shape[-1] // groups
        return lax.dynamic_slice_in_dim(values, ((side + step) % groups) * size, size, 1)

    def rows_product(values, parts):
        if len(parts) == 1:
            return dot_nn(values, parts[0])
        total = dot_nn(own_columns(values, 0), parts[0])
        for step in range(1, groups):
            total = total + dot_nn(own_columns(values, step), parts[step])
        return total

    small = jnp.concatenate([gain_attn[None], gain_ffn[None], router_weight.T], axis=0)
    small_full = in_order(ring(small), 1)
    gain_first = small_full[0].astype(jnp.float32)
    gain_second = small_full[1].astype(jnp.float32)
    w_router = small_full[2:]
    w_query, w_key, w_value, w_out = (
        ring(query_weight),
        ring(key_matrix),
        ring(value_matrix),
        ring(out_weight),
    )
    expert_ids = jnp.arange(experts, dtype=jnp.int32)
    chosen = jnp.any(routes[0][:, :, None] == expert_ids[None, None, :], axis=1)
    upstream_low = grad_out[0]
    upstream = upstream_low.astype(jnp.float32)

    x_rows = hidden_in[0].astype(jnp.float32)
    labels = segments[0]
    cosine, sine = rope_tables(positions[0])
    normed_one = rms_scale(x_rows, gain_first).astype(LOW)
    key_rows = rotate(
        rows_product(normed_one, w_key).reshape(tokens, KEY_HEADS, HEAD_DIM), cosine, sine
    ).astype(LOW)
    value_rows = rows_product(normed_one, w_value).astype(LOW)
    wide = KEY_HEADS * HEAD_DIM
    pair_rows = jnp.concatenate(
        [
            key_rows.reshape(tokens, wide),
            value_rows,
            jnp.pad(chosen.astype(LOW), ((0, 0), (0, 128 - experts))),
        ],
        axis=1,
    )
    here = place.reshape(1)
    queries = (
        rotate(
            rows_product(normed_one, w_query).reshape(tokens, QUERY_HEADS, HEAD_DIM), cosine, sine
        )
        .astype(LOW)
        .reshape(tokens, QUERY_HEADS * HEAD_DIM)
    )
    key_labels = labels[:, None]
    query_labels = lax.dynamic_slice_in_dim(labels, place * tokens, tokens)[None]
    (
        every_pair,
        upstream_each,
        gate_others,
        up_others,
        eg_others,
        eu_others,
        ed_others,
        attended,
        log_total,
    ) = carry(
        "attend",
        7,
        groups,
        gathers=[(1, pair_rows), (groups, upstream_low)],
        exchanges=[
            (shared_gate, True),
            (shared_up, True),
            (expert_gate[0], False),
            (expert_up[0], False),
            (expert_down[0], False),
        ],
        works=[attend_work(queries, 0, key_labels, query_labels)],
        lead=2,
    )
    every_pair = every_pair.reshape(length, 2 * wide + 128)
    chosen_all = every_pair[:, 2 * wide : 2 * wide + experts].T.astype(jnp.float32)
    upstream_each = upstream_each.reshape(groups * length, model)
    residual_one = x_rows + rows_product(attended, w_out)
    normed_two = rms_scale(residual_one, gain_second).astype(LOW)

    gate_parts = weight_parts(shared_gate, gate_others)
    up_parts = weight_parts(shared_up, up_others)
    normed_each, shared_d_act = carry(
        "rows",
        2,
        groups,
        gathers=[(groups, normed_two)],
        works=[down_back(upstream_each, shared_down)],
    )
    normed_blocks = normed_each.reshape(groups * experts, tokens, model)
    normed_each = normed_each.reshape(groups * length, model)

    logits = dot_nt(normed_two, w_router)
    router_probs = jax.nn.softmax(logits, axis=-1)
    chosen_probs = jnp.where(chosen, router_probs, 0.0)
    chosen_sum = jnp.sum(chosen_probs, axis=1, keepdims=True)
    gate_own = chosen_probs / chosen_sum

    def shares(own, others):
        parts = [own[0]] + [others[index] for index in range(groups - 1)]
        aligned = share % 128 == 0 and expert_down.shape[1] % 128 == 0
        return parts if aligned else [in_order(parts, 0)]

    member = (
        lax.dynamic_index_in_dim(chosen_all, place, 0, keepdims=False).reshape(experts, tokens)
        > 0.5
    )
    below = jnp.tril(jnp.ones((tokens, tokens), LOW), -1)
    rank = dot_nt(member.astype(LOW), below)
    slots = (
        member[:, None, :]
        & (rank.astype(jnp.int32)[:, None, :] == jnp.arange(capacity, dtype=jnp.int32)[None, :, None])
    )
    pick = slots.astype(LOW)

    rows_in, rows_up, d_pair, slot_weight = dispatch(
        here, normed_blocks, upstream_each, pick, chosen_all, w_router
    )
    here_side = side.reshape(1)
    expert_act, d_gate_pre, d_up_pre, d_gate_slots, out_terms, row_terms = run_expert(
        here_side,
        rows_in,
        rows_up,
        d_pair,
        slot_weight,
        pick,
        shares(expert_gate, eg_others),
        shares(expert_up, eu_others),
        shares(expert_down, ed_others),
    )
    d_gate_slots = d_gate_slots.reshape(experts, capacity, 1)
    d_gate_rows = jnp.sum(jnp.where(slots, d_gate_slots, 0.0), axis=1)
    d_gate_rows = jnp.broadcast_to(d_gate_rows[:, None, :], (experts, 8, tokens))
    half_model = model // 2
    (
        expert_back,
        out_left,
        d_gate_own,
        shared_act,
        shared_d_gate,
        shared_d_up,
        back_parts,
    ) = carry(
        "row_grads",
        3,
        1,
        scatters=[(row_terms, 0, model), (out_terms, 0, half_model)],
        directs=[d_gate_rows],
        works=[
            hidden_units(normed_each, shared_d_act, gate_parts, up_parts, tokens, groups)
        ],
    )
    d_gate_own = d_gate_own[:, 0, :].T
    def returned(terms):
        total = terms[0].astype(jnp.float32)
        for step in range(1, groups):
            back = lax.ppermute(
                terms[step], "fsdp", [(i, (i + step) % groups) for i in range(groups)]
            )
            total = total + back.astype(jnp.float32)
        return total

    shared_back = returned(back_parts.reshape(groups, tokens, model))

    d_chosen = jnp.where(
        chosen,
        (d_gate_own - jnp.sum(gate_own * d_gate_own, axis=1, keepdims=True)) / chosen_sum,
        0.0,
    )
    d_logits = router_probs * (
        d_chosen - jnp.sum(router_probs * d_chosen, axis=1, keepdims=True)
    )
    d_normed_two = (
        shared_back
        + expert_back
        + lax.dot_general(
            d_logits,
            w_router.astype(jnp.float32),
            (((1,), (0,)), ((), ())),
            precision=highest,
            preferred_element_type=jnp.float32,
        )
    )
    d_residual_norm, d_gain_two = rms_back(residual_one, gain_second, d_normed_two)
    d_residual = upstream + d_residual_norm
    d_attn_out = d_residual.astype(LOW)
    grad_router = lax.dot_general(
        d_logits,
        normed_two.astype(jnp.float32),
        (((0,), (0,)), ((), ())),
        precision=highest,
        preferred_element_type=jnp.float32,
    )

    def chip_term(left, right):
        return dot_tn(
            jnp.concatenate(scattered(left, 1), axis=0), jnp.concatenate(ring(right), axis=0)
        ).astype(LOW)

    def blocks(term):
        rows, width = term.shape
        rows = rows // experts
        term = term.reshape(experts, rows, width)
        return jnp.pad(term, ((0, 0), (0, -rows % 16), (0, 0)))

    term_o = chip_term(attended, d_attn_out)

    d_attended = in_order([dot_nt(d_attn_out, part) for part in w_out], 1).astype(LOW)
    d_query, term_pairs = attend_back(
        here, queries, every_pair, key_labels, query_labels, d_attended, log_total
    )
    d_pairs, out_right, mine_o, grad_sg, grad_su = carry(
        "pair_grads",
        4,
        1,
        scatters=[
            (term_pairs.reshape(experts, tokens, -1), 0, 2 * wide),
            (out_terms, half_model, half_model),
            (blocks(term_o), 0, model),
        ],
        works=[
            turned_products(normed_each, [shared_d_gate, shared_d_up], length)
        ],
    )
    d_pairs = d_pairs.reshape(tokens, KEY_HEADS, 2, HEAD_DIM)
    d_query_low = rotate(
        d_query.reshape(tokens, QUERY_HEADS, HEAD_DIM), cosine, -sine
    ).reshape(tokens, -1).astype(LOW)
    d_key_low = rotate(d_pairs[:, :, 0], cosine, -sine).reshape(tokens, -1).astype(LOW)
    d_value_low = d_pairs[:, :, 1].reshape(tokens, -1).astype(LOW)
    d_normed_one = in_order(
        [
            dot_nt(d_query_low, w_query[step])
            + dot_nt(d_key_low, w_key[step])
            + dot_nt(d_value_low, w_value[step])
            for step in range(groups)
        ],
        1,
    )
    d_rows_norm, d_gain_one = rms_back(x_rows, gain_first, d_normed_one)
    grad_in = (d_residual + d_rows_norm).astype(LOW)
    small_grads = jnp.concatenate([d_gain_one[None], d_gain_two[None], grad_router], axis=0)
    small_grads = jnp.pad(small_grads, ((0, 256 - small_grads.shape[0]), (0, 0))).astype(LOW)
    small_parts = [part.astype(jnp.float32) for part in scattered(small_grads, 1)]
    small_term = sum(small_parts).astype(LOW).T
    term_pre = chip_term(
        normed_one, jnp.concatenate([d_query_low, d_key_low, d_value_low], axis=1)
    )
    all_o, mine_pre, mine_small, term_eg, term_eu, term_ed = carry(
        "sums",
        5,
        1,
        gathers=[(1, mine_o.astype(LOW))],
        scatters=[(blocks(term_pre), 0, term_pre.shape[1]), (blocks(small_term), 0, 256)],
        works=[
            turned_products(rows_in, [d_gate_pre, d_up_pre], rows_in.shape[0]),
            turned_products(expert_act, [d_pair], rows_in.shape[0]),
        ],
    )
    all_o = all_o.reshape(experts, -1, model)[:, : share // experts].reshape(share, model)
    mine_pre = jnp.concatenate([mine_pre, mine_small], axis=1)[: share // experts].astype(LOW)
    all_pre = lax.all_gather(mine_pre, "expert", axis=0, tiled=True)

    mine_pre, shared_act, term_eg, term_eu, term_ed, grad_sg, grad_su = lax.optimization_barrier(
        (mine_pre, shared_act, term_eg, term_eu, term_ed, grad_sg, grad_su)
    )
    own_act = lax.dynamic_slice_in_dim(
        shared_act.reshape(groups, length, -1), place * tokens, tokens, 1
    ).reshape(groups * tokens, -1)
    out_parts = dot_nn(own_act, shared_down).astype(LOW).reshape(groups, tokens, model)
    expert_sum = jnp.concatenate([out_left, out_right], axis=1)
    output = residual_one + returned(out_parts) + expert_sum

    def summed(term):
        parts = scattered(term, 0)
        size = term.shape[0] // groups
        total = lax.dynamic_slice_in_dim(term, side * size, size, 0).astype(jnp.float32)
        for part in parts[1:]:
            total = total + part.astype(jnp.float32)
        return total

    grad_eg, grad_eu, grad_ed = summed(term_eg), summed(term_eu), summed(term_ed)
    grad_sd = dot_tn(shared_act, upstream_each)
    grad_sg, grad_su = [
        join_columns(here_side, groups, term, scattered(term, 0)[1:])
        for term in (grad_sg, grad_su)
    ]
    grad_o, grad_q, grad_k, grad_v, small_grads = widen(
        [all_o, all_pre], [[], [model, model + wide, model + 2 * wide]]
    )
    small_grads = small_grads[:, : 2 + experts].T
    return (
        output.astype(LOW)[None],
        grad_in[None],
        small_grads[0],
        grad_q,
        grad_k,
        grad_v,
        grad_o,
        small_grads[1],
        small_grads[2:].T,
        grad_sg,
        grad_su,
        grad_sd,
        grad_eg[None],
        grad_eu[None],
        grad_ed[None],
    )


def solution(mesh):
    rows, split = P("fsdp", None), P("fsdp")
    tokens, expert = P("fsdp", "expert", None), P("expert", "fsdp", None)
    return jax.shard_map(
        local,
        mesh=mesh,
        in_specs=(
            (tokens, split, rows, rows, rows, rows, split)
            + (rows,) * 4
            + (expert,) * 3
            + (tokens, rows, P("fsdp", "expert"), tokens)
        ),
        out_specs=(
            (tokens, tokens, split)
            + (rows,) * 4
            + (split,)
            + (rows,) * 4
            + (expert,) * 3
        ),
        check_vma=False,
    )
```

```python
import jax
import jax.numpy as jnp
from jax import lax
from jax.experimental import pallas as pl
from jax.experimental.pallas import tpu as pltpu
from jax.sharding import PartitionSpec as P

QUERY_HEADS = 20
KEY_HEADS = 4
HEAD_DIM = 128

epsilon = 1e-05
rope_base = 500000.0
masked_score = -1e30
highest = lax.Precision.HIGHEST
LOW = jnp.bfloat16
MESH = pl.DeviceIdType.MESH


def dot_nn(left, right):
    return jnp.dot(left, right, preferred_element_type=jnp.float32)


def dot_nt(left, right):
    return lax.dot_general(
        left, right, (((1,), (1,)), ((), ())), preferred_element_type=jnp.float32
    )


def dot_tn(left, right):
    return lax.dot_general(
        left, right, (((0,), (0,)), ((), ())), preferred_element_type=jnp.float32
    )


def rms_scale(vector, gain):
    factor = lax.rsqrt(jnp.mean(vector * vector, axis=-1, keepdims=True) + epsilon)
    return vector * factor * gain


def rms_back(vector, gain, grad):
    factor = lax.rsqrt(jnp.mean(vector * vector, axis=-1, keepdims=True) + epsilon)
    scaled = grad * gain
    inner = jnp.mean(scaled * vector, axis=-1, keepdims=True)
    d_vector = factor * scaled - vector * (factor * factor * factor * inner)
    return d_vector, jnp.sum(grad * vector * factor, axis=0)


def rotate(heads, cosine, sine):
    half = heads.shape[-1] // 2
    front, back = heads[..., :half], heads[..., half:]
    return jnp.concatenate([front * cosine - back * sine, back * cosine + front * sine], axis=-1)


def rope_tables(positions):
    frequency = 1.0 / rope_base ** (jnp.arange(0, HEAD_DIM, 2, dtype=jnp.float32) / HEAD_DIM)
    turned = positions.astype(jnp.float32)[:, None] * frequency[None, :]
    return jnp.cos(turned)[:, None, :], jnp.sin(turned)[:, None, :]


def swiglu(gate, up):
    return gate * jax.nn.sigmoid(gate) * up


def swiglu_back(gate, up, grad):
    sigma = jax.nn.sigmoid(gate)
    return grad * up * (sigma * (1.0 + gate * (1.0 - sigma))), grad * gate * sigma


def coordinates():
    me = lax.axis_index("expert")
    quarter = lax.rem(me, 4)
    depth = me // 4
    across = quarter + 1 - 2 * lax.rem(quarter, 2)
    beside = quarter + 2 - 4 * (quarter // 2)
    return me, quarter, depth, across, beside


def when(condition):
    return pl.when(condition)


def send(source, target, send_sem, recv_sem, **device):
    return pltpu.make_async_remote_copy(
        src_ref=source,
        dst_ref=target,
        send_sem=send_sem,
        recv_sem=recv_sem,
        device_id=device,
        device_id_type=MESH,
    )


def enter(peers, everyone):
    me, quarter, depth, across, beside = coordinates()
    barrier = pltpu.get_barrier_semaphore()

    def greet(**device):
        pl.semaphore_signal(barrier, inc=1, device_id=device, device_id_type=MESH)

    if everyone:
        for step in range(1, 16):
            greet(expert=lax.rem(me + step, 16))
        near = 15
    else:
        greet(expert=depth * 4 + across)
        greet(expert=depth * 4 + beside)

        @when(depth < 3)
        def _():
            greet(expert=me + 4)

        @when(depth > 0)
        def _():
            greet(expert=me - 4)

        near = 2 + jnp.minimum(depth, 1) + jnp.minimum(3 - depth, 1)

    side = lax.axis_index("fsdp")
    for step in range(1, peers):
        greet(fsdp=lax.rem(side - step + peers, peers))
    pl.semaphore_wait(barrier, near + (peers - 1))


class Gather:
    def __init__(self, rows, width, peers):
        self.rows, self.width = rows, width
        self.peers = peers
        self.half = self.width // 2 // 128 * 128

    def scratch(self):
        shapes = [pltpu.SemaphoreType.DMA((11, 4)), pltpu.SemaphoreType.DMA((2,))]
        if self.peers > 1:
            shapes += [pltpu.SemaphoreType.DMA((2, self.peers - 1, 16))]
        return shapes

    def stages(self, source, out, sems, own_sem, mate_sems=None):
        rows, half = self.rows, self.half
        names = ("zr", "xr", "yr", "ar", "br", "us", "ds", "xs", "ys", "as", "bs")
        row_of = {name: index for index, name in enumerate(names)}
        spans = {"a": pl.ds(0, half), "b": pl.ds(half, self.width - half)}

        def sem(name, plane):
            return sems.at[row_of[name], plane]

        columns = pl.ds(0, self.width)

        def block(index):
            return out.at[0, index, :, columns]

        def part(index, name):
            return out.at[0, index, :, spans[name]]

        def hop(name, plane):
            me, quarter, depth, across, beside = coordinates()
            own = plane * 4 + quarter
            if name in ("u", "d"):
                shift = 4 if name == "u" else -4
                return send(
                    block(own), block(own), sem(name + "s", plane), sem("zr", plane),
                    expert=me + shift,
                )
            if name == "x":
                return send(
                    block(own), block(own), sem("xs", plane), sem("xr", plane),
                    expert=depth * 4 + across,
                )
            if name == "y":
                return send(
                    block(own), block(own), sem("ys", plane), sem("yr", plane),
                    expert=depth * 4 + beside,
                )
            if name == "a":
                index = plane * 4 + across
                return send(
                    part(index, "a"), part(index, "a"), sem("as", plane), sem("ar", plane),
                    expert=depth * 4 + beside,
                )
            index = plane * 4 + beside
            return send(
                part(index, "b"), part(index, "b"), sem("bs", plane), sem("br", plane),
                expert=depth * 4 + across,
            )

        def landed(name, plane):
            me, quarter, depth, across, beside = coordinates()
            index = {
                "z": plane * 4 + quarter,
                "x": plane * 4 + across,
                "y": plane * 4 + beside,
                "a": plane * 4 + (3 - quarter),
                "b": plane * 4 + (3 - quarter),
            }[name]
            ref = part(index, name) if name in ("a", "b") else block(index)
            return send(ref, ref, sem("us", plane), sem(name + "r", plane), expert=me)

        def mates(index, start):
            side = lax.axis_index("fsdp")
            for step in range(1, self.peers):
                copy = send(
                    out.at[0, index, :, columns],
                    out.at[step, index, :, columns],
                    mate_sems.at[0, step - 1, index],
                    mate_sems.at[1, step - 1, index],
                    fsdp=lax.rem(side - step + self.peers, self.peers),
                )
                if start:
                    copy.start()
                else:
                    copy.wait()

        def own_copy():
            me = lax.axis_index("expert")
            return pltpu.make_async_copy(source.at[:, columns], block(me), own_sem.at[0])

        def spread(plane):
            hop("x", plane).start()
            hop("y", plane).start()
            mates(plane * 4 + coordinates()[1], True)

        def first():
            depth = coordinates()[2]
            own_copy().start()
            own_copy().wait()

            @when(depth < 3)
            def _():
                hop("u", depth).start()

            @when(depth > 0)
            def _():
                hop("d", depth).start()

            spread(depth)

        def arrive(distance):
            depth = coordinates()[2]

            @when(depth >= distance)
            def _():
                plane = depth - distance
                landed("z", plane).wait_recv()

                @when(depth < 3)
                def _():
                    hop("u", plane).start()

                spread(plane)

            @when(depth + distance <= 3)
            def _():
                plane = depth + distance
                landed("z", plane).wait_recv()

                @when(depth > 0)
                def _():
                    hop("d", plane).start()

                spread(plane)

        def both(distance, action):
            depth = coordinates()[2]
            if distance == 0:
                action(depth)
                return

            @when(depth >= distance)
            def _():
                action(depth - distance)

            @when(depth + distance <= 3)
            def _():
                action(depth + distance)

        def cross(plane):
            me, quarter, depth, across, beside = coordinates()
            landed("x", plane).wait_recv()
            hop("a", plane).start()
            mates(plane * 4 + across, True)
            landed("y", plane).wait_recv()
            hop("b", plane).start()
            mates(plane * 4 + beside, True)

        def corner(plane):
            quarter = coordinates()[1]
            landed("a", plane).wait_recv()
            landed("b", plane).wait_recv()
            mates(plane * 4 + 3 - quarter, True)

        def finish():
            me, quarter, depth, across, beside = coordinates()
            for plane in range(4):
                for name in ("x", "y", "a", "b"):
                    hop(name, plane).wait_send()

                @when((plane <= depth) & (depth < 3))
                def _():
                    hop("u", plane).wait_send()

                @when((plane >= depth) & (depth > 0))
                def _():
                    hop("d", plane).wait_send()

            if self.peers > 1:
                def settle(index, carry):
                    mates(index, False)
                    return carry

                lax.fori_loop(0, 16, settle, 0)

        stages = [first]
        stages.append(lambda: arrive(1))
        stages.append(lambda: both(0, cross))
        stages.append(lambda: arrive(2))
        stages.append(lambda: both(1, cross))
        stages.append(lambda: (both(0, corner), arrive(3)))
        stages.append(lambda: both(2, cross))
        stages.append(lambda: both(1, corner))
        stages.append(lambda: both(3, cross))
        stages.append(lambda: both(2, corner))
        stages.append(lambda: (both(3, corner), finish()))
        return stages


class GatherLast:
    def __init__(self, rows, start, width, peers):
        self.rows, self.start, self.width, self.peers = rows, start, width, peers
        self.half = (rows // 2 + 15) // 16 * 16

    def scratch(self):
        shapes = [pltpu.SemaphoreType.DMA((8,)), pltpu.SemaphoreType.DMA((3, 16))]
        shapes += [pltpu.SemaphoreType.DMA((1,))]
        if self.peers > 1:
            shapes += [pltpu.SemaphoreType.DMA((2, self.peers - 1, 16))]
        return shapes

    def stages(self, source, out, sems, line_sems, own_sem, mate_sems=None):
        columns = pl.ds(self.start, self.width)
        spans = {"a": pl.ds(0, self.half), "b": pl.ds(self.half, self.rows - self.half)}

        def block(index, slot=0):
            return out.at[slot, index, :, columns]

        def part(index, name):
            return out.at[0, index, spans[name], columns]

        def hop(name):
            me, quarter, depth, across, beside = coordinates()
            at_x, at_y = depth * 4 + across, depth * 4 + beside
            if name == "x":
                return send(block(me), block(me), sems.at[0], sems.at[1], expert=at_x)
            if name == "y":
                return send(block(me), block(me), sems.at[2], sems.at[3], expert=at_y)
            if name == "a":
                ref = part(at_x, "a")
                return send(ref, ref, sems.at[4], sems.at[5], expert=at_y)
            ref = part(at_y, "b")
            return send(ref, ref, sems.at[6], sems.at[7], expert=at_x)

        def landed(name):
            me, quarter, depth, across, beside = coordinates()
            corner = depth * 4 + 3 - quarter
            ref = {
                "x": lambda: block(depth * 4 + across),
                "y": lambda: block(depth * 4 + beside),
                "a": lambda: part(corner, "a"),
                "b": lambda: part(corner, "b"),
            }[name]()
            number = {"x": 1, "y": 3, "a": 5, "b": 7}[name]
            return send(ref, ref, sems.at[number - 1], sems.at[number], expert=me)

        def along(index, up):
            me = lax.axis_index("expert")
            return send(
                block(index), block(index),
                line_sems.at[0 if up else 1, index], line_sems.at[2, index],
                expert=me + 4 if up else me - 4,
            )

        def mates(index, start):
            side = lax.axis_index("fsdp")
            for step in range(1, self.peers):
                copy = send(
                    block(index), block(index, step),
                    mate_sems.at[0, step - 1, index], mate_sems.at[1, step - 1, index],
                    fsdp=lax.rem(side - step + self.peers, self.peers),
                )
                if start:
                    copy.start()
                else:
                    copy.wait()

        def both_ways(index):
            depth = coordinates()[2]

            @when(depth < 3)
            def _():
                along(index, True).start()

            @when(depth > 0)
            def _():
                along(index, False).start()

            mates(index, True)

        def first():
            me = lax.axis_index("expert")
            own = pltpu.make_async_copy(source.at[:, columns], block(me), own_sem.at[0])
            own.start()
            own.wait()
            hop("x").start()
            hop("y").start()
            both_ways(me)

        def cross():
            me, quarter, depth, across, beside = coordinates()
            landed("x").wait_recv()
            hop("a").start()
            both_ways(depth * 4 + across)
            landed("y").wait_recv()
            hop("b").start()
            both_ways(depth * 4 + beside)

        def corner():
            me, quarter, depth, across, beside = coordinates()
            landed("a").wait_recv()
            landed("b").wait_recv()
            both_ways(depth * 4 + 3 - quarter)

        def arrive(distance, which):
            depth = coordinates()[2]

            @when(depth >= distance)
            def _():
                for quarter in which:
                    index = (depth - distance) * 4 + quarter
                    along(index, True).wait_recv()

                    @when(depth < 3)
                    def _(index=index):
                        along(index, True).start()

                    mates(index, True)

            @when(depth + distance <= 3)
            def _():
                for quarter in which:
                    index = (depth + distance) * 4 + quarter
                    along(index, False).wait_recv()

                    @when(depth > 0)
                    def _(index=index):
                        along(index, False).start()

                    mates(index, True)

        def finish():
            depth = coordinates()[2]
            for name in ("x", "y", "a", "b"):
                hop(name).wait_send()

            def settle(index, carry):
                plane = index // 4

                @when((plane <= depth) & (depth < 3))
                def _():
                    along(index, True).wait_send()

                @when((plane >= depth) & (depth > 0))
                def _():
                    along(index, False).wait_send()

                if self.peers > 1:
                    mates(index, False)
                return carry

            lax.fori_loop(0, 16, settle, 0)

        stages = [first, cross, corner]
        for distance in (1, 2, 3):
            for which in ((0, 1), (2, 3)):
                stages.append(lambda d=distance, w=which: arrive(d, w))
        return stages + [finish]


def plane_at(order):
    depth = coordinates()[2]
    inner = lax.rem(lax.rem(depth, 2) + depth // 2, 2)
    upper = depth // 2
    plane = (3 - order) + inner * (0, -2, 1, 1)[order]
    return plane + upper * (3 - 2 * plane)


def wide(value):
    return value.astype(jnp.float32)


def by_rows(start, rows, action):
    def step(index, carry):
        action(pl.ds(pl.multiple_of(start + index * 16, 16), 16))
        return carry

    lax.fori_loop(0, rows // 16, step, 0)


class Scatter:
    def __init__(self, rows, start, width):
        self.rows, self.start, self.width = rows, start, width
        self.half = self.width // 2 // 128 * 128

    def scratch(self):
        rows, half = self.rows, self.half
        rest = self.width - half
        return [
            pltpu.VMEM((2, 2, rows, half), LOW),
            pltpu.VMEM((2, 2, rows, rest), LOW),
            pltpu.VMEM((4, 2, rows, half), LOW),
            pltpu.VMEM((4, 2, rows, rest), LOW),
            pltpu.VMEM((4, rows, half), LOW),
            pltpu.VMEM((4, rows, rest), LOW),
            pltpu.VMEM((5, rows, self.width), LOW),
            pltpu.SemaphoreType.DMA((18, 4)),
        ]

    def stages(
        self, terms, out, own_a, own_b, got_a, got_b, more_a, more_b, line, sems
    ):
        rows, half, width = self.rows, self.half, self.width
        left, right = pl.ds(0, half), pl.ds(half, width - half)
        mine = pl.ds(0, width)
        mine_left, mine_right = pl.ds(0, half), pl.ds(half, width - half)
        from_left = pl.ds(self.start, half)
        from_right = pl.ds(self.start + half, width - half)

        def over_rows(action):
            by_rows(0, rows, action)

        def bits():
            quarter = coordinates()[1]
            return lax.rem(quarter, 2), quarter // 2

        def load(order):
            plane, slot = plane_at(order), order % 2
            x, y = bits()
            return (
                pltpu.make_async_copy(
                    terms.at[plane, y, :, :, from_left], own_a.at[slot], sems.at[0, plane]
                ),
                pltpu.make_async_copy(
                    terms.at[plane, :, x, :, from_right], own_b.at[slot], sems.at[1, plane]
                ),
            )

        def first_hop(plane):
            me, quarter, depth, across, beside = coordinates()
            x, y = bits()
            return (
                send(
                    terms.at[plane, 1 - y, :, :, from_left], got_a.at[plane],
                    sems.at[2, plane], sems.at[3, plane], expert=depth * 4 + beside,
                ),
                send(
                    terms.at[plane, :, 1 - x, :, from_right], got_b.at[plane],
                    sems.at[4, plane], sems.at[5, plane], expert=depth * 4 + across,
                ),
            )

        def second_hop(order):
            me, quarter, depth, across, beside = coordinates()
            plane, slot = plane_at(order), order % 2
            x, y = bits()
            return (
                send(
                    own_a.at[slot, 1 - x], more_a.at[plane],
                    sems.at[6, plane], sems.at[7, plane], expert=depth * 4 + across,
                ),
                send(
                    own_b.at[slot, 1 - y], more_b.at[plane],
                    sems.at[8, plane], sems.at[9, plane], expert=depth * 4 + beside,
                ),
            )

        def upward(plane):
            me = lax.axis_index("expert")
            return (
                send(
                    more_a.at[plane], line.at[plane, :, left],
                    sems.at[10, plane], sems.at[11, plane], expert=me + 4,
                ),
                send(
                    more_b.at[plane], line.at[plane, :, right],
                    sems.at[12, plane], sems.at[13, plane], expert=me + 4,
                ),
            )

        def downward(plane, receiver):
            me = lax.axis_index("expert")
            slot = plane + (4 - plane) * (1 - jnp.minimum(jnp.abs(plane - receiver), 1))
            return (
                send(
                    more_a.at[plane], line.at[slot, :, left],
                    sems.at[14, plane], sems.at[15, plane], expert=me - 4,
                ),
                send(
                    more_b.at[plane], line.at[slot, :, right],
                    sems.at[16, plane], sems.at[17, plane], expert=me - 4,
                ),
            )

        def arrived(copies):
            for copy in copies:
                copy.wait_recv()

        def begin(copies):
            for copy in copies:
                copy.start()

        def pair_sums(order):
            plane, slot = plane_at(order), order % 2
            for copy in load(order):
                copy.wait()
            for copy in first_hop(plane):
                copy.wait_recv()
            for mine, got in ((own_a, got_a), (own_b, got_b)):
                for index in range(2):
                    def add(span, mine=mine, got=got, index=index):
                        mine[slot, index, span, :] = (
                            wide(mine[slot, index, span, :]) + wide(got[plane, index, span, :])
                        ).astype(LOW)

                    over_rows(add)
            begin(second_hop(order))
            if order + 2 < 4:
                begin(first_hop(plane_at(order + 2)))

        def plane_sums(order):
            plane, slot = plane_at(order), order % 2
            x, y = bits()
            for copy in second_hop(order):
                copy.wait_recv()

            def add(span):
                more_a[plane, span, :] = (
                    wide(own_a[slot, x, span, :]) + wide(more_a[plane, span, :])
                ).astype(LOW)
                more_b[plane, span, :] = (
                    wide(own_b[slot, y, span, :]) + wide(more_b[plane, span, :])
                ).astype(LOW)

            over_rows(add)
            for copy in second_hop(order):
                copy.wait_send()
            if order + 2 < 4:
                begin(load(order + 2))

        def pass_on(order):
            plane = plane_at(order)
            depth = coordinates()[2]

            def join(slot):
                def add(span):
                    more_a[plane, span, :] = (
                        wide(more_a[plane, span, :]) + wide(line[slot, span, left])
                    ).astype(LOW)
                    more_b[plane, span, :] = (
                        wide(more_b[plane, span, :]) + wide(line[slot, span, right])
                    ).astype(LOW)

                over_rows(add)

            @when(plane > depth)
            def _():
                @when(depth > 0)
                def _():
                    arrived(upward(plane))
                    join(plane)

                begin(upward(plane))

            @when(plane < depth)
            def _():
                @when(depth < 3)
                def _():
                    arrived(downward(plane, depth))
                    join(plane)

                begin(downward(plane, depth - 1))

        def start():
            for order in range(2):
                begin(first_hop(plane_at(order)) + load(order))

        def finish():
            depth = coordinates()[2]

            def plain(span):
                out[span, mine_left] = wide(more_a[depth, span, :])
                out[span, mine_right] = wide(more_b[depth, span, :])

            over_rows(plain)

            @when(depth > 0)
            def _():
                arrived(upward(depth))

                def add(span):
                    out[span, mine] = out[span, mine] + wide(line[depth, span, :])

                over_rows(add)

            @when(depth < 3)
            def _():
                arrived(downward(depth, depth))

                def add(span):
                    out[span, mine] = out[span, mine] + wide(line[4, span, :])

                over_rows(add)

            for plane in range(4):
                for copy in first_hop(plane):
                    copy.wait_send()

                @when(plane > depth)
                def _(plane=plane):
                    for copy in upward(plane):
                        copy.wait_send()

                @when(plane < depth)
                def _(plane=plane):
                    for copy in downward(plane, depth - 1):
                        copy.wait_send()

        return [
            start,
            lambda: pair_sums(0),
            lambda: plane_sums(0),
            lambda: pair_sums(1),
            lambda: pass_on(0),
            lambda: plane_sums(1),
            lambda: pair_sums(2),
            lambda: pass_on(1),
            lambda: plane_sums(2),
            lambda: pair_sums(3),
            lambda: pass_on(2),
            lambda: plane_sums(3),
            finish,
        ]


class ScatterLast:
    def __init__(self, rows, start, width, place):
        self.rows, self.start, self.width, self.place = rows, start, width, place
        self.half = (rows // 2 + 15) // 16 * 16

    def scratch(self):
        rows, width, half = self.rows, self.width, self.half
        return [
            pltpu.VMEM((4, 2, 2, rows, width), LOW),
            pltpu.VMEM((5, 2, 2, rows, width), LOW),
            pltpu.VMEM((2, half, width), LOW),
            pltpu.VMEM((2, rows - half, width), LOW),
            pltpu.VMEM((half, width), LOW),
            pltpu.VMEM((rows - half, width), LOW),
            pltpu.SemaphoreType.DMA((5, 4)),
            pltpu.SemaphoreType.DMA((8,)),
        ]

    def stages(self, terms, out, own, line, got_a, got_b, more_a, more_b, sems, plane_sems):
        rows, half = self.rows, self.half
        columns = pl.ds(self.start, self.width)
        mine = pl.ds(self.place, self.width)
        upper, lower = pl.ds(0, half), pl.ds(half, rows - half)

        def bits():
            quarter = coordinates()[1]
            return lax.rem(quarter, 2), quarter // 2

        def load(plane):
            return pltpu.make_async_copy(
                terms.at[plane, :, :, :, columns], own.at[plane], sems.at[0, plane]
            )

        def upward(plane):
            me = lax.axis_index("expert")
            return send(
                own.at[plane], line.at[plane], sems.at[1, plane], sems.at[2, plane], expert=me + 4
            )

        def downward(plane, receiver):
            me = lax.axis_index("expert")
            slot = plane + (4 - plane) * (1 - jnp.minimum(jnp.abs(plane - receiver), 1))
            return send(
                own.at[plane], line.at[slot], sems.at[3, plane], sems.at[4, plane], expert=me - 4
            )

        def first_hop():
            me, quarter, depth, across, beside = coordinates()
            x, y = bits()
            return (
                send(
                    own.at[depth, 1 - y, :, upper], got_a, plane_sems.at[0], plane_sems.at[1],
                    expert=depth * 4 + beside,
                ),
                send(
                    own.at[depth, :, 1 - x, lower], got_b, plane_sems.at[2], plane_sems.at[3],
                    expert=depth * 4 + across,
                ),
            )

        def second_hop():
            me, quarter, depth, across, beside = coordinates()
            x, y = bits()
            return (
                send(
                    got_a.at[1 - x], more_a, plane_sems.at[4], plane_sems.at[5],
                    expert=depth * 4 + across,
                ),
                send(
                    got_b.at[1 - y], more_b, plane_sems.at[6], plane_sems.at[7],
                    expert=depth * 4 + beside,
                ),
            )

        def join(plane, slot):
            for index in range(4):
                y, x = index // 2, index % 2

                def add(span):
                    own[plane, y, x, span, :] = (
                        wide(own[plane, y, x, span, :]) + wide(line[slot, y, x, span, :])
                    ).astype(LOW)

                by_rows(0, rows, add)

        def start():
            for order in range(4):
                load(plane_at(order)).start()

        def pass_on(order):
            plane = plane_at(order)
            depth = coordinates()[2]
            load(plane).wait()

            @when(plane > depth)
            def _():
                @when(depth > 0)
                def _():
                    upward(plane).wait_recv()
                    join(plane, plane)

                upward(plane).start()

            @when(plane < depth)
            def _():
                @when(depth < 3)
                def _():
                    downward(plane, depth).wait_recv()
                    join(plane, plane)

                downward(plane, depth - 1).start()

        def gather_own():
            depth = coordinates()[2]
            load(depth).wait()

            @when(depth > 0)
            def _():
                upward(depth).wait_recv()
                join(depth, depth)

            @when(depth < 3)
            def _():
                downward(depth, depth).wait_recv()
                join(depth, 4)

            for copy in first_hop():
                copy.start()

        def pair():
            depth = coordinates()[2]
            x, y = bits()
            for copy in first_hop():
                copy.wait_recv()
            for index in range(2):

                def add_a(span):
                    got_a[index, span, :] = (
                        wide(got_a[index, span, :]) + wide(own[depth, y, index, span, :])
                    ).astype(LOW)

                by_rows(0, half, add_a)

                def add_b(span, index=index):
                    there = pl.ds(pl.multiple_of(span.start + half, 16), 16)
                    got_b[index, span, :] = (
                        wide(got_b[index, span, :]) + wide(own[depth, index, x, there, :])
                    ).astype(LOW)

                by_rows(0, rows - half, add_b)
            for copy in second_hop():
                copy.start()

        def finish():
            depth = coordinates()[2]
            x, y = bits()
            for copy in second_hop():
                copy.wait_recv()

            def total_a(span):
                out[span, mine] = wide(got_a[x, span, :]) + wide(more_a[span, :])

            by_rows(0, half, total_a)

            def total_b(span):
                there = pl.ds(pl.multiple_of(span.start + half, 16), 16)
                out[there, mine] = wide(got_b[y, span, :]) + wide(more_b[span, :])

            by_rows(0, rows - half, total_b)
            for copy in first_hop() + second_hop():
                copy.wait_send()
            for plane in range(4):

                @when(plane > depth)
                def _(plane=plane):
                    upward(plane).wait_send()

                @when(plane < depth)
                def _(plane=plane):
                    downward(plane, depth - 1).wait_send()

        return [start] + [lambda k=k: pass_on(k) for k in range(3)] + [gather_own, pair, finish]


class Direct:
    def scratch(self):
        return [pltpu.SemaphoreType.DMA((2, 16)), pltpu.SemaphoreType.DMA((1,))]

    def stages(self, source, out, sems, own_sem):
        def copy(step):
            me = lax.axis_index("expert")
            peer = lax.rem(me + step, 16)
            return send(source.at[peer], out.at[me], sems.at[0, peer], sems.at[1, me], expert=peer)

        def own():
            me = lax.axis_index("expert")
            return pltpu.make_async_copy(source.at[me], out.at[me], own_sem.at[0])

        def begin():
            own().start()
            for step in range(1, 16):
                copy(step).start()

        def finish():
            own().wait()
            me = lax.axis_index("expert")
            for step in range(1, 16):
                copy(step).wait_send()
                peer = lax.rem(me + step, 16)
                landed = send(
                    source.at[peer], out.at[peer], sems.at[0, peer], sems.at[1, peer], expert=peer
                )
                landed.wait_recv()

        return [begin, finish]


class Exchange:
    def __init__(self, peers, split):
        self.peers, self.split = peers, split

    def scratch(self):
        return [pltpu.SemaphoreType.DMA((2, self.peers - 1))]

    def stages(self, source, out, sems):
        def copies():
            side = lax.axis_index("fsdp")
            for step in range(1, self.peers):
                peer = lax.rem(side - step + self.peers, self.peers)
                part = source
                if self.split:
                    width = source.shape[1] // self.peers
                    part = source.at[:, pl.ds(pl.multiple_of(peer * width, 128), width)]
                yield send(
                    part, out.at[step - 1], sems.at[0, step - 1], sems.at[1, step - 1], fsdp=peer
                )

        def begin():
            for copy in copies():
                copy.start()

        def finish():
            for copy in copies():
                copy.wait()

        return [begin, finish]


class Work:
    def __init__(self, steps, inputs, outputs, body, scratch=(), held=()):
        self.steps, self.inputs, self.outputs, self.body = steps, inputs, outputs, body
        self.scratch, self.held = list(scratch), list(held)


def in_turn(lists):
    placed = []
    for number, one in enumerate(lists):
        for index, stage in enumerate(one[:-1]):
            placed.append((index / (len(one) - 1), number, index, stage))
    placed.sort(key=lambda item: item[:3])
    return [item[3] for item in placed] + [lambda: [one[-1]() for one in lists]]


def last_columns(width):
    return width // 4 // 128 * 128


def carry(
    name,
    collective_id,
    peers,
    gathers=(),
    scatters=(),
    directs=(),
    exchanges=(),
    works=(),
    lead=0,
    vmem=62,
):
    steps = max(1, sum(work.steps for work in works))
    any_spec = pl.BlockSpec(memory_space=pl.ANY)
    vmem_spec = pl.BlockSpec(memory_space=pltpu.VMEM)
    operands, in_specs, out_shapes, out_specs, scratch = [], [], [], [], []
    programs, places = [], []

    def add(array, out_shape, out_spec, *mine):
        for program in mine:
            programs.append(program)
            places.append((len(operands), len(out_shapes)))
        operands.append(array)
        in_specs.append(any_spec)
        out_shapes.append(out_shape)
        out_specs.append(out_spec)

    for block, own in gathers:
        rows, width = own.shape
        last = last_columns(width)
        mine = [Gather(rows, width - last, block)]
        if last:
            mine.append(GatherLast(rows, width - last, last, block))
        add(own, jax.ShapeDtypeStruct((block, 16, rows, width), own.dtype), any_spec, *mine)
    for terms, start, width in scatters:
        rows, columns = terms.shape[1:]
        last = last_columns(width)
        mine = [Scatter(rows, start, width - last)]
        if last:
            mine.append(ScatterLast(rows, start + width - last, last, width - last))
        add(
            terms.reshape(4, 2, 2, rows, columns),
            jax.ShapeDtypeStruct((rows, width), jnp.float32),
            vmem_spec,
            *mine,
        )
    for blocks in directs:
        add(blocks, jax.ShapeDtypeStruct(blocks.shape, blocks.dtype), any_spec, Direct())
    for array, split in exchanges:
        rows, width = array.shape
        width = width // peers if split else width
        shape = jax.ShapeDtypeStruct((peers - 1, rows, width), array.dtype)
        add(array, shape, any_spec, Exchange(peers, split))
    transfers = len(operands)
    scratch_counts = []
    for program in programs:
        shapes = program.scratch()
        scratch_counts.append(len(shapes))
        scratch += shapes
    begun = 0
    spans = []
    for work in works:
        def local(index, begun=begun, steps=work.steps):
            return jnp.clip(index - begun, 0, steps - 1)

        for array, shape, index_of in work.inputs:
            operands.append(array)
            in_specs.append(pl.BlockSpec(shape, lambda i, f=index_of, at=local: f(at(i))))
        for array, shape, _ in work.held:
            if isinstance(array, int):
                scratch.append(pltpu.VMEM(shape, out_shapes[array].dtype))
                continue
            operands.append(array)
            in_specs.append(any_spec)
            scratch.append(pltpu.VMEM(shape, array.dtype))
        if work.held:
            scratch.append(pltpu.SemaphoreType.DMA((len(work.held),)))
        for shape, dtype, block_shape, index_of in work.outputs:
            out_shapes.append(jax.ShapeDtypeStruct(shape, dtype))
            out_specs.append(pl.BlockSpec(block_shape, lambda i, f=index_of, at=local: f(at(i))))
        scratch += work.scratch
        spans.append((begun, begun + work.steps))
        begun += work.steps
    counts = (len(operands), len(out_shapes))

    def kernel(*refs):
        ins = refs[: counts[0]]
        outs = refs[counts[0] : counts[0] + counts[1]]
        rest = list(refs[counts[0] + counts[1] :])
        step = pl.program_id(0)
        lists = []
        for index, program in enumerate(programs):
            mine, rest = rest[: scratch_counts[index]], rest[scratch_counts[index] :]
            in_place, out_place = places[index]
            lists.append(program.stages(ins[in_place], outs[out_place], *mine))
        at = {0: [one[0] for one in lists[:lead]]}
        if lead:
            at[0] += [one[0] for one in lists[lead:]]
            at[0] += in_turn([one[1:] for one in lists[:lead]])
            lists = [one[1:] for one in lists[lead:]]
        stages = in_turn(lists)
        for index, stage in enumerate(stages):
            place = index * steps // len(stages) if index + 1 < len(stages) else steps - 1
            if lead:
                place = max(place, min(1, steps - 1))
            at.setdefault(place, []).append(stage)
        in_at, out_at = transfers, transfers
        holds, tasks = [], []
        for work, (low, high) in zip(works, spans):
            work_ins = list(ins[in_at : in_at + len(work.inputs)])
            in_at += len(work.inputs)
            sources = []
            for array, _, _ in work.held:
                sources.append(None if isinstance(array, int) else ins[in_at])
                in_at += not isinstance(array, int)
            work_outs = outs[out_at : out_at + len(work.outputs)]
            out_at += len(work.outputs)
            if work.held:
                held, sems, rest = rest[: len(sources)], rest[len(sources)], rest[len(sources) + 1 :]
                for index, (array, _, view) in enumerate(work.held):
                    source = outs[array] if isinstance(array, int) else sources[index]
                    holds.append((view(source), held[index], sems.at[index]))
                work_ins += held
            own, rest = rest[: len(work.scratch)], rest[len(work.scratch) :]
            tasks.append((work, low, high, work_ins, work_outs, own))
        for place in sorted(at):
            def act(place=place):
                if place == 0:
                    enter(peers, len(directs) > 0)
                for stage in at[place]:
                    stage()
                if place == 0:
                    for action in ("start", "wait"):
                        for hold in holds:
                            getattr(pltpu.make_async_copy(*hold), action)()

            if steps == 1:
                act()
            else:
                pl.when(step == place)(act)
        for work, low, high, work_ins, work_outs, own in tasks:
            def do(work=work, low=low, work_ins=work_ins, work_outs=work_outs, own=own):
                work.body(step - low, work_ins, work_outs, *own)

            if len(works) == 1:
                do()
            else:
                pl.when((step >= low) & (step < high))(do)

    return pl.pallas_call(
        kernel,
        name=name,
        grid=(steps,),
        out_shape=out_shapes,
        in_specs=in_specs,
        out_specs=out_specs,
        scratch_shapes=scratch,
        compiler_params=pltpu.CompilerParams(
            collective_id=collective_id,
            has_side_effects=True,
            vmem_limit_bytes=vmem * 1024 * 1024,
            dimension_semantics=("arbitrary",),
        ),
    )(*operands)


def tile_of(size):
    return 512 if size % 512 == 0 else size


def weight_parts(own, others):
    count, share, hidden = others.shape
    if share % 128:
        side = lax.axis_index("fsdp")
        mine = lax.dynamic_slice_in_dim(own, side * hidden, hidden, 1)
        twice = jnp.concatenate([mine] + [others[i] for i in range(count)], axis=0)
        twice = jnp.concatenate([twice, twice], axis=0)
        start = lax.rem(count + 1 - side, count + 1) * share
        whole = lax.dynamic_slice_in_dim(twice, start, (count + 1) * share, 0)
        return [(whole, whole.shape, lambda ref: ref)]

    def own_view(ref):
        start = pl.multiple_of(lax.axis_index("fsdp") * hidden, 128)
        return ref.at[:, pl.ds(start, hidden)]

    return [(own, (share, hidden), own_view)] + [
        (others, (share, hidden), lambda ref, w=w: ref.at[w]) for w in range(count)
    ]


def down_back(upstream, down):
    total, model = upstream.shape
    hidden = down.shape[0]
    tile = tile_of(hidden)
    across = hidden // tile

    def body(step, ins, outs):
        part = pl.ds(pl.multiple_of(lax.rem(step, across) * tile, tile), tile)
        outs[0][...] = dot_nt(ins[0][...], ins[1][part, :]).astype(LOW)

    return Work(
        total // 512 * across,
        [(upstream, (512, model), lambda s: (s // across, 0))],
        [((total, hidden), LOW, (512, tile), lambda s: (s // across, lax.rem(s, across)))],
        body,
        held=[(down, down.shape, lambda ref: ref)],
    )


def hidden_units(rows_all, d_act, gates, ups, tokens, groups):
    total, model = rows_all.shape
    count = len(gates)
    share, hidden = gates[0][1]
    tile = tile_of(hidden)
    across, height = hidden // tile, 512
    each, holds = total // groups // height, height // tokens

    def body(step, ins, outs, own_gate, own_up):
        part = pl.ds(pl.multiple_of(lax.rem(step, across) * tile, tile), tile)
        side = lax.axis_index("fsdp")
        me = lax.axis_index("expert")
        weights = ins[2:]
        pre_gate = pre_up = None
        for which in range(count):
            start = 0
            if count > 1:
                start = pl.multiple_of(lax.rem(side + which, count) * share, 128)
            rows = ins[0][:, pl.ds(start, share)]
            more_gate = dot_nn(rows, weights[which][:, part])
            more_up = dot_nn(rows, weights[count + which][:, part])
            pre_gate = more_gate if pre_gate is None else pre_gate + more_gate
            pre_up = more_up if pre_up is None else pre_up + more_up
        grad = ins[1][...].astype(jnp.float32)
        sigma = 0.5 + 0.5 * jnp.tanh(0.5 * pre_gate)
        silu = pre_gate * sigma
        outs[0][...] = (silu * pre_up).astype(LOW)
        outs[1][...] = (grad * pre_up * (sigma * (1.0 + pre_gate * (1.0 - sigma)))).astype(LOW)
        outs[2][...] = (grad * silu).astype(LOW)
        row_tile = step // across

        @pl.when(lax.rem(row_tile, each) == 0)
        def _():
            here = pl.ds(pl.multiple_of(lax.rem(me, holds) * tokens, tokens), tokens)
            there = pl.ds(pl.multiple_of(row_tile // each * tokens, tokens), tokens)
            own_gate[there, part] = outs[1][here, :]
            own_up[there, part] = outs[2][here, :]

        for which in range(count):

            @pl.when(step == (groups - 1) * each * across + across + which)
            def _(which=which):
                start = 0
                if count > 1:
                    start = pl.multiple_of(lax.rem(side + which, count) * share, 128)
                outs[3][:, pl.ds(start, share)] = (
                    dot_nt(own_gate[...], weights[which][...])
                    + dot_nt(own_up[...], weights[count + which][...])
                ).astype(LOW)

    def row_tile(s):
        number = s // across
        turned = lax.rem(lax.rem(number, each) + lax.axis_index("expert") // holds, each)
        return number // each * each + turned

    def spot(s):
        return row_tile(s), lax.rem(s, across)

    return Work(
        total // height * across,
        [(rows_all, (height, model), lambda s: (row_tile(s), 0)), (d_act, (height, tile), spot)],
        [((total, hidden), LOW, (height, tile), spot)] * 3
        + [((groups * tokens, model), LOW, (groups * tokens, model), lambda s: (0, 0))],
        body,
        [pltpu.VMEM((groups * tokens, hidden), LOW)] * 2,
        held=list(gates) + list(ups),
    )


def turned_products(left, rights, dtype, depth):
    total, height = left.shape
    width = rights[0].shape[1]
    tall, tile = tile_of(height), tile_of(width)
    across, deep = width // tile, total // depth

    def body(step, ins, outs, turned, *sums):
        now = lax.rem(step, deep)
        span = pl.ds(pl.multiple_of(now * depth, depth), depth)

        @pl.when(lax.rem(step // deep, across) == 0)
        def _():
            turned[:, span] = ins[0][...].T

        for which in range(len(rights)):
            product = dot_nn(turned[:, span], ins[1 + which][...])
            if deep == 1:
                outs[which][...] = product.astype(dtype)
            else:
                sums[which][...] = jnp.where(now == 0, 0.0, sums[which][...]) + product

        if deep > 1:

            @pl.when(now == deep - 1)
            def _():
                for which in range(len(rights)):
                    outs[which][...] = sums[which][...].astype(dtype)

    def left_spot(s):
        first = lax.rem(s // deep, across) == 0
        return jnp.where(first, lax.rem(s, deep), deep - 1), s // (deep * across)

    def right_spot(s):
        return lax.rem(s, deep), lax.rem(s // deep, across)

    return Work(
        height // tall * across * deep,
        [(left, (depth, tall), left_spot)]
        + [(right, (depth, tile), right_spot) for right in rights],
        [
            (
                (height, width),
                dtype,
                (tall, tile),
                lambda s: (s // (deep * across), lax.rem(s // deep, across)),
            )
        ]
        * len(rights),
        body,
        [pltpu.VMEM((tall, total), left.dtype)]
        + [pltpu.VMEM((tall, tile), jnp.float32)] * (len(rights) if deep > 1 else 0),
    )


CHUNK = 256


def tile_columns(value, count):
    return jnp.concatenate([value] * count, axis=1)


def stacked(ref, count):
    return jnp.concatenate(
        [ref[:, index * HEAD_DIM : (index + 1) * HEAD_DIM] for index in range(count)], axis=0
    )


def unstacked(turned, count, tokens):
    return jnp.concatenate(
        [turned[:, index * tokens : (index + 1) * tokens].T for index in range(count)], axis=1
    )


def chunks_of(ref, columns=None):
    def chunk(index):
        if columns is None:
            return ref[pl.ds(pl.multiple_of(index * CHUNK, CHUNK), CHUNK), :]
        blocks = CHUNK // ref.shape[1]
        return ref[pl.ds(index * blocks, blocks), :, columns].reshape(CHUNK, HEAD_DIM)

    return chunk


def chunk_scores(keys, queries, key_labels, query_labels, chunk, place, count):
    tokens = queries.shape[0] // count
    span = pl.ds(pl.multiple_of(chunk * CHUNK, CHUNK), CHUNK)
    raw = dot_nt(keys(chunk), queries) * HEAD_DIM ** (-0.5)
    row = chunk * CHUNK + lax.broadcasted_iota(jnp.int32, (CHUNK, tokens), 0)
    column = place * tokens + lax.broadcasted_iota(jnp.int32, (CHUNK, tokens), 1)
    allowed = (key_labels[span, :] == query_labels[...]) & (row <= column)
    bias = jnp.where(allowed, 0.0, masked_score)
    return span, raw + tile_columns(bias, count)


def attend_kernel(place, q_ref, keys, values, kl_ref, ql_ref, out_ref, log_ref, score_ref):
    tokens = q_ref.shape[0]
    count = q_ref.shape[1] // HEAD_DIM
    queries = stacked(q_ref, count)
    chunks = kl_ref.shape[0] // CHUNK

    def scores(chunk, top):
        span, value = chunk_scores(keys, queries, kl_ref, ql_ref, chunk, place[0], count)
        score_ref[span, :] = value
        return jnp.maximum(top, jnp.max(value, axis=0, keepdims=True))

    top = lax.fori_loop(
        0, chunks, scores, jnp.full((1, count * tokens), masked_score, jnp.float32)
    )

    def mix(chunk, carried):
        total, mixed = carried
        span = pl.ds(pl.multiple_of(chunk * CHUNK, CHUNK), CHUNK)
        prob = jnp.exp(score_ref[span, :] - top)
        return (
            total + jnp.sum(prob, axis=0, keepdims=True),
            mixed + dot_tn(values(chunk), prob.astype(LOW)),
        )

    total, mixed = lax.fori_loop(
        0,
        chunks,
        mix,
        (
            jnp.zeros((1, count * tokens), jnp.float32),
            jnp.zeros((HEAD_DIM, count * tokens), jnp.float32),
        ),
    )
    out_ref[...] = unstacked(mixed / total, count, tokens).astype(LOW)
    log_ref[0] = jnp.broadcast_to(top + jnp.log(total), log_ref.shape[1:])


def attend_back_kernel(
    place, q_ref, k_ref, v_ref, kl_ref, ql_ref, grad_ref, log_ref, dq_ref, pair_ref, p_ref, dp_ref
):
    tokens = q_ref.shape[0]
    count = q_ref.shape[1] // HEAD_DIM
    queries = stacked(q_ref, count)
    grads = stacked(grad_ref, count)
    chunks = k_ref.shape[0] // CHUNK
    keys, values = chunks_of(k_ref), chunks_of(v_ref)
    log_total = log_ref[0, 0:1, :]
    scale = HEAD_DIM ** (-0.5)

    def probs(chunk, row_dot):
        span, value = chunk_scores(keys, queries, kl_ref, ql_ref, chunk, place[0], count)
        prob = jnp.exp(value - log_total)
        d_prob = dot_nt(values(chunk), grads)
        p_ref[span, :] = prob
        dp_ref[span, :] = d_prob
        return row_dot + jnp.sum(prob * d_prob, axis=0, keepdims=True)

    row_dot = lax.fori_loop(
        0, chunks, probs, jnp.zeros((1, count * tokens), jnp.float32)
    )

    def back(chunk, d_query):
        span = pl.ds(pl.multiple_of(chunk * CHUNK, CHUNK), CHUNK)
        prob = p_ref[span, :]
        d_score = (prob * (dp_ref[span, :] - row_dot)).astype(LOW)
        pair_ref[span, :HEAD_DIM] = (dot_nn(d_score, queries) * scale).astype(LOW)
        pair_ref[span, HEAD_DIM:] = dot_nn(prob.astype(LOW), grads).astype(LOW)
        return d_query + dot_tn(keys(chunk), d_score)

    d_query = lax.fori_loop(
        0, chunks, back, jnp.zeros((HEAD_DIM, count * tokens), jnp.float32)
    )
    dq_ref[...] = unstacked(d_query * scale, count, tokens)


def attention_specs(tokens, length, group):
    return [
        pl.BlockSpec(memory_space=pltpu.SMEM),
        pl.BlockSpec((tokens, group), lambda g: (0, g)),
        pl.BlockSpec((length, HEAD_DIM), lambda g: (0, g)),
        pl.BlockSpec((length, HEAD_DIM), lambda g: (0, KEY_HEADS + g)),
        pl.BlockSpec((length, 1), lambda g: (0, 0)),
        pl.BlockSpec((1, tokens), lambda g: (0, 0)),
    ]


def attend_work(queries, pairs_at, key_labels, query_labels):
    tokens, width = queries.shape
    length, group = key_labels.shape[0], width // KEY_HEADS
    stack = group // HEAD_DIM * tokens
    pair_width = 2 * KEY_HEADS * HEAD_DIM

    def body(step, ins, outs, scores):
        q_ref, kl_ref, ql_ref, pairs = ins
        start = pl.multiple_of(step * HEAD_DIM, HEAD_DIM)
        keys = chunks_of(pairs, pl.ds(start, HEAD_DIM))
        values = chunks_of(pairs, pl.ds(KEY_HEADS * HEAD_DIM + start, HEAD_DIM))
        place = [lax.axis_index("expert")]
        attend_kernel(place, q_ref, keys, values, kl_ref, ql_ref, *outs, scores)

    return Work(
        KEY_HEADS,
        [
            (queries, (tokens, group), lambda s: (0, s)),
            (key_labels, (length, 1), lambda s: (0, 0)),
            (query_labels, (1, tokens), lambda s: (0, 0)),
        ],
        [
            ((tokens, width), LOW, (tokens, group), lambda s: (0, s)),
            ((KEY_HEADS, 8, stack), jnp.float32, (1, 8, stack), lambda s: (s, 0, 0)),
        ],
        body,
        [pltpu.VMEM((length, stack), jnp.float32)],
        held=[
            (
                pairs_at,
                (length // tokens, tokens, pair_width),
                lambda ref: ref.at[0, :, :, pl.ds(0, pair_width)],
            )
        ],
    )


def attend_back(place, queries, pairs, key_labels, query_labels, grads, log_total):
    tokens, width = queries.shape
    length, group = pairs.shape[0], width // KEY_HEADS
    stack = group // HEAD_DIM * tokens
    return pl.pallas_call(
        attend_back_kernel,
        name="attend_back",
        grid=(KEY_HEADS,),
        in_specs=attention_specs(tokens, length, group)
        + [
            pl.BlockSpec((tokens, group), lambda g: (0, g)),
            pl.BlockSpec((1, 8, stack), lambda g: (g, 0, 0)),
        ],
        out_specs=[
            pl.BlockSpec((tokens, group), lambda g: (0, g)),
            pl.BlockSpec((length, 2 * HEAD_DIM), lambda g: (0, g)),
        ],
        out_shape=[
            jax.ShapeDtypeStruct((tokens, width), jnp.float32),
            jax.ShapeDtypeStruct((length, 2 * KEY_HEADS * HEAD_DIM), LOW),
        ],
        scratch_shapes=[pltpu.VMEM((length, stack), jnp.float32)] * 2,
        compiler_params=pltpu.CompilerParams(vmem_limit_bytes=50 * 1024 * 1024),
    )(place, queries, pairs, pairs, key_labels, query_labels, grads, log_total)


def dispatch_kernel(
    place, n_ref, u_ref, p_ref, m_ref, w_ref, rows_ref, up_ref, pair_ref, g_ref, pick_ref
):
    blocks, tokens, model = n_ref.shape
    capacity = p_ref.shape[1]

    @pl.when(pl.program_id(0) == 0)
    def _():
        pick_ref[...] = jnp.zeros(pick_ref.shape, LOW)

    for block in range(blocks):
        pick_ref[
            block * capacity : (block + 1) * capacity, block * tokens : (block + 1) * tokens
        ] = p_ref[block]
    pick = pick_ref[...]
    logits = dot_nt(w_ref[...], n_ref[...].reshape(blocks * tokens, model))
    chosen = m_ref[...] > 0.5
    top = jnp.max(jnp.where(chosen, logits, masked_score), axis=0, keepdims=True)
    power = jnp.where(chosen, jnp.exp(jnp.where(chosen, logits - top, 0.0)), 0.0)
    mine = lax.broadcasted_iota(jnp.int32, logits.shape, 0) == place[0]
    gate = jnp.sum(jnp.where(mine, power, 0.0), axis=0, keepdims=True) / jnp.sum(
        power, axis=0, keepdims=True
    )
    slot_gate = jnp.sum(pick.astype(jnp.float32) * gate, axis=1, keepdims=True)
    g_ref[...] = slot_gate
    tile = tile_of(model)
    for index in range(model // tile):
        span = pl.ds(index * tile, tile)
        rows = n_ref[:, :, span].reshape(blocks * tokens, tile)
        rows_ref[:, span] = dot_nn(pick, rows).astype(LOW)
        ups = dot_nn(pick, u_ref[:, span])
        up_ref[:, span] = ups.astype(LOW)
        pair_ref[:, span] = (slot_gate * ups).astype(LOW)


def dispatch(place, normed, upstream, pick, chosen, w_router):
    blocks, capacity, tokens = pick.shape
    model = upstream.shape[1]
    experts = w_router.shape[0]
    group = 4
    wide_spec = pl.BlockSpec((group * capacity, model), lambda b: (b, 0))
    return pl.pallas_call(
        dispatch_kernel,
        name="dispatch",
        grid=(blocks // group,),
        in_specs=[
            pl.BlockSpec(memory_space=pltpu.SMEM),
            pl.BlockSpec((group, tokens, model), lambda b: (b, 0, 0)),
            pl.BlockSpec((group * tokens, model), lambda b: (b, 0)),
            pl.BlockSpec((group, capacity, tokens), lambda b: (b, 0, 0)),
            pl.BlockSpec((experts, group * tokens), lambda b: (0, b)),
            pl.BlockSpec((experts, model), lambda b: (0, 0)),
        ],
        out_specs=[wide_spec] * 3 + [pl.BlockSpec((group * capacity, 1), lambda b: (b, 0))],
        out_shape=[jax.ShapeDtypeStruct((blocks * capacity, model), LOW)] * 3
        + [jax.ShapeDtypeStruct((blocks * capacity, 1), jnp.float32)],
        scratch_shapes=[pltpu.VMEM((group * capacity, group * tokens), LOW)],
        compiler_params=pltpu.CompilerParams(vmem_limit_bytes=50 * 1024 * 1024),
    )(place, normed, upstream, pick, chosen, w_router)


def join_columns(side, groups, own, others):
    rows, columns = others[0].shape
    tile = rows // 10

    def kernel(side_ref, *refs):
        for step, ref in enumerate(refs[:-1]):
            start = lax.rem(side_ref[0] + step, groups) * columns
            refs[-1][:, pl.ds(pl.multiple_of(start, 128), columns)] = ref[...].astype(jnp.float32)

    return pl.pallas_call(
        kernel,
        name="join_columns",
        grid_spec=pltpu.PrefetchScalarGridSpec(
            num_scalar_prefetch=1,
            grid=(10,),
            in_specs=[pl.BlockSpec((tile, columns), lambda i, side: (side[0] * 10 + i, 0))]
            + [pl.BlockSpec((tile, columns), lambda i, side: (i, 0))] * len(others),
            out_specs=pl.BlockSpec((tile, groups * columns), lambda i, side: (i, 0)),
        ),
        out_shape=jax.ShapeDtypeStruct((rows, groups * columns), jnp.float32),
    )(side, own, *others)


def widen(arrays, cuts):
    rows = arrays[0].shape[0]
    steps = 10 if rows % 10 == 0 else 12
    tile = rows // steps
    widths = [
        [high - low for low, high in zip([0] + cut, cut + [array.shape[1]])]
        for array, cut in zip(arrays, cuts)
    ]

    def kernel(*refs):
        outs = iter(refs[len(arrays) :])
        for ref, parts in zip(refs, widths):
            start = 0
            for part in parts:
                next(outs)[...] = ref[:, start : start + part].astype(jnp.float32)
                start += part

    flat = [part for parts in widths for part in parts]
    return pl.pallas_call(
        kernel,
        name="widen",
        grid=(steps,),
        in_specs=[pl.BlockSpec((tile, array.shape[1]), lambda i: (i, 0)) for array in arrays],
        out_specs=[pl.BlockSpec((tile, part), lambda i: (i, 0)) for part in flat],
        out_shape=[jax.ShapeDtypeStruct((rows, part), jnp.float32) for part in flat],
    )(*arrays)


def expert_kernel(
    count, side, rows_ref, up_ref, pair_ref, gate_ref, back_ref, *refs
):
    w_gate, w_up, w_down = refs[:count], refs[count : 2 * count], refs[2 * count : 3 * count]
    act_ref, dg_ref, du_ref, d_gate_ref, out_ref, term_ref = refs[3 * count :]
    share = w_gate[0].shape[0]
    units = w_down[0].shape[0]
    model = rows_ref.shape[1]
    blocks, tokens, capacity = back_ref.shape

    def place(which, size):
        if count == 1:
            return pl.ds(0, size)
        return pl.ds(pl.multiple_of(lax.rem(side[0] + which, count) * size, 128), size)

    for which in range(count):
        span = place(which, units)
        pre_gate = pre_up = None
        for part in range(count):
            rows = rows_ref[:, place(part, share)]
            more_gate = dot_nn(rows, w_gate[part][:, span])
            more_up = dot_nn(rows, w_up[part][:, span])
            pre_gate = more_gate if pre_gate is None else pre_gate + more_gate
            pre_up = more_up if pre_up is None else pre_up + more_up
        d_act = dot_nt(pair_ref[...], w_down[which][...])
        sigma = 0.5 + 0.5 * jnp.tanh(0.5 * pre_gate)
        silu = pre_gate * sigma
        act_ref[:, span] = (silu * pre_up).astype(LOW)
        dg_ref[:, span] = (
            d_act * pre_up * (sigma * (1.0 + pre_gate * (1.0 - sigma)))
        ).astype(LOW)
        du_ref[:, span] = (d_act * silu).astype(LOW)

    def returned(target, values, span):
        for block in range(blocks):
            mine = values[block * capacity : (block + 1) * capacity]
            target[block, :, span] = dot_nn(back_ref[block], mine).astype(LOW)

    d_gate = jnp.zeros(d_gate_ref.shape, jnp.float32)
    tile = tile_of(model)
    for index in range(model // tile):
        span = pl.ds(index * tile, tile)
        produced = None
        for part in range(count):
            more = dot_nn(act_ref[:, place(part, units)], w_down[part][:, span])
            produced = more if produced is None else produced + more
        produced = produced.astype(LOW).astype(jnp.float32)
        d_gate += jnp.sum(produced * up_ref[:, span].astype(jnp.float32), axis=1, keepdims=True)
        returned(out_ref, (gate_ref[...] * produced).astype(LOW), span)
    d_gate_ref[...] = d_gate
    for part in range(count):
        pieces = 2 if share % 256 == 0 else 1
        for piece in range(pieces):
            width = share // pieces
            rows = pl.ds(piece * width, width)
            d_rows = dot_nt(dg_ref[...], w_gate[part][rows, :]) + dot_nt(
                du_ref[...], w_up[part][rows, :]
            )
            start = piece * width
            if count > 1:
                start = pl.multiple_of(lax.rem(side[0] + part, count) * share + start, 128)
            returned(term_ref, d_rows.astype(LOW), pl.ds(start, width))


def run_expert(side, rows_in, rows_up, d_pair, slot_gate, pick, gates, ups, downs):
    slots, model = rows_in.shape
    blocks, capacity, tokens = pick.shape
    hidden = gates[0].shape[1]
    count = len(gates)
    group = 4
    tile = group * capacity
    wide = pl.BlockSpec((tile, model), lambda i, side: (i, 0))
    narrow = pl.BlockSpec((tile, hidden), lambda i, side: (i, 0))
    single = pl.BlockSpec((tile, 1), lambda i, side: (i, 0))
    terms = pl.BlockSpec((group, tokens, model), lambda i, side: (i, 0, 0))
    weights = list(gates) + list(ups) + list(downs)

    def kernel(*refs):
        expert_kernel(count, *refs)

    return pl.pallas_call(
        kernel,
        name="expert",
        grid_spec=pltpu.PrefetchScalarGridSpec(
            num_scalar_prefetch=1,
            grid=(blocks // group,),
            in_specs=[
                wide,
                wide,
                wide,
                single,
                pl.BlockSpec((group, tokens, capacity), lambda i, side: (i, 0, 0)),
            ]
            + [
                pl.BlockSpec(w.shape, lambda i, side: (0, 0), pipeline_mode=pl.Buffered(1))
                for w in weights
            ],
            out_specs=[narrow, narrow, narrow, single, terms, terms],
        ),
        out_shape=[jax.ShapeDtypeStruct((slots, hidden), LOW)] * 3
        + [jax.ShapeDtypeStruct((slots, 1), jnp.float32)]
        + [jax.ShapeDtypeStruct((blocks, tokens, model), LOW)] * 2,
        compiler_params=pltpu.CompilerParams(vmem_limit_bytes=60 * 1024 * 1024),
    )(side, rows_in, rows_up, d_pair, slot_gate, pick.transpose(0, 2, 1), *weights)


def local(
    hidden_in,
    gain_attn,
    query_weight,
    key_matrix,
    value_matrix,
    out_weight,
    gain_ffn,
    router_weight,
    shared_gate,
    shared_up,
    shared_down,
    expert_gate,
    expert_up,
    expert_down,
    routes,
    segments,
    positions,
    grad_out,
):
    tokens = hidden_in.shape[1]
    model = hidden_in.shape[2]
    experts = lax.axis_size("expert")
    groups = lax.axis_size("fsdp")
    topk = routes.shape[2]
    capacity = min(tokens, 4 * tokens * topk // (3 * experts))
    length = tokens * experts
    group_width = QUERY_HEADS // KEY_HEADS
    score_scale = HEAD_DIM ** (-0.5)
    place = lax.axis_index("expert")
    side = lax.axis_index("fsdp")
    share = model // groups

    def peer(values, step):
        if step == 0:
            return values
        return lax.ppermute(
            values, "fsdp", [((i + step) % groups, i) for i in range(groups)]
        )

    def ring(values):
        return [peer(values, step) for step in range(groups)]

    def scattered(values, axis):
        size = values.shape[axis] // groups
        return [
            peer(
                lax.dynamic_slice_in_dim(
                    values, ((side - step + groups) % groups) * size, size, axis
                ),
                step,
            )
            for step in range(groups)
        ]

    def in_order(parts, axis):
        if groups == 2:
            first = side == 0
            return jnp.concatenate(
                [jnp.where(first, parts[0], parts[1]), jnp.where(first, parts[1], parts[0])], axis
            )
        size = parts[0].shape[axis]
        twice = jnp.concatenate(parts + parts, axis)
        start = ((groups - side) % groups) * size
        return lax.dynamic_slice_in_dim(twice, start, groups * size, axis)

    def own_columns(values, step):
        size = values.shape[-1] // groups
        return lax.dynamic_slice_in_dim(values, ((side + step) % groups) * size, size, 1)

    def rows_product(values, parts):
        if len(parts) == 1:
            return dot_nn(values, parts[0])
        total = dot_nn(own_columns(values, 0), parts[0])
        for step in range(1, groups):
            total = total + dot_nn(own_columns(values, step), parts[step])
        return total

    small = jnp.concatenate([gain_attn[None], gain_ffn[None], router_weight.T], axis=0)
    small_full = in_order(ring(small), 1)
    gain_first = small_full[0].astype(jnp.float32)
    gain_second = small_full[1].astype(jnp.float32)
    w_router = small_full[2:]
    w_query, w_key, w_value, w_out = (
        ring(query_weight),
        ring(key_matrix),
        ring(value_matrix),
        ring(out_weight),
    )
    expert_ids = jnp.arange(experts, dtype=jnp.int32)
    chosen = jnp.any(routes[0][:, :, None] == expert_ids[None, None, :], axis=1)
    upstream_low = grad_out[0]
    upstream = upstream_low.astype(jnp.float32)

    x_rows = hidden_in[0].astype(jnp.float32)
    labels = segments[0]
    cosine, sine = rope_tables(positions[0])
    normed_one = rms_scale(x_rows, gain_first).astype(LOW)
    key_rows = rotate(
        rows_product(normed_one, w_key).reshape(tokens, KEY_HEADS, HEAD_DIM), cosine, sine
    ).astype(LOW)
    value_rows = rows_product(normed_one, w_value).astype(LOW)
    wide = KEY_HEADS * HEAD_DIM
    pair_rows = jnp.concatenate(
        [
            key_rows.reshape(tokens, wide),
            value_rows,
            jnp.pad(chosen.astype(LOW), ((0, 0), (0, 128 - experts))),
        ],
        axis=1,
    )
    here = place.reshape(1)
    queries = (
        rotate(
            rows_product(normed_one, w_query).reshape(tokens, QUERY_HEADS, HEAD_DIM), cosine, sine
        )
        .astype(LOW)
        .reshape(tokens, QUERY_HEADS * HEAD_DIM)
    )
    key_labels = labels[:, None]
    query_labels = lax.dynamic_slice_in_dim(labels, place * tokens, tokens)[None]
    (
        every_pair,
        upstream_each,
        gate_others,
        up_others,
        eg_others,
        eu_others,
        ed_others,
        attended,
        log_total,
    ) = carry(
        "attend",
        7,
        groups,
        gathers=[(1, pair_rows), (groups, upstream_low)],
        exchanges=[
            (shared_gate, True),
            (shared_up, True),
            (expert_gate[0], False),
            (expert_up[0], False),
            (expert_down[0], False),
        ],
        works=[attend_work(queries, 0, key_labels, query_labels)],
        lead=2,
    )
    every_pair = every_pair.reshape(length, 2 * wide + 128)
    chosen_all = every_pair[:, 2 * wide : 2 * wide + experts].T.astype(jnp.float32)
    upstream_each = upstream_each.reshape(groups * length, model)
    residual_one = x_rows + rows_product(attended, w_out)
    normed_two = rms_scale(residual_one, gain_second).astype(LOW)

    gate_parts = weight_parts(shared_gate, gate_others)
    up_parts = weight_parts(shared_up, up_others)
    normed_each, shared_d_act = carry(
        "rows",
        2,
        groups,
        gathers=[(groups, normed_two)],
        works=[down_back(upstream_each, shared_down)],
    )
    normed_blocks = normed_each.reshape(groups * experts, tokens, model)
    normed_each = normed_each.reshape(groups * length, model)

    logits = dot_nt(normed_two, w_router)
    router_probs = jax.nn.softmax(logits, axis=-1)
    chosen_probs = jnp.where(chosen, router_probs, 0.0)
    chosen_sum = jnp.sum(chosen_probs, axis=1, keepdims=True)
    gate_own = chosen_probs / chosen_sum

    def shares(own, others):
        parts = [own[0]] + [others[index] for index in range(groups - 1)]
        aligned = share % 128 == 0 and expert_down.shape[1] % 128 == 0
        return parts if aligned else [in_order(parts, 0)]

    member = (
        lax.dynamic_index_in_dim(chosen_all, place, 0, keepdims=False).reshape(experts, tokens)
        > 0.5
    )
    below = jnp.tril(jnp.ones((tokens, tokens), LOW), -1)
    rank = dot_nt(member.astype(LOW), below)
    slots = (
        member[:, None, :]
        & (rank.astype(jnp.int32)[:, None, :] == jnp.arange(capacity, dtype=jnp.int32)[None, :, None])
    )
    pick = slots.astype(LOW)

    rows_in, rows_up, d_pair, slot_weight = dispatch(
        here, normed_blocks, upstream_each, pick, chosen_all, w_router
    )
    here_side = side.reshape(1)
    expert_act, d_gate_pre, d_up_pre, d_gate_slots, out_terms, row_terms = run_expert(
        here_side,
        rows_in,
        rows_up,
        d_pair,
        slot_weight,
        pick,
        shares(expert_gate, eg_others),
        shares(expert_up, eu_others),
        shares(expert_down, ed_others),
    )
    d_gate_slots = d_gate_slots.reshape(experts, capacity, 1)
    d_gate_rows = jnp.sum(jnp.where(slots, d_gate_slots, 0.0), axis=1)
    d_gate_rows = jnp.broadcast_to(d_gate_rows[:, None, :], (experts, 8, tokens))
    half_model = model // 2
    (
        expert_back,
        out_left,
        d_gate_own,
        shared_act,
        shared_d_gate,
        shared_d_up,
        back_parts,
    ) = carry(
        "row_grads",
        3,
        1,
        scatters=[(row_terms, 0, model), (out_terms, 0, half_model)],
        directs=[d_gate_rows],
        works=[
            hidden_units(normed_each, shared_d_act, gate_parts, up_parts, tokens, groups)
        ],
    )
    d_gate_own = d_gate_own[:, 0, :].T
    def returned(terms):
        total = terms[0].astype(jnp.float32)
        for step in range(1, groups):
            back = lax.ppermute(
                terms[step], "fsdp", [(i, (i + step) % groups) for i in range(groups)]
            )
            total = total + back.astype(jnp.float32)
        return total

    shared_back = returned(back_parts.reshape(groups, tokens, model))

    d_chosen = jnp.where(
        chosen,
        (d_gate_own - jnp.sum(gate_own * d_gate_own, axis=1, keepdims=True)) / chosen_sum,
        0.0,
    )
    d_logits = router_probs * (
        d_chosen - jnp.sum(router_probs * d_chosen, axis=1, keepdims=True)
    )
    d_normed_two = (
        shared_back
        + expert_back
        + lax.dot_general(
            d_logits,
            w_router.astype(jnp.float32),
            (((1,), (0,)), ((), ())),
            precision=highest,
            preferred_element_type=jnp.float32,
        )
    )
    d_residual_norm, d_gain_two = rms_back(residual_one, gain_second, d_normed_two)
    d_residual = upstream + d_residual_norm
    d_attn_out = d_residual.astype(LOW)
    grad_router = lax.dot_general(
        d_logits,
        normed_two.astype(jnp.float32),
        (((0,), (0,)), ((), ())),
        precision=highest,
        preferred_element_type=jnp.float32,
    )

    def chip_term(left, right):
        return dot_tn(
            jnp.concatenate(scattered(left, 1), axis=0), jnp.concatenate(ring(right), axis=0)
        ).astype(LOW)

    def blocks(term):
        rows, width = term.shape
        rows = rows // experts
        term = term.reshape(experts, rows, width)
        return jnp.pad(term, ((0, 0), (0, -rows % 16), (0, 0)))

    term_o = chip_term(attended, d_attn_out)

    d_attended = in_order([dot_nt(d_attn_out, part) for part in w_out], 1).astype(LOW)
    d_query, term_pairs = attend_back(
        here, queries, every_pair, key_labels, query_labels, d_attended, log_total
    )
    d_pairs, out_right, mine_o, grad_sg, grad_su = carry(
        "pair_grads",
        4,
        1,
        scatters=[
            (term_pairs.reshape(experts, tokens, -1), 0, 2 * wide),
            (out_terms, half_model, half_model),
            (blocks(term_o), 0, model),
        ],
        works=[
            turned_products(normed_each, [shared_d_gate, shared_d_up], LOW, length)
        ],
    )
    d_pairs = d_pairs.reshape(tokens, KEY_HEADS, 2, HEAD_DIM)
    d_query_low = rotate(
        d_query.reshape(tokens, QUERY_HEADS, HEAD_DIM), cosine, -sine
    ).reshape(tokens, -1).astype(LOW)
    d_key_low = rotate(d_pairs[:, :, 0], cosine, -sine).reshape(tokens, -1).astype(LOW)
    d_value_low = d_pairs[:, :, 1].reshape(tokens, -1).astype(LOW)
    d_normed_one = in_order(
        [
            dot_nt(d_query_low, w_query[step])
            + dot_nt(d_key_low, w_key[step])
            + dot_nt(d_value_low, w_value[step])
            for step in range(groups)
        ],
        1,
    )
    d_rows_norm, d_gain_one = rms_back(x_rows, gain_first, d_normed_one)
    grad_in = (d_residual + d_rows_norm).astype(LOW)
    small_grads = jnp.concatenate([d_gain_one[None], d_gain_two[None], grad_router], axis=0)
    small_grads = jnp.pad(small_grads, ((0, 256 - small_grads.shape[0]), (0, 0))).astype(LOW)
    small_parts = [part.astype(jnp.float32) for part in scattered(small_grads, 1)]
    small_term = sum(small_parts).astype(LOW).T
    term_pre = chip_term(
        normed_one, jnp.concatenate([d_query_low, d_key_low, d_value_low], axis=1)
    )
    all_o, mine_pre, mine_small, term_eg, term_eu, term_ed = carry(
        "sums",
        5,
        1,
        gathers=[(1, mine_o.astype(LOW))],
        scatters=[(blocks(term_pre), 0, term_pre.shape[1]), (blocks(small_term), 0, 256)],
        works=[
            turned_products(rows_in, [d_gate_pre, d_up_pre], LOW, rows_in.shape[0]),
            turned_products(expert_act, [d_pair], LOW, rows_in.shape[0]),
        ],
    )
    all_o = all_o.reshape(experts, -1, model)[:, : share // experts].reshape(share, model)
    mine_pre = jnp.concatenate([mine_pre, mine_small], axis=1)[: share // experts].astype(LOW)
    all_pre = lax.all_gather(mine_pre, "expert", axis=0, tiled=True)

    mine_pre, shared_act, term_eg, term_eu, term_ed, grad_sg, grad_su = lax.optimization_barrier(
        (mine_pre, shared_act, term_eg, term_eu, term_ed, grad_sg, grad_su)
    )
    own_act = lax.dynamic_slice_in_dim(
        shared_act.reshape(groups, length, -1), place * tokens, tokens, 1
    ).reshape(groups * tokens, -1)
    out_parts = dot_nn(own_act, shared_down).astype(LOW).reshape(groups, tokens, model)
    expert_sum = jnp.concatenate([out_left, out_right], axis=1)
    output = residual_one + returned(out_parts) + expert_sum

    def summed(term):
        parts = scattered(term, 0)
        size = term.shape[0] // groups
        total = lax.dynamic_slice_in_dim(term, side * size, size, 0).astype(jnp.float32)
        for part in parts[1:]:
            total = total + part.astype(jnp.float32)
        return total

    grad_eg, grad_eu, grad_ed = summed(term_eg), summed(term_eu), summed(term_ed)
    grad_sd = dot_tn(shared_act, upstream_each)
    grad_sg, grad_su = [
        join_columns(here_side, groups, term, scattered(term, 0)[1:])
        for term in (grad_sg, grad_su)
    ]
    (grad_o,) = widen([all_o], [[]])
    grad_q, grad_k, grad_v, small_grads = widen(
        [all_pre], [[model, model + wide, model + 2 * wide]]
    )
    small_grads = small_grads[:, : 2 + experts].T
    return (
        output.astype(LOW)[None],
        grad_in[None],
        small_grads[0],
        grad_q,
        grad_k,
        grad_v,
        grad_o,
        small_grads[1],
        small_grads[2:].T,
        grad_sg,
        grad_su,
        grad_sd,
        grad_eg[None],
        grad_eu[None],
        grad_ed[None],
    )


def solution(mesh):
    rows, split = P("fsdp", None), P("fsdp")
    tokens, expert = P("fsdp", "expert", None), P("expert", "fsdp", None)
    return jax.shard_map(
        local,
        mesh=mesh,
        in_specs=(
            (tokens, split, rows, rows, rows, rows, split)
            + (rows,) * 4
            + (expert,) * 3
            + (tokens, rows, P("fsdp", "expert"), tokens)
        ),
        out_specs=(
            (tokens, tokens, split)
            + (rows,) * 4
            + (split,)
            + (rows,) * 4
            + (expert,) * 3
        ),
        check_vma=False,
    )
```
